32 devices in a mesh: tm: 8 (over z, x), phase: 4 (over y, core).
Axes of the slice: x: 2, y: 2, z: 4, core: 2. Of those that a mesh axis runs over, the one named last changes fastest.
Arguments:
- frames: bfloat16 [2, 1024, 1024], P(None, 'tm'), may hold values from -6 to 6
- frame_counts: int32 [2, 32], replicated, may hold values from 1 to 32, as said below
- w_query: bfloat16 [4, 1024, 1024], P('phase')
- w_key: bfloat16 [4, 1024, 1024], P('phase')
- w_value: bfloat16 [4, 1024, 1024], P('phase'), may hold values from -0.1875 to 0.1875
- w_out: bfloat16 [4, 1024, 1024], P('phase'), may hold values from -0.1875 to 0.1875
- conv_kernel: bfloat16 [4, 31, 1024], P('phase'), may hold values from -1 to 1
- w_point: bfloat16 [4, 1024, 1024], P('phase'), may hold values from -0.1875 to 0.1875
Outputs:
- layer_outputs: bfloat16 [4, 2, 1024, 1024], P('phase', None, 'tm')
The draws below stay inside these ranges and needn't reach their ends.
Inputs may be any that keep to these rules, and one draw needn't show every extreme that they name: `frame_counts`: A segment's valid frames are its first ones; the largest count 32 occurs in every draw.
All inputs are finite; a program needn't handle non-finite values.
Results may differ from the reference program's by a relative error of at most 0.034.
Values may be sent and summed in bfloat16 or wider, within the bound.
No kernel may reach another device: no remote copies, remote signals or barrier semaphores. Data moves between devices by JAX's collectives and lax.ppermute only.
A program may use at most 64 MiB of HBM per device.

```python
import math
import jax
import jax.numpy as jnp
from jax import lax

D = 1024
HEADS = 16
SEG = 32
LC = 64
NMEM = 4
KW = 31
MICRO = 2
SPAN = 1024
NSEGS = 32
LAYERS = 4


def draw_frame_counts(key, part):
    shape = (MICRO, NSEGS)
    picker = jax.random.randint(jax.random.fold_in(key, 21), shape, 0, 4)
    shorter = jax.random.randint(jax.random.fold_in(key, 22), shape, 1, SEG + 1)
    return jnp.where(picker == 0, shorter, SEG).astype(jnp.int32)


def projection(key, salt):
    shape = (LAYERS, D, D)
    own_part = jax.random.normal(jax.random.fold_in(key, salt), shape, jnp.float32)
    values = own_part / jnp.sqrt(jnp.float32(D))
    return values


def draw_w_query(key, part):
    return projection(key, 32).astype(jnp.bfloat16)


def draw_w_key(key, part):
    return projection(key, 33).astype(jnp.bfloat16)


def block_scale(stream_key, dims, pieces, low, high):
    gain = 1.0
    for axis_at, blocks in pieces:
        draws = jax.random.uniform(jax.random.fold_in(jax.random.fold_in(stream_key, 6), axis_at), (blocks,), jnp.float32, low / len(pieces), high / len(pieces))
        gain = gain * jnp.repeat(jnp.exp(draws), dims[axis_at] // blocks).reshape((-1,) + (1,) * (len(dims) - 1 - axis_at))
    return gain


def bell_draw(own_key, shape, scale, reach, cuts=(), kind=jnp.bfloat16):
    factor_of = block_scale(own_key, shape, cuts, -0.22, 0.18) if cuts else 1.0
    drawn = jax.random.normal(own_key, shape, jnp.float32) * scale * factor_of
    return jnp.minimum(jnp.maximum(drawn, -reach), reach).astype(kind)


def setup_inputs(seed: int = 0) -> dict:
    streams_of = jax.random.split(jax.random.key(seed), 9)
    return {
        "frames": bell_draw(streams_of[0], (MICRO, SPAN, D), 1.0, 6.0, ((1, 8),)),
        "frame_counts": draw_frame_counts(jax.random.fold_in(streams_of[8], 71), 0),
        "w_query": draw_w_query(jax.random.fold_in(streams_of[8], 71), 0),
        "w_key": draw_w_key(jax.random.fold_in(streams_of[8], 71), 0),
        "w_value": bell_draw(streams_of[4], (LAYERS, D, D), D ** -0.5, 0.1875, ((0, 4),)),
        "w_out": bell_draw(streams_of[5], (LAYERS, D, D), D ** -0.5, 0.1875, ((0, 4),)),
        "conv_kernel": bell_draw(streams_of[6], (LAYERS, KW, D), KW ** -0.5, 1.0, ((0, 4),)),
        "w_point": bell_draw(streams_of[7], (LAYERS, D, D), D ** -0.5, 0.1875, ((0, 4),)),
    }


EPSILON = 1e-05

def layer_norm(values):
    center = values - lax.optimization_barrier(jnp.mean(values, axis=-1, keepdims=True))
    spread = lax.optimization_barrier(jnp.mean(center * center, axis=-1, keepdims=True))
    return center * lax.rsqrt(spread + EPSILON)

def attend(queries, key_rows, value_rows, allowed):
    segments, query_len, model_width = queries.shape
    head_dim = model_width // HEADS
    split_q = queries.astype(jnp.float32).reshape(segments, query_len, HEADS, head_dim)
    split_k = key_rows.astype(jnp.float32).reshape(segments, key_rows.shape[1], HEADS, head_dim)
    split_v = value_rows.astype(jnp.float32).reshape(segments, value_rows.shape[1], HEADS, head_dim)
    scores = jnp.einsum('sqhd,skhd->shqk', split_q, split_k) / math.sqrt(head_dim)
    scores = jnp.where(allowed[:, None, None, :], scores, -1e+30)
    top_score = lax.optimization_barrier(jnp.max(scores, axis=-1, keepdims=True))
    exponent = jnp.exp(scores - top_score)
    weights = (exponent / lax.optimization_barrier(jnp.sum(exponent, axis=-1, keepdims=True))).astype(jnp.bfloat16)
    context = jnp.einsum('shqk,skhd->sqhd', weights.astype(jnp.float32), split_v)
    return context.reshape(segments, query_len, model_width)

def windows(rows_all, segments):
    back_blocks = LC // SEG
    blocks = rows_all.reshape((segments + back_blocks, SEG) + rows_all.shape[1:])
    return jnp.concatenate([blocks[offset:offset + segments] for offset in range(back_blocks + 1)], axis=1)

def bank(rows_all, segments):
    return jnp.stack([rows_all[offset:offset + segments] for offset in range(NMEM)], axis=1)

def one_layer(layer_in, counts, valid, query_weight, key_weight, value_weight, out_weight, kernel, point_weight):
    total_frames, model_width = layer_in.shape
    segments = counts.shape[0]
    inputs = layer_in.astype(jnp.float32)
    normed = layer_norm(inputs).astype(jnp.bfloat16)
    queries = jnp.dot(normed, query_weight, preferred_element_type=jnp.float32).astype(jnp.bfloat16)
    key_rows = jnp.dot(normed, key_weight, preferred_element_type=jnp.float32).astype(jnp.bfloat16)
    value_rows = jnp.dot(normed, value_weight, preferred_element_type=jnp.float32).astype(jnp.bfloat16)
    seg_mask = valid.reshape(segments, SEG)
    seg_rows = normed.reshape(segments, SEG, model_width).astype(jnp.float32)
    summary = (lax.optimization_barrier(jnp.sum(seg_rows * seg_mask[:, :, None], axis=1)) / counts[:, None].astype(jnp.float32)).astype(jnp.bfloat16)
    summary_q = jnp.dot(summary, query_weight, preferred_element_type=jnp.float32).astype(jnp.bfloat16)
    lead_rows = jnp.zeros((LC, model_width), jnp.bfloat16)
    key_win = windows(jnp.concatenate([lead_rows, key_rows]), segments)
    value_win = windows(jnp.concatenate([lead_rows, value_rows]), segments)
    mask_win = windows(jnp.concatenate([jnp.zeros((LC,), jnp.float32), valid]), segments) > 0.5
    memory = attend(summary_q[:, None, :], key_win, value_win, mask_win)[:, 0, :].astype(jnp.bfloat16)
    mem_k = jnp.dot(memory, key_weight, preferred_element_type=jnp.float32).astype(jnp.bfloat16)
    mem_v = jnp.dot(memory, value_weight, preferred_element_type=jnp.float32).astype(jnp.bfloat16)
    lead_mem = jnp.zeros((NMEM, model_width), jnp.bfloat16)
    bank_k = bank(jnp.concatenate([lead_mem, mem_k]), segments)
    bank_v = bank(jnp.concatenate([lead_mem, mem_v]), segments)
    bank_ok = bank(jnp.concatenate([jnp.zeros((NMEM,), jnp.int32), counts]), segments) > 0
    all_keys = jnp.concatenate([bank_k, key_win], axis=1)
    all_values = jnp.concatenate([bank_v, value_win], axis=1)
    all_ok = jnp.concatenate([bank_ok, mask_win], axis=1)
    context = attend(queries.reshape(segments, SEG, model_width), all_keys, all_values, all_ok)
    context = context.reshape(total_frames, model_width).astype(jnp.bfloat16)
    residual = (inputs + jnp.dot(context, out_weight, preferred_element_type=jnp.float32)).astype(jnp.bfloat16)
    conv_in = (layer_norm(residual.astype(jnp.float32)) * valid[:, None]).astype(jnp.bfloat16)
    extended = jnp.concatenate([jnp.zeros((KW - 1, model_width), jnp.bfloat16), conv_in])
    depth = jnp.zeros((total_frames, model_width), jnp.float32)
    for offset in range(KW):
        depth = depth + kernel[offset].astype(jnp.float32) * extended[offset:offset + total_frames].astype(jnp.float32)
    gated = jax.nn.silu(layer_norm(depth)).astype(jnp.bfloat16)
    mixed = residual.astype(jnp.float32) + jnp.dot(gated, point_weight, preferred_element_type=jnp.float32)
    return (mixed * valid[:, None]).astype(jnp.bfloat16)

def reference(frames, frame_counts, w_query, w_key, w_value, w_out, conv_kernel, w_point):
    micro_count, span_rows, model_width = frames.shape
    counts = frame_counts.reshape(-1).astype(jnp.int32)
    valid = (jnp.arange(SEG, dtype=jnp.int32)[None, :] < counts[:, None]).astype(jnp.float32).reshape(-1)
    hidden = frames.reshape(micro_count * span_rows, model_width)
    results = []
    for layer in range(LAYERS):
        hidden = one_layer(hidden, counts, valid, w_query[layer], w_key[layer], w_value[layer], w_out[layer], conv_kernel[layer], w_point[layer])
        results.append(hidden.reshape(micro_count, span_rows, model_width))
    return jnp.stack(results)
```

```python
import functools
import math

import jax
import jax.numpy as jnp
from jax import lax
from jax.experimental import pallas as pl
from jax.experimental.pallas import tpu as pltpu
from jax.sharding import PartitionSpec as P

HEADS = 16
SEG = 32
LC = 64
NMEM = 4
KW = 31

EPSILON = 1e-05
BACK = LC // SEG
HALO_SEGS = 1 + NMEM + BACK
HALO = HALO_SEGS * SEG
FAR = -1e30
OPEN = 3e38
TILE = 256
PAIR = 128


def layer_norm(values):
    center = values - jnp.mean(values, axis=-1, keepdims=True)
    spread = jnp.mean(center * center, axis=-1, keepdims=True)
    return center * lax.rsqrt(spread + EPSILON)


def dot(a, b):
    return jnp.dot(a, b, preferred_element_type=jnp.float32)


def dot_nt(a, b):
    return lax.dot_general(a, b, (((1,), (1,)), ((), ())), preferred_element_type=jnp.float32)


def halo_pieces(rows):
    pieces = []
    left = HALO
    while left > 0:
        take = min(rows, left)
        pieces.append((len(pieces) + 1, take))
        left -= take
    return pieces


def by_segment(index, counts, first, number):
    out = jnp.zeros(index.shape, jnp.int32)
    for s in range(number):
        out = jnp.where(index == s, counts[first + s], out)
    return out


def layer_kernel(cfg, *refs):
    rows, width, step, micro, phases, shards, segs_row, pieces = cfg
    refs = list(refs)
    meta, counts_ref = refs[:2]
    hbm_weights = refs[2:7]
    taps_hbm = refs[7]
    refs = refs[8:]
    count_p = len(pieces)
    with_frames = step < micro
    with_inbox = step >= 1
    with_prev = step >= 2
    if with_frames:
        frames_hbm, frame_halos = refs[0], refs[1 : 1 + count_p]
        refs = refs[1 + count_p :]
    if with_inbox:
        inbox, halos = refs[0], refs[1 : 1 + count_p]
        refs = refs[1 + count_p :]
    if with_prev:
        prevs = refs[:count_p]
        refs = refs[count_p:]
    if step >= 1:
        refs = refs[1:]
    outputs = refs[0]
    refs = refs[1:]
    with_relay = step < micro + phases - 2
    relays = []
    if with_relay:
        number = 1 + sum(1 for _, take in pieces if take < rows)
        relays = refs[:number]
        refs = refs[number:]
    (xe, normed, ke, ve, qe, ctx, res, cin, depth, gated, result, bias, mem_bias,
     wk, wv, wq, wo, wp, taps, wsem, xsem, osem) = refs

    ext = HALO + rows
    segs = ext // SEG
    q_rows = rows + SEG
    q_seg = HALO_SEGS - 1
    mem_first = q_seg - NMEM
    mems = segs - 1 - mem_first
    mem_pad = ke.shape[0] - ext
    key_seg = q_seg - BACK
    key_row = key_seg * SEG
    keys = ke.shape[0] - key_row
    win = ext - key_row
    heads_dim = width // HEADS
    sum_rows = qe.shape[0] - q_rows

    phase, shard = meta[0], meta[1]
    position = step - phase
    active = (position >= 0) & (position < micro)

    def fetch(source, target, index):
        pltpu.make_async_copy(source, target, xsem.at[index]).start()

    @pl.when(active)
    def _():
        names = (wk, wv, wq, wo, wp)
        own = xe.at[pl.ds(HALO, rows)]
        spots = []
        for distance, take in pieces:
            top = HALO - (distance - 1) * rows - take
            spots.append((distance, xe.at[pl.ds(top, take)]))
        if with_frames:
            @pl.when(phase == 0)
            def _():
                fetch(frames_hbm.at[step], own, 0)
                for n, (distance, spot) in enumerate(spots):
                    @pl.when(shard >= distance)
                    def _():
                        fetch(frame_halos[n].at[step], spot, 1 + n)
                    if step >= 1:
                        @pl.when(shard < distance)
                        def _():
                            fetch(frame_halos[n].at[step - 1], spot, 1 + n)
        if with_inbox:
            @pl.when(phase > 0)
            def _():
                fetch(inbox, own, 0)
                for n, (distance, spot) in enumerate(spots):
                    @pl.when(shard >= distance)
                    def _():
                        fetch(halos[n], spot, 1 + n)
                    if with_prev:
                        @pl.when((shard < distance) & (position > 0))
                        def _():
                            fetch(prevs[n], spot, 1 + n)
        for n, (source, target) in enumerate(zip(hbm_weights, names)):
            pltpu.make_async_copy(source, target, wsem.at[n]).start()
        pltpu.make_async_copy(taps_hbm, taps, wsem.at[5]).start()

        def need(n):
            if n == 5:
                pltpu.make_async_copy(taps_hbm, taps, wsem.at[5]).wait()
            else:
                pltpu.make_async_copy(hbm_weights[n], names[n], wsem.at[n]).wait()

        for n, (distance, spot) in enumerate(spots):
            @pl.when((shard < distance) & (position == 0))
            def _():
                spot[...] = jnp.zeros(spot.shape, jnp.bfloat16)

        first = position * segs_row + shard * (rows // SEG) - HALO_SEGS
        counts = []
        for s in range(segs):
            g = first + s
            safe = jnp.maximum(g, 0)
            value = counts_ref[safe // segs_row, safe % segs_row]
            counts.append(jnp.where(g >= 0, value, 0))

        row = lax.broadcasted_iota(jnp.int32, (q_rows, keys), 0)
        col = lax.broadcasted_iota(jnp.int32, (q_rows, keys), 1)
        line = lax.broadcasted_iota(jnp.int32, (1, keys), 1)
        kcount = by_segment(line // SEG, counts, key_seg, win // SEG)
        kvalid = (line % SEG) < kcount
        mvalid = by_segment(line - win, counts, mem_first, mems) > 0
        live = jnp.where((kvalid & (line < win)) | (mvalid & (line >= win)), 1, 0)
        segment = q_seg + row // SEG
        key_at = jnp.where(
            col < win, key_seg + col // SEG, mem_first + (col - win) + (BACK + 1000)
        )
        low = jnp.where(col < win, segment - BACK, segment - NMEM + (BACK + 1000))
        high = jnp.where(col < win, segment, segment - 1 + (BACK + 1000))
        good = (key_at >= low) & (key_at <= high) & (live > 0)
        bias[...] = jnp.where(good, OPEN, FAR)

        mem_keys = mem_bias.shape[1]
        mrow = lax.broadcasted_iota(jnp.int32, (mems * HEADS, mem_keys), 0)
        mcol = lax.broadcasted_iota(jnp.int32, (mems * HEADS, mem_keys), 1)
        mline = lax.broadcasted_iota(jnp.int32, (1, mem_keys), 1)
        mlive = (mline % SEG) < by_segment(mline // SEG, counts, 0, mem_keys // SEG)
        mseg = mem_first + mrow // HEADS
        mgood = (mcol // SEG >= mseg - BACK) & (mcol // SEG <= mseg) & mlive
        mem_bias[...] = jnp.where(mgood, OPEN, FAR)

        pltpu.make_async_copy(
            frames_hbm.at[step] if with_frames else inbox, own, xsem.at[0]
        ).wait()
        for n, (distance, spot) in enumerate(spots):
            @pl.when((shard >= distance) | (position > 0))
            def _():
                pltpu.make_async_copy(
                    frame_halos[n].at[step] if with_frames else halos[n], spot, xsem.at[1 + n]
                ).wait()
        for r in range(0, ext, SEG):
            part = xe[pl.ds(r, SEG), :].astype(jnp.float32)
            normed[pl.ds(r, SEG), :] = layer_norm(part).astype(jnp.bfloat16)

        def columns(n):
            return pl.ds(pl.multiple_of(n * TILE, TILE), TILE)

        need(0)

        @pl.loop(0, width // TILE)
        def _(n):
            at = columns(n)
            ke[pl.ds(0, ext), at] = dot(normed[...], wk[:, at]).astype(jnp.bfloat16)

        need(1)

        @pl.loop(0, width // TILE)
        def _(n):
            at = columns(n)
            ve[pl.ds(0, ext), at] = dot(normed[...], wv[:, at]).astype(jnp.bfloat16)

        srow = lax.broadcasted_iota(jnp.int32, (sum_rows, ext), 0)
        scol = lax.broadcasted_iota(jnp.int32, (sum_rows, ext), 1)
        sline = lax.broadcasted_iota(jnp.int32, (1, ext), 1)
        slive = (sline % SEG) < by_segment(sline // SEG, counts, 0, segs)
        pick = jnp.where((scol // SEG == srow + mem_first) & slive, 1.0, 0.0).astype(jnp.bfloat16)
        scount = by_segment(
            lax.broadcasted_iota(jnp.int32, (sum_rows, 1), 0), counts, mem_first, mems
        )
        divisor = jnp.maximum(scount, 1).astype(jnp.float32)
        summary = (dot(pick, normed[...]) / divisor).astype(jnp.bfloat16)

        scale = 1.0 / math.sqrt(heads_dim)
        need(2)

        @pl.loop(0, width // TILE)
        def _(n):
            at = columns(n)
            lhs = jnp.concatenate([normed[pl.ds(ext - q_rows, q_rows), :], summary])
            qe[:, at] = (dot(lhs, wq[:, at]) * scale).astype(jnp.bfloat16)

        head_of = lax.broadcasted_iota(jnp.int32, (HEADS, width), 1) // heads_dim
        own_head = head_of == lax.broadcasted_iota(jnp.int32, (HEADS, width), 0)
        sq = qe[pl.ds(q_rows, sum_rows), :].astype(jnp.float32)
        spread_q = []
        for m in range(mems):
            line_q = jnp.broadcast_to(sq[m : m + 1, :], (HEADS, width))
            spread_q.append(jnp.where(own_head, line_q, 0.0).astype(jnp.bfloat16))
        spread_q = jnp.concatenate(spread_q)
        ms = dot_nt(spread_q, ke[pl.ds(0, mem_keys), :])
        ms = jnp.minimum(ms, mem_bias[...])
        me = jnp.exp(ms - jnp.max(ms, axis=-1, keepdims=True))
        mw = (me / jnp.sum(me, axis=-1, keepdims=True)).astype(jnp.bfloat16)
        mo = dot(mw, ve[pl.ds(0, mem_keys), :])
        lines = []
        for m in range(mems):
            part = jnp.where(own_head, mo[m * HEADS : (m + 1) * HEADS, :], 0.0)
            lines.append(jnp.sum(part, axis=0, keepdims=True))
        lines.append(jnp.zeros((mem_pad - mems, width), jnp.float32))
        memory = jnp.concatenate(lines).astype(jnp.bfloat16)

        @pl.loop(0, width // TILE)
        def _(n):
            at = columns(n)
            ke[pl.ds(ext, mem_pad), at] = dot(memory, wk[:, at]).astype(jnp.bfloat16)
            ve[pl.ds(ext, mem_pad), at] = dot(memory, wv[:, at]).astype(jnp.bfloat16)

        lane = lax.broadcasted_iota(jnp.int32, (q_rows, PAIR), 1)
        even = lane < heads_dim

        @pl.loop(0, width // PAIR)
        def _(n):
            at = pl.ds(pl.multiple_of(n * PAIR, PAIR), PAIR)
            qp = qe[pl.ds(0, q_rows), at]
            zero = jnp.zeros_like(qp)
            kp = ke[pl.ds(key_row, keys), at]
            vp = ve[pl.ds(key_row, keys), at]
            halves = []
            for q_half in (jnp.where(even, qp, zero), jnp.where(even, zero, qp)):
                scores = jnp.minimum(dot_nt(q_half, kp), bias[...])
                weight = jnp.exp(scores - jnp.max(scores, axis=-1, keepdims=True))
                total = jnp.sum(weight, axis=-1, keepdims=True)
                halves.append(dot(weight.astype(jnp.bfloat16), vp) / total)
            ctx[:, at] = jnp.where(even, halves[0], halves[1]).astype(jnp.bfloat16)

        need(3)

        @pl.loop(0, width // TILE)
        def _(n):
            at = columns(n)
            x_part = xe[pl.ds(ext - q_rows, q_rows), at].astype(jnp.float32)
            res[:, at] = (x_part + dot(ctx[...], wo[:, at])).astype(jnp.bfloat16)

        inner = lax.broadcasted_iota(jnp.int32, (SEG, 1), 0)
        for s in range(q_rows // SEG):
            mask = (inner < counts[q_seg + s]).astype(jnp.float32)
            part = res[pl.ds(s * SEG, SEG), :].astype(jnp.float32)
            part = (layer_norm(part) * mask).astype(jnp.bfloat16)
            cin[pl.ds(s * SEG, SEG), :] = part.astype(jnp.float32)

        need(5)

        @pl.loop(0, width // PAIR)
        def _(n):
            at = pl.ds(pl.multiple_of(n * PAIR, PAIR), PAIR)
            total = jnp.zeros((rows, PAIR), jnp.float32)
            for j in range(KW):
                total = total + taps[pl.ds(j, 1), at] * cin[pl.ds(SEG - (KW - 1) + j, rows), at]
            depth[:, at] = total

        for r in range(0, rows, SEG):
            part = layer_norm(depth[pl.ds(r, SEG), :])
            gated[pl.ds(r, SEG), :] = (part / (1.0 + jnp.exp(-part))).astype(jnp.bfloat16)

        need(4)
        frame = lax.broadcasted_iota(jnp.int32, (rows, 1), 0)
        frame_ok = (frame % SEG) < by_segment(frame // SEG, counts, HALO_SEGS, rows // SEG)
        row_mask = frame_ok.astype(jnp.float32)

        @pl.loop(0, width // TILE)
        def _(n):
            at = columns(n)
            mixed = res[pl.ds(SEG, rows), at].astype(jnp.float32) + dot(gated[...], wp[:, at])
            result[:, at] = (mixed * row_mask).astype(jnp.bfloat16)

        copies = [pltpu.make_async_copy(result, outputs.at[position], osem.at[0])]
        if with_relay:
            copies.append(pltpu.make_async_copy(result, relays[0], osem.at[1]))
            spot = 1
            for _, take in pieces:
                if take < rows:
                    copies.append(
                        pltpu.make_async_copy(
                            result.at[pl.ds(rows - take, take)], relays[spot], osem.at[1 + spot]
                        )
                    )
                    spot += 1
        for copy in copies:
            copy.start()
        for copy in copies:
            copy.wait()


def per_device(frames, frame_counts, w_query, w_key, w_value, w_out, conv_kernel, w_point):
    micro, rows, width = frames.shape
    phases = lax.axis_size("phase")
    shards = lax.axis_size("tm")
    segs_row = frame_counts.shape[1]
    pieces = halo_pieces(rows)
    ext = HALO + rows
    q_rows = rows + SEG
    mems = ext // SEG - 1 - (HALO_SEGS - 1 - NMEM)
    mem_pad = -(-mems // SEG) * SEG
    sum_rows = -(-mems // 16) * 16
    mem_keys = (mems + BACK) * SEG
    keys = ext + mem_pad - (HALO_SEGS - 1 - BACK) * SEG

    meta = jnp.stack([lax.axis_index("phase"), lax.axis_index("tm")]).astype(jnp.int32)
    taps = jnp.pad(conv_kernel[0].astype(jnp.float32), ((0, 32 - KW), (0, 0)))

    frame_halos = []
    for distance, take in pieces:
        route = [(s * phases, (s + distance) % shards * phases) for s in range(shards)]
        frame_halos.append(
            lax.ppermute(frames[:, rows - take :, :], ("tm", "phase"), route)
        )

    def relay(blocks, step):
        senders = [p for p in range(phases - 1) if 0 <= step - p < micro]

        def send(block, distance):
            route = [
                (s * phases + p, (s + distance) % shards * phases + p + 1)
                for s in range(shards)
                for p in senders
            ]
            return lax.ppermute(block, ("tm", "phase"), route)

        got = [send(blocks[0], 0)]
        spot = 1
        for distance, take in pieces:
            if take < rows:
                got.append(send(blocks[spot], distance))
                spot += 1
            else:
                got.append(send(blocks[0], distance))
        return got

    def vmem(*shape, dtype=jnp.bfloat16):
        return pltpu.VMEM(shape, dtype)

    scratch = [
        vmem(ext, width), vmem(ext, width), vmem(ext + mem_pad, width), vmem(ext + mem_pad, width),
        vmem(q_rows + sum_rows, width), vmem(q_rows, width), vmem(q_rows, width),
        vmem(q_rows, width, dtype=jnp.float32), vmem(rows, width, dtype=jnp.float32),
        vmem(rows, width), vmem(rows, width),
        vmem(q_rows, keys, dtype=jnp.float32), vmem(mems * HEADS, mem_keys, dtype=jnp.float32),
        vmem(width, width), vmem(width, width), vmem(width, width), vmem(width, width),
        vmem(width, width), vmem(32, width, dtype=jnp.float32),
        pltpu.SemaphoreType.DMA((6,)),
        pltpu.SemaphoreType.DMA((1 + len(pieces),)),
        pltpu.SemaphoreType.DMA((2 + len(pieces),)),
    ]
    smem = pl.BlockSpec(memory_space=pltpu.SMEM)
    hbm = pl.BlockSpec(memory_space=pl.ANY)
    weights = [w_key[0], w_value[0], w_query[0], w_out[0], w_point[0]]
    block = jax.ShapeDtypeStruct((rows, width), jnp.bfloat16)
    tails = [
        jax.ShapeDtypeStruct((take, width), jnp.bfloat16) for _, take in pieces if take < rows
    ]
    whole = jax.ShapeDtypeStruct((micro, rows, width), jnp.bfloat16)

    outputs = None
    got, before = [], []
    steps = micro + phases - 1
    for step in range(steps):
        args = [meta, frame_counts, *weights, taps]
        if step < micro:
            args += [frames, *frame_halos]
        if step >= 1:
            args += got
        if step >= 2:
            args += before[1:]
        aliases = {}
        if step >= 1:
            aliases = {len(args): 0}
            args.append(outputs)
        last = step == steps - 1
        outs = [whole] if last else [whole, block, *tails]
        cfg = (rows, width, step, micro, phases, shards, segs_row, pieces)
        made = pl.pallas_call(
            functools.partial(layer_kernel, cfg),
            out_shape=outs,
            in_specs=[smem, smem] + [hbm] * (len(args) - 2),
            out_specs=[hbm] * len(outs),
            scratch_shapes=scratch,
            input_output_aliases=aliases,
            compiler_params=pltpu.CompilerParams(vmem_limit_bytes=48 * 1024 * 1024),
            name="layer",
        )(*args)
        outputs = made[0]
        if not last:
            before, got = got, relay(made[1:], step)
    return outputs[None]


def solution(mesh):
    in_specs = (
        P(None, "tm", None),
        P(),
        P("phase", None, None),
        P("phase", None, None),
        P("phase", None, None),
        P("phase", None, None),
        P("phase", None, None),
        P("phase", None, None),
    )
    out_specs = P("phase", None, "tm", None)
    return jax.shard_map(
        per_device, mesh=mesh, in_specs=in_specs, out_specs=out_specs, check_vma=False
    )
```

```python
import functools
import math

import jax
import jax.numpy as jnp
from jax import lax
from jax.experimental import pallas as pl
from jax.experimental.pallas import tpu as pltpu
from jax.sharding import PartitionSpec as P

HEADS = 16
SEG = 32
LC = 64
NMEM = 4
KW = 31

EPSILON = 1e-05
BACK = LC // SEG
HALO_SEGS = 1 + NMEM + BACK
HALO = HALO_SEGS * SEG
FAR = -1e30
OPEN = 3e38
TILE = 256
PAIR = 128
SHIFT = 5
HEAD_SHIFT = 4
VMEM_BYTES = 40 * 1024 * 1024


def layer_norm(values):
    center = values - jnp.mean(values, axis=-1, keepdims=True)
    spread = jnp.mean(center * center, axis=-1, keepdims=True)
    return center * lax.rsqrt(spread + EPSILON)


def dot(a, b):
    return jnp.dot(a, b, preferred_element_type=jnp.float32)


def dot_nt(a, b):
    return lax.dot_general(a, b, (((1,), (1,)), ((), ())), preferred_element_type=jnp.float32)


def halo_pieces(rows):
    pieces = []
    left = HALO
    while left > 0:
        take = min(rows, left)
        pieces.append((len(pieces) + 1, take))
        left -= take
    return pieces


def by_segment(index, counts, first, number):
    out = jnp.zeros(index.shape, jnp.int32)
    for s in range(number):
        out = jnp.where(index == s, counts[first + s], out)
    return out


def iota(shape, dimension):
    return lax.broadcasted_iota(jnp.int32, shape, dimension)


def layer_kernel(cfg, *refs):
    rows, width, section, chunk, sections, shards, segs_row, pieces = cfg
    refs = list(refs)
    info = refs[0]
    hbm_weights = refs[1:6]
    taps_hbm, source = refs[6:8]
    refs = refs[8:]
    count_p = len(pieces)
    halos, refs = refs[:count_p], refs[count_p:]
    if chunk > 0:
        befores, refs = refs[:count_p], refs[count_p:]
    if section + chunk > 0:
        refs = refs[1:]
    outputs, refs = refs[0], refs[1:]
    with_relay = section < sections - 1
    relays = []
    if with_relay:
        number = 1 + sum(1 for _, take in pieces if take < rows)
        relays, refs = refs[:number], refs[number:]
    (xe, normed, ke, ve, qe, ctx, res, cin, depth, gated, result, bias, mem_bias,
     wk, wv, wq, wo, wp, taps, wsem, xsem, osem) = refs

    ext = HALO + rows
    segs = ext // SEG
    q_rows = rows + SEG
    q_seg = HALO_SEGS - 1
    mem_first = q_seg - NMEM
    mems = segs - 1 - mem_first
    mem_pad = ke.shape[0] - ext
    key_seg = q_seg - BACK
    key_row = key_seg * SEG
    keys = ke.shape[0] - key_row
    win = ext - key_row
    head_dim = width // HEADS
    sum_rows = qe.shape[0] - q_rows
    phase, shard = info[0], info[1]

    @pl.when(phase == section)
    def _():
        own = xe.at[pl.ds(HALO, rows)]
        spots = []
        for distance, take in pieces:
            top = HALO - (distance - 1) * rows - take
            spots.append((distance, xe.at[pl.ds(top, take)]))
        own_copy = pltpu.make_async_copy(
            source.at[chunk] if section == 0 else source, own, xsem.at[0]
        )
        own_copy.start()
        for n, (distance, spot) in enumerate(spots):
            @pl.when(shard >= distance)
            def _():
                pltpu.make_async_copy(halos[n], spot, xsem.at[1 + n]).start()
            if chunk > 0:
                @pl.when(shard < distance)
                def _():
                    pltpu.make_async_copy(befores[n], spot, xsem.at[1 + n]).start()
        names = (wk, wv, wq, wo, wp)
        loads = [
            pltpu.make_async_copy(hbm_weights[n], names[n], wsem.at[n]) for n in range(5)
        ]
        loads.append(pltpu.make_async_copy(taps_hbm, taps, wsem.at[5]))
        loads[0].start()
        loads[1].start()
        if chunk == 0:
            for distance, spot in spots:
                @pl.when(shard < distance)
                def _():
                    spot[...] = jnp.zeros(spot.shape, jnp.bfloat16)

        first = chunk * segs_row + shard * (rows // SEG) - HALO_SEGS
        counts = []
        for s in range(segs):
            g = first + s
            value = info[2 + jnp.maximum(g, 0)]
            counts.append(jnp.where(g >= 0, value, 0))

        row_seg = q_seg + (iota((q_rows, keys), 0) >> SHIFT)
        col = iota((q_rows, keys), 1)
        line = iota((1, keys), 1)
        kvalid = (line & (SEG - 1)) < by_segment(line >> SHIFT, counts, key_seg, win // SEG)
        mvalid = by_segment(line - win, counts, mem_first, mems) > 0
        live = (kvalid & (line < win)) | (mvalid & (line >= win))
        lows = jnp.where(line < win, key_seg + (line >> SHIFT), mem_first + 1 + line - win)
        highs = jnp.where(line < win, lows + BACK, lows + NMEM - 1)
        lows = jnp.where(live, lows, segs)
        good = (row_seg >= lows) & (row_seg <= highs)
        bias[...] = jnp.where(good, OPEN, FAR)

        mem_keys = mem_bias.shape[1]
        mseg = mem_first + (iota((mems * HEADS, mem_keys), 0) >> HEAD_SHIFT)
        mline = iota((1, mem_keys), 1)
        mlow = mline >> SHIFT
        mlive = (mline & (SEG - 1)) < by_segment(mlow, counts, 0, mem_keys // SEG)
        mhigh = mlow + BACK
        mlow = jnp.where(mlive, mlow, segs)
        mem_bias[...] = jnp.where((mseg >= mlow) & (mseg <= mhigh), OPEN, FAR)

        own_copy.wait()
        for n, (distance, spot) in enumerate(spots):
            if chunk > 0:
                pltpu.make_async_copy(halos[n], spot, xsem.at[1 + n]).wait()
            else:
                @pl.when(shard >= distance)
                def _():
                    pltpu.make_async_copy(halos[n], spot, xsem.at[1 + n]).wait()
        for r in range(0, ext, SEG):
            part = xe[pl.ds(r, SEG), :].astype(jnp.float32)
            normed[pl.ds(r, SEG), :] = layer_norm(part).astype(jnp.bfloat16)

        def columns(n):
            return pl.ds(pl.multiple_of(n * TILE, TILE), TILE)

        def tiles(unroll):
            return pl.loop(0, width // TILE, unroll=unroll)

        loads[0].wait()
        loads[1].wait()
        for n in range(2, 6):
            loads[n].start()

        @tiles(2)
        def _(n):
            at = columns(n)
            ke[pl.ds(0, ext), at] = dot(normed[...], wk[:, at]).astype(jnp.bfloat16)
            ve[pl.ds(0, ext), at] = dot(normed[...], wv[:, at]).astype(jnp.bfloat16)

        sseg = iota((sum_rows, ext), 0) + mem_first
        sline = iota((1, ext), 1)
        smine = sline >> SHIFT
        slive = (sline & (SEG - 1)) < by_segment(smine, counts, 0, segs)
        smine = jnp.where(slive, smine, -1)
        pick = jnp.where(sseg == smine, 1.0, 0.0).astype(jnp.bfloat16)
        scount = by_segment(iota((sum_rows, 1), 0), counts, mem_first, mems)
        divisor = jnp.maximum(scount, 1).astype(jnp.float32)
        summary = (dot(pick, normed[...]) / divisor).astype(jnp.bfloat16)

        scale = 1.0 / math.sqrt(head_dim)
        loads[2].wait()

        @tiles(4)
        def _(n):
            at = columns(n)
            lhs = jnp.concatenate([normed[pl.ds(ext - q_rows, q_rows), :], summary])
            qe[:, at] = (dot(lhs, wq[:, at]) * scale).astype(jnp.bfloat16)

        own_head = (iota((HEADS, width), 1) // head_dim) == iota((HEADS, width), 0)
        sq = qe[pl.ds(q_rows, sum_rows), :].astype(jnp.float32)
        spread_q = []
        for m in range(mems):
            line_q = jnp.broadcast_to(sq[m : m + 1, :], (HEADS, width))
            spread_q.append(jnp.where(own_head, line_q, 0.0).astype(jnp.bfloat16))
        spread_q = jnp.concatenate(spread_q)
        ms = jnp.minimum(dot_nt(spread_q, ke[pl.ds(0, mem_keys), :]), mem_bias[...])
        me = jnp.exp(ms - jnp.max(ms, axis=-1, keepdims=True))
        mw = me * (1.0 / jnp.sum(me, axis=-1, keepdims=True))
        mo = dot(mw.astype(jnp.bfloat16), ve[pl.ds(0, mem_keys), :])
        lines = []
        for m in range(mems):
            part = jnp.where(own_head, mo[m * HEADS : (m + 1) * HEADS, :], 0.0)
            lines.append(jnp.sum(part, axis=0, keepdims=True))
        lines.append(jnp.zeros((mem_pad - mems, width), jnp.float32))
        memory = jnp.concatenate(lines).astype(jnp.bfloat16)

        @tiles(4)
        def _(n):
            at = columns(n)
            ke[pl.ds(ext, mem_pad), at] = dot(memory, wk[:, at]).astype(jnp.bfloat16)
            ve[pl.ds(ext, mem_pad), at] = dot(memory, wv[:, at]).astype(jnp.bfloat16)

        even = iota((q_rows, PAIR), 1) < head_dim

        @pl.loop(0, width // PAIR, unroll=2)
        def _(n):
            at = pl.ds(pl.multiple_of(n * PAIR, PAIR), PAIR)
            qp = qe[pl.ds(0, q_rows), at]
            zero = jnp.zeros_like(qp)
            q_both = jnp.concatenate([jnp.where(even, qp, zero), jnp.where(even, zero, qp)])
            raw = dot_nt(q_both, ke[pl.ds(key_row, keys), at])
            edge = bias[...]
            scores = jnp.minimum(raw, jnp.concatenate([edge, edge]))
            weight = jnp.exp(scores - jnp.max(scores, axis=-1, keepdims=True))
            inverse = 1.0 / jnp.sum(weight, axis=-1, keepdims=True)
            both = dot(weight.astype(jnp.bfloat16), ve[pl.ds(key_row, keys), at]) * inverse
            ctx[:, at] = jnp.where(even, both[:q_rows], both[q_rows:]).astype(jnp.bfloat16)

        loads[3].wait()

        @tiles(4)
        def _(n):
            at = columns(n)
            x_part = xe[pl.ds(ext - q_rows, q_rows), at].astype(jnp.float32)
            res[:, at] = (x_part + dot(ctx[...], wo[:, at])).astype(jnp.bfloat16)

        inner = iota((SEG, 1), 0)
        for s in range(q_rows // SEG):
            mask = (inner < counts[q_seg + s]).astype(jnp.float32)
            part = res[pl.ds(s * SEG, SEG), :].astype(jnp.float32)
            part = (layer_norm(part) * mask).astype(jnp.bfloat16)
            cin[pl.ds(s * SEG, SEG), :] = part.astype(jnp.float32)

        loads[5].wait()

        @pl.loop(0, width // PAIR)
        def _(n):
            at = pl.ds(pl.multiple_of(n * PAIR, PAIR), PAIR)
            total = jnp.zeros((rows, PAIR), jnp.float32)
            start = SEG - (KW - 1)
            for residue in range(8):
                offsets = [o for o in range(start, start + KW) if o % 8 == residue]
                size = offsets[-1] - residue + rows
                block = cin[pl.ds(residue, size), at]
                for o in offsets:
                    shifted = block[o - residue : o - residue + rows]
                    total = total + taps[pl.ds(o - start, 1), at] * shifted
            depth[:, at] = total

        for r in range(0, rows, SEG):
            part = layer_norm(depth[pl.ds(r, SEG), :])
            gated[pl.ds(r, SEG), :] = (part / (1.0 + jnp.exp(-part))).astype(jnp.bfloat16)

        loads[4].wait()
        frame = iota((rows, 1), 0)
        frame_count = by_segment(frame >> SHIFT, counts, HALO_SEGS, rows // SEG)
        row_mask = ((frame & (SEG - 1)) < frame_count).astype(jnp.float32)

        @tiles(4)
        def _(n):
            at = columns(n)
            mixed = res[pl.ds(SEG, rows), at].astype(jnp.float32) + dot(gated[...], wp[:, at])
            result[:, at] = (mixed * row_mask).astype(jnp.bfloat16)

        copies = []
        if with_relay:
            copies.append(pltpu.make_async_copy(result, relays[0], osem.at[1]))
            spot = 1
            for _, take in pieces:
                if take < rows:
                    tail = result.at[pl.ds(rows - take, take)]
                    copies.append(pltpu.make_async_copy(tail, relays[spot], osem.at[1 + spot]))
                    spot += 1
        copies.append(pltpu.make_async_copy(result, outputs.at[chunk], osem.at[0]))
        for copy in copies:
            copy.start()
        for copy in copies:
            copy.wait()


def per_device(frames, frame_counts, w_query, w_key, w_value, w_out, conv_kernel, w_point):
    micro, rows, width = frames.shape
    sections = lax.axis_size("phase")
    shards = lax.axis_size("tm")
    segs_row = frame_counts.shape[1]
    pieces = halo_pieces(rows)
    ext = HALO + rows
    q_rows = rows + SEG
    mems = ext // SEG - 1 - (HALO_SEGS - 1 - NMEM)
    mem_pad = -(-mems // SEG) * SEG
    sum_rows = -(-mems // 16) * 16
    mem_keys = (mems + BACK) * SEG
    keys = ext + mem_pad - (HALO_SEGS - 1 - BACK) * SEG

    def send(block, distance, section, ahead):
        route = [
            (s * sections + section, (s + distance) % shards * sections + section + ahead)
            for s in range(shards)
        ]
        return lax.ppermute(block, ("tm", "phase"), route)

    inbox = []
    for chunk in range(micro):
        halos = [
            send(frames[chunk, rows - take :, :], distance, 0, 0) for distance, take in pieces
        ]
        inbox.append([None, *halos])

    where = jnp.stack([lax.axis_index("phase"), lax.axis_index("tm")]).astype(jnp.int32)
    info = jnp.concatenate([where, frame_counts.reshape(-1)])
    taps = jnp.pad(conv_kernel[0].astype(jnp.float32), ((0, 32 - KW), (0, 0)))

    def vmem(*shape, dtype=jnp.bfloat16):
        return pltpu.VMEM(shape, dtype)

    scratch = [
        vmem(ext, width), vmem(ext, width), vmem(ext + mem_pad, width), vmem(ext + mem_pad, width),
        vmem(q_rows + sum_rows, width), vmem(q_rows, width), vmem(q_rows, width),
        vmem(q_rows, width, dtype=jnp.float32), vmem(rows, width, dtype=jnp.float32),
        vmem(rows, width), vmem(rows, width),
        vmem(q_rows, keys, dtype=jnp.float32), vmem(mems * HEADS, mem_keys, dtype=jnp.float32),
        vmem(width, width), vmem(width, width), vmem(width, width), vmem(width, width),
        vmem(width, width), vmem(32, width, dtype=jnp.float32),
        pltpu.SemaphoreType.DMA((6,)),
        pltpu.SemaphoreType.DMA((1 + len(pieces),)),
        pltpu.SemaphoreType.DMA((2 + len(pieces),)),
    ]
    smem = pl.BlockSpec(memory_space=pltpu.SMEM)
    any_space = pl.BlockSpec(memory_space=pl.ANY)
    hbm = pl.BlockSpec(memory_space=pltpu.HBM)
    weights = [
        pltpu.with_memory_space_constraint(w[0], pltpu.HBM)
        for w in (w_key, w_value, w_query, w_out, w_point)
    ]
    frames_kept = pltpu.with_memory_space_constraint(frames, pltpu.HBM)
    block = jax.ShapeDtypeStruct((rows, width), jnp.bfloat16)
    tails = [
        jax.ShapeDtypeStruct((take, width), jnp.bfloat16) for _, take in pieces if take < rows
    ]
    whole = jax.ShapeDtypeStruct((micro, rows, width), jnp.bfloat16)
    cost = pl.CostEstimate(flops=6 * 10**9, bytes_accessed=12 * 10**6, transcendentals=10**6)

    outputs = None
    for section in range(sections):
        outbox = []
        for chunk in range(micro):
            source = frames_kept if section == 0 else inbox[chunk][0]
            args = [info, *weights, taps, source, *inbox[chunk][1:]]
            if chunk > 0:
                args += inbox[chunk - 1][1:]
            in_specs = [smem] + [hbm] * 7 + [any_space] * (len(args) - 8)
            if section > 0:
                in_specs[7] = any_space
            aliases = {}
            if outputs is not None:
                aliases = {len(args): 0}
                args.append(outputs)
                in_specs.append(hbm)
            last = section == sections - 1
            outs = [whole] if last else [whole, block, *tails]
            cfg = (rows, width, section, chunk, sections, shards, segs_row, pieces)
            made = pl.pallas_call(
                functools.partial(layer_kernel, cfg),
                out_shape=outs,
                in_specs=in_specs,
                out_specs=[hbm] + [any_space] * (len(outs) - 1),
                scratch_shapes=scratch,
                input_output_aliases=aliases,
                cost_estimate=cost,
                compiler_params=pltpu.CompilerParams(vmem_limit_bytes=VMEM_BYTES),
                name="layer",
            )(*args)
            outputs = made[0]
            if not last:
                tail_of = iter(made[2:])
                got = [
                    send(next(tail_of) if take < rows else made[1], distance, section, 1)
                    for distance, take in pieces
                ]
                outbox.append([send(made[1], 0, section, 1), *got])
        inbox = outbox
    return outputs[None]


def solution(mesh):
    in_specs = (
        P(None, "tm", None),
        P(),
        P("phase", None, None),
        P("phase", None, None),
        P("phase", None, None),
        P("phase", None, None),
        P("phase", None, None),
        P("phase", None, None),
    )
    out_specs = P("phase", None, "tm", None)
    return jax.shard_map(
        per_device, mesh=mesh, in_specs=in_specs, out_specs=out_specs, check_vma=False
    )
```

```python
import functools
import math

import jax
import jax.numpy as jnp
from jax import lax
from jax.experimental import pallas as pl
from jax.experimental.pallas import tpu as pltpu
from jax.sharding import PartitionSpec as P

HEADS = 16
SEG = 32
LC = 64
NMEM = 4
KW = 31

EPSILON = 1e-05
BACK = LC // SEG
HALO_SEGS = 1 + NMEM + BACK
HALO = HALO_SEGS * SEG
FAR = -1e30
OPEN = 3e38
TILE = 256
PAIR = 128
SHIFT = 5
HEAD_SHIFT = 4
VMEM_BYTES = 40 * 1024 * 1024


def layer_norms(number, load, store):
    means = [jnp.mean(load(s), axis=-1, keepdims=True) for s in range(number)]
    scales = []
    for s in range(number):
        center = load(s) - means[s]
        scales.append(lax.rsqrt(jnp.mean(center * center, axis=-1, keepdims=True) + EPSILON))
    for s in range(number):
        store(s, (load(s) - means[s]) * scales[s])


def dot(a, b):
    return jnp.dot(a, b, preferred_element_type=jnp.float32)


def dot_nt(a, b):
    return lax.dot_general(a, b, (((1,), (1,)), ((), ())), preferred_element_type=jnp.float32)


def halo_pieces(rows):
    pieces = []
    left = HALO
    while left > 0:
        take = min(rows, left)
        pieces.append((len(pieces) + 1, take))
        left -= take
    return pieces


def by_segment(index, counts, first, number):
    out = jnp.zeros(index.shape, jnp.int32)
    for s in range(number):
        out = jnp.where(index == s, counts[first + s], out)
    return out


def iota(shape, dimension):
    return lax.broadcasted_iota(jnp.int32, shape, dimension)


def layer_kernel(cfg, *refs):
    rows, width, section, chunk, sections, shards, segs_row, pieces = cfg
    refs = list(refs)
    info = refs[0]
    hbm_weights = refs[1:6]
    taps_hbm, source = refs[6:8]
    refs = refs[8:]
    count_p = len(pieces)
    halos, refs = refs[:count_p], refs[count_p:]
    if chunk > 0:
        befores, refs = refs[:count_p], refs[count_p:]
    if section + chunk > 0:
        refs = refs[1:]
    outputs, refs = refs[0], refs[1:]
    with_relay = section < sections - 1
    relays = []
    if with_relay:
        number = 1 + sum(1 for _, take in pieces if take < rows)
        relays, refs = refs[:number], refs[number:]
    (xe, normed, ke, ve, qe, ctx, res, cin, depth, gated, result, bias, mem_bias,
     wk, wv, wq, wo, wp, taps, wsem, xsem, osem) = refs

    ext = HALO + rows
    segs = ext // SEG
    q_rows = rows + SEG
    q_seg = HALO_SEGS - 1
    mem_first = q_seg - NMEM
    mems = segs - 1 - mem_first
    mem_pad = ke.shape[0] - ext
    key_seg = q_seg - BACK
    key_row = key_seg * SEG
    keys = ke.shape[0] - key_row
    win = ext - key_row
    head_dim = width // HEADS
    sum_rows = qe.shape[0] - q_rows
    phase, shard = info[0], info[1]

    @pl.when(phase == section)
    def _():
        own = xe.at[pl.ds(HALO, rows)]
        spots = []
        for distance, take in pieces:
            top = HALO - (distance - 1) * rows - take
            spots.append((distance, xe.at[pl.ds(top, take)]))
        own_copy = pltpu.make_async_copy(
            source.at[chunk] if section == 0 else source, own, xsem.at[0]
        )
        own_copy.start()
        for n, (distance, spot) in enumerate(spots):
            @pl.when(shard >= distance)
            def _():
                pltpu.make_async_copy(halos[n], spot, xsem.at[1 + n]).start()
            if chunk > 0:
                @pl.when(shard < distance)
                def _():
                    pltpu.make_async_copy(befores[n], spot, xsem.at[1 + n]).start()
        names = (wk, wv, wq, wo, wp)
        loads = [
            pltpu.make_async_copy(hbm_weights[n], names[n], wsem.at[n]) for n in range(5)
        ]
        loads.append(pltpu.make_async_copy(taps_hbm, taps, wsem.at[5]))
        for n in range(3):
            loads[n].start()
        if chunk == 0:
            for distance, spot in spots:
                @pl.when(shard < distance)
                def _():
                    spot[...] = jnp.zeros(spot.shape, jnp.bfloat16)

        first = chunk * segs_row + shard * (rows // SEG) - HALO_SEGS
        counts = []
        for s in range(segs):
            g = first + s
            value = info[2 + jnp.maximum(g, 0)]
            counts.append(jnp.where(g >= 0, value, 0))

        row_seg = q_seg + (iota((q_rows, keys), 0) >> SHIFT)
        col = iota((q_rows, keys), 1)
        line = iota((1, keys), 1)
        kvalid = (line & (SEG - 1)) < by_segment(line >> SHIFT, counts, key_seg, win // SEG)
        mvalid = by_segment(line - win, counts, mem_first, mems) > 0
        live = (kvalid & (line < win)) | (mvalid & (line >= win))
        lows = jnp.where(line < win, key_seg + (line >> SHIFT), mem_first + 1 + line - win)
        highs = jnp.where(line < win, lows + BACK, lows + NMEM - 1)
        lows = jnp.where(live, lows, segs)
        good = (row_seg >= lows) & (row_seg <= highs)
        bias[...] = jnp.where(good, OPEN, FAR)

        mem_keys = mem_bias.shape[1]
        mseg = mem_first + (iota((mems * HEADS, mem_keys), 0) >> HEAD_SHIFT)
        mline = iota((1, mem_keys), 1)
        mlow = mline >> SHIFT
        mlive = (mline & (SEG - 1)) < by_segment(mlow, counts, 0, mem_keys // SEG)
        mhigh = mlow + BACK
        mlow = jnp.where(mlive, mlow, segs)
        mem_bias[...] = jnp.where((mseg >= mlow) & (mseg <= mhigh), OPEN, FAR)

        own_copy.wait()
        for n, (distance, spot) in enumerate(spots):
            if chunk > 0:
                pltpu.make_async_copy(halos[n], spot, xsem.at[1 + n]).wait()
            else:
                @pl.when(shard >= distance)
                def _():
                    pltpu.make_async_copy(halos[n], spot, xsem.at[1 + n]).wait()
        def set_normed(s, value):
            normed[pl.ds(s * SEG, SEG), :] = value.astype(jnp.bfloat16)

        layer_norms(segs, lambda s: xe[pl.ds(s * SEG, SEG), :].astype(jnp.float32), set_normed)

        def columns(n):
            return pl.ds(pl.multiple_of(n * TILE, TILE), TILE)

        def tiles(unroll):
            return pl.loop(0, width // TILE, unroll=unroll)

        sseg = iota((sum_rows, ext), 0) + mem_first
        sline = iota((1, ext), 1)
        smine = sline >> SHIFT
        slive = (sline & (SEG - 1)) < by_segment(smine, counts, 0, segs)
        smine = jnp.where(slive, smine, -1)
        pick = jnp.where(sseg == smine, 1.0, 0.0).astype(jnp.bfloat16)
        scount = by_segment(iota((sum_rows, 1), 0), counts, mem_first, mems)
        divisor = jnp.maximum(scount, 1).astype(jnp.float32)
        normed[pl.ds(ext, sum_rows), :] = (dot(pick, normed[pl.ds(0, ext), :]) / divisor).astype(
            jnp.bfloat16
        )

        scale = 1.0 / math.sqrt(head_dim)
        for n in range(3):
            loads[n].wait()
        for n in range(3, 6):
            loads[n].start()

        @tiles(2)
        def _(n):
            at = columns(n)
            block = normed[pl.ds(0, ext), :]
            ke[pl.ds(0, ext), at] = dot(block, wk[:, at]).astype(jnp.bfloat16)
            ve[pl.ds(0, ext), at] = dot(block, wv[:, at]).astype(jnp.bfloat16)
            askers = normed[pl.ds(ext - q_rows, q_rows + sum_rows), :]
            qe[:, at] = (dot(askers, wq[:, at]) * scale).astype(jnp.bfloat16)

        own_head = (iota((HEADS, width), 1) // head_dim) == iota((HEADS, width), 0)
        sq = qe[pl.ds(q_rows, sum_rows), :].astype(jnp.float32)
        spread_q = []
        for m in range(mems):
            line_q = jnp.broadcast_to(sq[m : m + 1, :], (HEADS, width))
            spread_q.append(jnp.where(own_head, line_q, 0.0).astype(jnp.bfloat16))
        spread_q = jnp.concatenate(spread_q)
        ms = jnp.minimum(dot_nt(spread_q, ke[pl.ds(0, mem_keys), :]), mem_bias[...])
        me = jnp.exp(ms - jnp.max(ms, axis=-1, keepdims=True))
        mw = me * (1.0 / jnp.sum(me, axis=-1, keepdims=True))
        mo = dot(mw.astype(jnp.bfloat16), ve[pl.ds(0, mem_keys), :])
        lines = []
        for m in range(mems):
            part = jnp.where(own_head, mo[m * HEADS : (m + 1) * HEADS, :], 0.0)
            lines.append(jnp.sum(part, axis=0, keepdims=True))
        lines.append(jnp.zeros((mem_pad - mems, width), jnp.float32))
        memory = jnp.concatenate(lines).astype(jnp.bfloat16)

        @tiles(4)
        def _(n):
            at = columns(n)
            ke[pl.ds(ext, mem_pad), at] = dot(memory, wk[:, at]).astype(jnp.bfloat16)
            ve[pl.ds(ext, mem_pad), at] = dot(memory, wv[:, at]).astype(jnp.bfloat16)

        even = iota((q_rows, PAIR), 1) < head_dim

        @pl.loop(0, width // PAIR, unroll=4)
        def _(n):
            at = pl.ds(pl.multiple_of(n * PAIR, PAIR), PAIR)
            qp = qe[pl.ds(0, q_rows), at]
            zero = jnp.zeros_like(qp)
            q_both = jnp.concatenate([jnp.where(even, qp, zero), jnp.where(even, zero, qp)])
            raw = dot_nt(q_both, ke[pl.ds(key_row, keys), at])
            edge = bias[...]
            scores = jnp.minimum(raw, jnp.concatenate([edge, edge]))
            weight = jnp.exp(scores - jnp.max(scores, axis=-1, keepdims=True))
            inverse = 1.0 / jnp.sum(weight, axis=-1, keepdims=True)
            both = dot(weight.astype(jnp.bfloat16), ve[pl.ds(key_row, keys), at]) * inverse
            ctx[:, at] = jnp.where(even, both[:q_rows], both[q_rows:]).astype(jnp.bfloat16)

        loads[3].wait()

        @tiles(4)
        def _(n):
            at = columns(n)
            x_part = xe[pl.ds(ext - q_rows, q_rows), at].astype(jnp.float32)
            res[:, at] = (x_part + dot(ctx[...], wo[:, at])).astype(jnp.bfloat16)

        inner = iota((SEG, 1), 0)

        def set_cin(s, value):
            mask = (inner < counts[q_seg + s]).astype(jnp.float32)
            value = (value * mask).astype(jnp.bfloat16)
            cin[pl.ds(s * SEG, SEG), :] = value.astype(jnp.float32)

        layer_norms(
            q_rows // SEG, lambda s: res[pl.ds(s * SEG, SEG), :].astype(jnp.float32), set_cin
        )

        loads[5].wait()

        @pl.loop(0, width // PAIR)
        def _(n):
            at = pl.ds(pl.multiple_of(n * PAIR, PAIR), PAIR)
            total = jnp.zeros((rows, PAIR), jnp.float32)
            start = SEG - (KW - 1)
            for residue in range(8):
                offsets = [o for o in range(start, start + KW) if o % 8 == residue]
                size = offsets[-1] - residue + rows
                block = cin[pl.ds(residue, size), at]
                for o in offsets:
                    shifted = block[o - residue : o - residue + rows]
                    total = total + taps[pl.ds(o - start, 1), at] * shifted
            depth[:, at] = total

        def set_gated(s, value):
            value = value * (1.0 / (1.0 + jnp.exp(-value)))
            gated[pl.ds(s * SEG, SEG), :] = value.astype(jnp.bfloat16)

        layer_norms(rows // SEG, lambda s: depth[pl.ds(s * SEG, SEG), :], set_gated)

        loads[4].wait()
        frame = iota((rows, 1), 0)
        frame_count = by_segment(frame >> SHIFT, counts, HALO_SEGS, rows // SEG)
        row_mask = ((frame & (SEG - 1)) < frame_count).astype(jnp.float32)

        @tiles(4)
        def _(n):
            at = columns(n)
            mixed = res[pl.ds(SEG, rows), at].astype(jnp.float32) + dot(gated[...], wp[:, at])
            result[:, at] = (mixed * row_mask).astype(jnp.bfloat16)

        copies = []
        if with_relay:
            copies.append(pltpu.make_async_copy(result, relays[0], osem.at[1]))
            spot = 1
            for _, take in pieces:
                if take < rows:
                    tail = result.at[pl.ds(rows - take, take)]
                    copies.append(pltpu.make_async_copy(tail, relays[spot], osem.at[1 + spot]))
                    spot += 1
        copies.append(pltpu.make_async_copy(result, outputs.at[chunk], osem.at[0]))
        for copy in copies:
            copy.start()
        for copy in copies:
            copy.wait()


def per_device(frames, frame_counts, w_query, w_key, w_value, w_out, conv_kernel, w_point):
    micro, rows, width = frames.shape
    sections = lax.axis_size("phase")
    shards = lax.axis_size("tm")
    segs_row = frame_counts.shape[1]
    pieces = halo_pieces(rows)
    ext = HALO + rows
    q_rows = rows + SEG
    mems = ext // SEG - 1 - (HALO_SEGS - 1 - NMEM)
    mem_pad = -(-mems // SEG) * SEG
    sum_rows = -(-mems // 16) * 16
    mem_keys = (mems + BACK) * SEG
    keys = ext + mem_pad - (HALO_SEGS - 1 - BACK) * SEG

    def send(block, distance, section, ahead):
        route = [
            (s * sections + section, (s + distance) % shards * sections + section + ahead)
            for s in range(shards)
        ]
        return lax.ppermute(block, ("tm", "phase"), route)

    inbox = []
    for chunk in range(micro):
        halos = [
            send(frames[chunk, rows - take :, :], distance, 0, 0) for distance, take in pieces
        ]
        inbox.append([None, *halos])

    where = jnp.stack([lax.axis_index("phase"), lax.axis_index("tm")]).astype(jnp.int32)
    info = jnp.concatenate([where, frame_counts.reshape(-1)])
    taps = jnp.pad(conv_kernel[0].astype(jnp.float32), ((0, 32 - KW), (0, 0)))

    def vmem(*shape, dtype=jnp.bfloat16):
        return pltpu.VMEM(shape, dtype)

    scratch = [
        vmem(ext, width), vmem(ext + sum_rows, width), vmem(ext + mem_pad, width), vmem(ext + mem_pad, width),
        vmem(q_rows + sum_rows, width), vmem(q_rows, width), vmem(q_rows, width),
        vmem(q_rows, width, dtype=jnp.float32), vmem(rows, width, dtype=jnp.float32),
        vmem(rows, width), vmem(rows, width),
        vmem(q_rows, keys, dtype=jnp.float32), vmem(mems * HEADS, mem_keys, dtype=jnp.float32),
        vmem(width, width), vmem(width, width), vmem(width, width), vmem(width, width),
        vmem(width, width), vmem(32, width, dtype=jnp.float32),
        pltpu.SemaphoreType.DMA((6,)),
        pltpu.SemaphoreType.DMA((1 + len(pieces),)),
        pltpu.SemaphoreType.DMA((2 + len(pieces),)),
    ]
    smem = pl.BlockSpec(memory_space=pltpu.SMEM)
    any_space = pl.BlockSpec(memory_space=pl.ANY)
    hbm = pl.BlockSpec(memory_space=pltpu.HBM)
    weights = [
        pltpu.with_memory_space_constraint(w[0], pltpu.HBM)
        for w in (w_key, w_value, w_query, w_out, w_point)
    ]
    frames_kept = pltpu.with_memory_space_constraint(frames, pltpu.HBM)
    block = jax.ShapeDtypeStruct((rows, width), jnp.bfloat16)
    tails = [
        jax.ShapeDtypeStruct((take, width), jnp.bfloat16) for _, take in pieces if take < rows
    ]
    whole = jax.ShapeDtypeStruct((micro, rows, width), jnp.bfloat16)
    cost = pl.CostEstimate(flops=6 * 10**9, bytes_accessed=12 * 10**6, transcendentals=10**6)

    outputs = None
    for section in range(sections):
        outbox = []
        for chunk in range(micro):
            source = frames_kept if section == 0 else inbox[chunk][0]
            args = [info, *weights, taps, source, *inbox[chunk][1:]]
            if chunk > 0:
                args += inbox[chunk - 1][1:]
            in_specs = [smem] + [hbm] * 7 + [any_space] * (len(args) - 8)
            if section > 0:
                in_specs[7] = any_space
            aliases = {}
            if outputs is not None:
                aliases = {len(args): 0}
                args.append(outputs)
                in_specs.append(hbm)
            last = section == sections - 1
            outs = [whole] if last else [whole, block, *tails]
            cfg = (rows, width, section, chunk, sections, shards, segs_row, pieces)
            made = pl.pallas_call(
                functools.partial(layer_kernel, cfg),
                out_shape=outs,
                in_specs=in_specs,
                out_specs=[hbm] + [any_space] * (len(outs) - 1),
                scratch_shapes=scratch,
                input_output_aliases=aliases,
                cost_estimate=cost,
                compiler_params=pltpu.CompilerParams(vmem_limit_bytes=VMEM_BYTES),
                name="layer",
            )(*args)
            outputs = made[0]
            if not last:
                tail_of = iter(made[2:])
                got = [
                    send(next(tail_of) if take < rows else made[1], distance, section, 1)
                    for distance, take in pieces
                ]
                outbox.append([send(made[1], 0, section, 1), *got])
        inbox = outbox
    return outputs[None]


def solution(mesh):
    in_specs = (
        P(None, "tm", None),
        P(),
        P("phase", None, None),
        P("phase", None, None),
        P("phase", None, None),
        P("phase", None, None),
        P("phase", None, None),
        P("phase", None, None),
    )
    out_specs = P("phase", None, "tm", None)
    return jax.shard_map(
        per_device, mesh=mesh, in_specs=in_specs, out_specs=out_specs, check_vma=False
    )
```

```python
import functools
import math

import jax
import jax.numpy as jnp
from jax import lax
from jax.experimental import pallas as pl
from jax.experimental.pallas import tpu as pltpu
from jax.sharding import PartitionSpec as P

HEADS = 16
SEG = 32
LC = 64
NMEM = 4
KW = 31

EPSILON = 1e-05
BACK = LC // SEG
HALO_SEGS = 1 + NMEM + BACK
HALO = HALO_SEGS * SEG
FAR = -1e30
OPEN = 3e38
TILE = 256
PAIR = 128
SHIFT = 5
HEAD_SHIFT = 4
VMEM_BYTES = 32 * 1024 * 1024


def layer_norms(number, load, store):
    means = [jnp.mean(load(s), axis=-1, keepdims=True) for s in range(number)]
    scales = []
    for s in range(number):
        center = load(s) - means[s]
        scales.append(lax.rsqrt(jnp.mean(center * center, axis=-1, keepdims=True) + EPSILON))
    for s in range(number):
        store(s, (load(s) - means[s]) * scales[s])


def dot(a, b):
    return jnp.dot(a, b, preferred_element_type=jnp.float32)


def dot_nt(a, b):
    return lax.dot_general(a, b, (((1,), (1,)), ((), ())), preferred_element_type=jnp.float32)


def halo_pieces(rows):
    pieces = []
    left = HALO
    while left > 0:
        take = min(rows, left)
        pieces.append((len(pieces) + 1, take))
        left -= take
    return pieces


def by_segment(index, counts, first, number):
    out = jnp.zeros(index.shape, jnp.int32)
    for s in range(number):
        out = jnp.where(index == s, counts[first + s], out)
    return out


def iota(shape, dimension):
    return lax.broadcasted_iota(jnp.int32, shape, dimension)


def layer_kernel(cfg, *refs):
    rows, width, section, chunk, sections, shards, segs_row, pieces = cfg
    refs = list(refs)
    info = refs[0]
    wk, wv, wq, wo, wp, taps, source = refs[1:8]
    refs = refs[8:]
    count_p = len(pieces)
    halos, refs = refs[:count_p], refs[count_p:]
    if chunk > 0:
        befores, refs = refs[:count_p], refs[count_p:]
    if section + chunk > 0:
        refs = refs[1:]
    outputs, refs = refs[0], refs[1:]
    with_relay = section < sections - 1
    relays = []
    if with_relay:
        number = 1 + sum(1 for _, take in pieces if take < rows)
        relays, refs = refs[:number], refs[number:]
    (xe, normed, ke, ve, qe, ctx, res, cin, depth, gated, result, bias, mem_bias,
     xsem, osem) = refs

    ext = HALO + rows
    segs = ext // SEG
    q_rows = rows + SEG
    q_seg = HALO_SEGS - 1
    mem_first = q_seg - NMEM
    mems = segs - 1 - mem_first
    mem_pad = ke.shape[0] - ext
    key_seg = q_seg - BACK
    key_row = key_seg * SEG
    keys = ke.shape[0] - key_row
    win = ext - key_row
    head_dim = width // HEADS
    sum_rows = qe.shape[0] - q_rows
    phase, shard = info[0], info[1]

    @pl.when(phase == section)
    def _():
        own = xe.at[pl.ds(HALO, rows)]
        spots = []
        for distance, take in pieces:
            top = HALO - (distance - 1) * rows - take
            spots.append((distance, xe.at[pl.ds(top, take)]))
        own_copy = pltpu.make_async_copy(
            source.at[chunk] if section == 0 else source, own, xsem.at[0]
        )
        own_copy.start()
        for n, (distance, spot) in enumerate(spots):
            @pl.when(shard >= distance)
            def _():
                pltpu.make_async_copy(halos[n], spot, xsem.at[1 + n]).start()
            if chunk > 0:
                @pl.when(shard < distance)
                def _():
                    pltpu.make_async_copy(befores[n], spot, xsem.at[1 + n]).start()
        if chunk == 0:
            for distance, spot in spots:
                @pl.when(shard < distance)
                def _():
                    spot[...] = jnp.zeros(spot.shape, jnp.bfloat16)

        first = chunk * segs_row + shard * (rows // SEG) - HALO_SEGS
        counts = []
        for s in range(segs):
            g = first + s
            value = info[2 + jnp.maximum(g, 0)]
            counts.append(jnp.where(g >= 0, value, 0))

        row_seg = q_seg + (iota((q_rows, keys), 0) >> SHIFT)
        col = iota((q_rows, keys), 1)
        line = iota((1, keys), 1)
        kvalid = (line & (SEG - 1)) < by_segment(line >> SHIFT, counts, key_seg, win // SEG)
        mvalid = by_segment(line - win, counts, mem_first, mems) > 0
        live = (kvalid & (line < win)) | (mvalid & (line >= win))
        lows = jnp.where(line < win, key_seg + (line >> SHIFT), mem_first + 1 + line - win)
        highs = jnp.where(line < win, lows + BACK, lows + NMEM - 1)
        lows = jnp.where(live, lows, segs)
        good = (row_seg >= lows) & (row_seg <= highs)
        bias[...] = jnp.where(good, OPEN, FAR)

        mem_keys = mem_bias.shape[1]
        mseg = mem_first + (iota((mems * HEADS, mem_keys), 0) >> HEAD_SHIFT)
        mline = iota((1, mem_keys), 1)
        mlow = mline >> SHIFT
        mlive = (mline & (SEG - 1)) < by_segment(mlow, counts, 0, mem_keys // SEG)
        mhigh = mlow + BACK
        mlow = jnp.where(mlive, mlow, segs)
        mem_bias[...] = jnp.where((mseg >= mlow) & (mseg <= mhigh), OPEN, FAR)

        own_copy.wait()
        for n, (distance, spot) in enumerate(spots):
            if chunk > 0:
                pltpu.make_async_copy(halos[n], spot, xsem.at[1 + n]).wait()
            else:
                @pl.when(shard >= distance)
                def _():
                    pltpu.make_async_copy(halos[n], spot, xsem.at[1 + n]).wait()
        def set_normed(s, value):
            normed[pl.ds(s * SEG, SEG), :] = value.astype(jnp.bfloat16)

        layer_norms(segs, lambda s: xe[pl.ds(s * SEG, SEG), :].astype(jnp.float32), set_normed)

        def columns(n):
            return pl.ds(pl.multiple_of(n * TILE, TILE), TILE)

        def tiles(unroll):
            return pl.loop(0, width // TILE, unroll=unroll)

        sseg = iota((sum_rows, ext), 0) + mem_first
        sline = iota((1, ext), 1)
        smine = sline >> SHIFT
        slive = (sline & (SEG - 1)) < by_segment(smine, counts, 0, segs)
        smine = jnp.where(slive, smine, -1)
        pick = jnp.where(sseg == smine, 1.0, 0.0).astype(jnp.bfloat16)
        scount = by_segment(iota((sum_rows, 1), 0), counts, mem_first, mems)
        divisor = jnp.maximum(scount, 1).astype(jnp.float32)
        normed[pl.ds(ext, sum_rows), :] = (dot(pick, normed[pl.ds(0, ext), :]) / divisor).astype(
            jnp.bfloat16
        )

        scale = 1.0 / math.sqrt(head_dim)

        @tiles(2)
        def _(n):
            at = columns(n)
            block = normed[pl.ds(0, ext), :]
            ke[pl.ds(0, ext), at] = dot(block, wk[:, at]).astype(jnp.bfloat16)
            ve[pl.ds(0, ext), at] = dot(block, wv[:, at]).astype(jnp.bfloat16)
            askers = normed[pl.ds(ext - q_rows, q_rows + sum_rows), :]
            qe[:, at] = (dot(askers, wq[:, at]) * scale).astype(jnp.bfloat16)

        own_head = (iota((HEADS, width), 1) // head_dim) == iota((HEADS, width), 0)
        sq = qe[pl.ds(q_rows, sum_rows), :].astype(jnp.float32)
        spread_q = []
        for m in range(mems):
            line_q = jnp.broadcast_to(sq[m : m + 1, :], (HEADS, width))
            spread_q.append(jnp.where(own_head, line_q, 0.0).astype(jnp.bfloat16))
        spread_q = jnp.concatenate(spread_q)
        ms = jnp.minimum(dot_nt(spread_q, ke[pl.ds(0, mem_keys), :]), mem_bias[...])
        me = jnp.exp(ms - jnp.max(ms, axis=-1, keepdims=True))
        mw = me * (1.0 / jnp.sum(me, axis=-1, keepdims=True))
        mo = dot(mw.astype(jnp.bfloat16), ve[pl.ds(0, mem_keys), :])
        lines = []
        for m in range(mems):
            part = jnp.where(own_head, mo[m * HEADS : (m + 1) * HEADS, :], 0.0)
            lines.append(jnp.sum(part, axis=0, keepdims=True))
        lines.append(jnp.zeros((mem_pad - mems, width), jnp.float32))
        memory = jnp.concatenate(lines).astype(jnp.bfloat16)

        @tiles(4)
        def _(n):
            at = columns(n)
            ke[pl.ds(ext, mem_pad), at] = dot(memory, wk[:, at]).astype(jnp.bfloat16)
            ve[pl.ds(ext, mem_pad), at] = dot(memory, wv[:, at]).astype(jnp.bfloat16)

        even = iota((q_rows, PAIR), 1) < head_dim

        @pl.loop(0, width // PAIR, unroll=4)
        def _(n):
            at = pl.ds(pl.multiple_of(n * PAIR, PAIR), PAIR)
            qp = qe[pl.ds(0, q_rows), at]
            zero = jnp.zeros_like(qp)
            q_both = jnp.concatenate([jnp.where(even, qp, zero), jnp.where(even, zero, qp)])
            raw = dot_nt(q_both, ke[pl.ds(key_row, keys), at])
            edge = bias[...]
            scores = jnp.minimum(raw, jnp.concatenate([edge, edge]))
            weight = jnp.exp(scores - jnp.max(scores, axis=-1, keepdims=True))
            inverse = 1.0 / jnp.sum(weight, axis=-1, keepdims=True)
            both = dot(weight.astype(jnp.bfloat16), ve[pl.ds(key_row, keys), at]) * inverse
            ctx[:, at] = jnp.where(even, both[:q_rows], both[q_rows:]).astype(jnp.bfloat16)

        @tiles(4)
        def _(n):
            at = columns(n)
            x_part = xe[pl.ds(ext - q_rows, q_rows), at].astype(jnp.float32)
            res[:, at] = (x_part + dot(ctx[...], wo[:, at])).astype(jnp.bfloat16)

        inner = iota((SEG, 1), 0)

        def set_cin(s, value):
            mask = (inner < counts[q_seg + s]).astype(jnp.float32)
            value = (value * mask).astype(jnp.bfloat16)
            cin[pl.ds(s * SEG, SEG), :] = value.astype(jnp.float32)

        layer_norms(
            q_rows // SEG, lambda s: res[pl.ds(s * SEG, SEG), :].astype(jnp.float32), set_cin
        )

        @pl.loop(0, width // PAIR)
        def _(n):
            at = pl.ds(pl.multiple_of(n * PAIR, PAIR), PAIR)
            total = jnp.zeros((rows, PAIR), jnp.float32)
            block = cin[:, at]
            start = SEG - (KW - 1)
            for residue in range(8):
                size = rows + (8 if residue else 0)
                part = None
                for o in range(start, start + KW):
                    if o % 8 == residue:
                        base = o - residue
                        term = taps[pl.ds(o - start, 1), at] * block[base : base + size]
                        part = term if part is None else part + term
                if residue:
                    part = pltpu.roll(part, size - residue, 0)[:rows]
                total = total + part
            depth[:, at] = total

        def set_gated(s, value):
            value = value * (1.0 / (1.0 + jnp.exp(-value)))
            gated[pl.ds(s * SEG, SEG), :] = value.astype(jnp.bfloat16)

        layer_norms(rows // SEG, lambda s: depth[pl.ds(s * SEG, SEG), :], set_gated)

        frame = iota((rows, 1), 0)
        frame_count = by_segment(frame >> SHIFT, counts, HALO_SEGS, rows // SEG)
        row_mask = ((frame & (SEG - 1)) < frame_count).astype(jnp.float32)

        @tiles(4)
        def _(n):
            at = columns(n)
            mixed = res[pl.ds(SEG, rows), at].astype(jnp.float32) + dot(gated[...], wp[:, at])
            result[:, at] = (mixed * row_mask).astype(jnp.bfloat16)

        copies = []
        if with_relay:
            copies.append(pltpu.make_async_copy(result, relays[0], osem.at[1]))
            spot = 1
            for _, take in pieces:
                if take < rows:
                    tail = result.at[pl.ds(rows - take, take)]
                    copies.append(pltpu.make_async_copy(tail, relays[spot], osem.at[1 + spot]))
                    spot += 1
        copies.append(pltpu.make_async_copy(result, outputs.at[chunk], osem.at[0]))
        for copy in copies:
            copy.start()
        for copy in copies:
            copy.wait()


def load_kernel(*refs):
    sources, kernel, targets, taps, sem = refs[:5], refs[5], refs[6:11], refs[11], refs[12]
    copies = [
        pltpu.make_async_copy(source, target, sem.at[n])
        for n, (source, target) in enumerate(zip(sources, targets))
    ]
    for copy in copies:
        copy.start()
    taps[pl.ds(0, KW), :] = kernel[...].astype(jnp.float32)
    for copy in copies:
        copy.wait()


def per_device(frames, frame_counts, w_query, w_key, w_value, w_out, conv_kernel, w_point):
    micro, rows, width = frames.shape
    sections = lax.axis_size("phase")
    shards = lax.axis_size("tm")
    segs_row = frame_counts.shape[1]
    pieces = halo_pieces(rows)
    ext = HALO + rows
    q_rows = rows + SEG
    mems = ext // SEG - 1 - (HALO_SEGS - 1 - NMEM)
    mem_pad = -(-mems // SEG) * SEG
    sum_rows = -(-mems // 16) * 16
    mem_keys = (mems + BACK) * SEG
    keys = ext + mem_pad - (HALO_SEGS - 1 - BACK) * SEG

    def send(block, distance, section, ahead):
        route = [
            (s * sections + section, (s + distance) % shards * sections + section + ahead)
            for s in range(shards)
        ]
        return lax.ppermute(block, ("tm", "phase"), route)

    inbox = []
    for chunk in range(micro):
        halos = [
            send(frames[chunk, rows - take :, :], distance, 0, 0) for distance, take in pieces
        ]
        inbox.append([None, *halos])

    where = jnp.stack([lax.axis_index("phase"), lax.axis_index("tm")]).astype(jnp.int32)
    info = jnp.concatenate([where, frame_counts.reshape(-1)])

    def vmem(*shape, dtype=jnp.bfloat16):
        return pltpu.VMEM(shape, dtype)

    scratch = [
        vmem(ext, width), vmem(ext + sum_rows, width), vmem(ext + mem_pad, width), vmem(ext + mem_pad, width),
        vmem(q_rows + sum_rows, width), vmem(q_rows, width), vmem(q_rows, width),
        vmem(q_rows, width, dtype=jnp.float32), vmem(rows, width, dtype=jnp.float32),
        vmem(rows, width), vmem(rows, width),
        vmem(q_rows, keys, dtype=jnp.float32), vmem(mems * HEADS, mem_keys, dtype=jnp.float32),
        pltpu.SemaphoreType.DMA((1 + len(pieces),)),
        pltpu.SemaphoreType.DMA((2 + len(pieces),)),
    ]
    smem = pl.BlockSpec(memory_space=pltpu.SMEM)
    any_space = pl.BlockSpec(memory_space=pl.ANY)
    hbm = pl.BlockSpec(memory_space=pltpu.HBM)
    in_vmem = pl.BlockSpec(memory_space=pltpu.VMEM)
    weights = pl.pallas_call(
        load_kernel,
        out_shape=[vmem(width, width)] * 5 + [vmem(32, width, dtype=jnp.float32)],
        in_specs=[hbm] * 5 + [in_vmem],
        out_specs=[in_vmem] * 6,
        scratch_shapes=[pltpu.SemaphoreType.DMA((5,))],
        cost_estimate=pl.CostEstimate(flops=0, bytes_accessed=10**7, transcendentals=0),
        compiler_params=pltpu.CompilerParams(vmem_limit_bytes=4 * 1024 * 1024),
        name="load",
    )(
        *[
            pltpu.with_memory_space_constraint(w[0], pltpu.HBM)
            for w in (w_key, w_value, w_query, w_out, w_point)
        ],
        conv_kernel[0],
    )
    weights = [pltpu.with_memory_space_constraint(w, pltpu.VMEM) for w in weights]
    frames_kept = pltpu.with_memory_space_constraint(frames, pltpu.HBM)
    block = jax.ShapeDtypeStruct((rows, width), jnp.bfloat16)
    tails = [
        jax.ShapeDtypeStruct((take, width), jnp.bfloat16) for _, take in pieces if take < rows
    ]
    whole = jax.ShapeDtypeStruct((micro, rows, width), jnp.bfloat16)
    cost = pl.CostEstimate(flops=6 * 10**9, bytes_accessed=12 * 10**6, transcendentals=10**6)

    outputs = None
    for section in range(sections):
        outbox = []
        for chunk in range(micro):
            source = frames_kept if section == 0 else inbox[chunk][0]
            args = [info, *weights, source, *inbox[chunk][1:]]
            if chunk > 0:
                args += inbox[chunk - 1][1:]
            in_specs = [smem] + [in_vmem] * 6 + [any_space] * (len(args) - 7)
            if section == 0:
                in_specs[7] = hbm
            aliases = {}
            if outputs is not None:
                aliases = {len(args): 0}
                args.append(outputs)
                in_specs.append(hbm)
            last = section == sections - 1
            outs = [whole] if last else [whole, block, *tails]
            cfg = (rows, width, section, chunk, sections, shards, segs_row, pieces)
            made = pl.pallas_call(
                functools.partial(layer_kernel, cfg),
                out_shape=outs,
                in_specs=in_specs,
                out_specs=[hbm] + [any_space] * (len(outs) - 1),
                scratch_shapes=scratch,
                input_output_aliases=aliases,
                cost_estimate=cost,
                compiler_params=pltpu.CompilerParams(vmem_limit_bytes=VMEM_BYTES),
                name="layer",
            )(*args)
            outputs = made[0]
            if not last:
                tail_of = iter(made[2:])
                got = [
                    send(next(tail_of) if take < rows else made[1], distance, section, 1)
                    for distance, take in pieces
                ]
                outbox.append([send(made[1], 0, section, 1), *got])
        inbox = outbox
    return outputs[None]


def solution(mesh):
    in_specs = (
        P(None, "tm", None),
        P(),
        P("phase", None, None),
        P("phase", None, None),
        P("phase", None, None),
        P("phase", None, None),
        P("phase", None, None),
        P("phase", None, None),
    )
    out_specs = P("phase", None, "tm", None)
    return jax.shard_map(
        per_device, mesh=mesh, in_specs=in_specs, out_specs=out_specs, check_vma=False
    )
```

```python
import functools
import math

import jax
import jax.numpy as jnp
from jax import lax
from jax.experimental import pallas as pl
from jax.experimental.pallas import tpu as pltpu
from jax.sharding import PartitionSpec as P

HEADS = 16
SEG = 32
LC = 64
NMEM = 4
KW = 31

EPSILON = 1e-05
BACK = LC // SEG
HALO_SEGS = 1 + NMEM + BACK
HALO = HALO_SEGS * SEG
FAR = -1e30
OPEN = 3e38
TILE = 256
PAIR = 128
SHIFT = 5
HEAD_SHIFT = 4
VMEM_BYTES = 32 * 1024 * 1024


def layer_norms(number, load, store):
    means = [jnp.mean(load(s), axis=-1, keepdims=True) for s in range(number)]
    scales = []
    for s in range(number):
        center = load(s) - means[s]
        scales.append(lax.rsqrt(jnp.mean(center * center, axis=-1, keepdims=True) + EPSILON))
    for s in range(number):
        store(s, (load(s) - means[s]) * scales[s])


def dot(a, b):
    return jnp.dot(a, b, preferred_element_type=jnp.float32)


def dot_nt(a, b):
    return lax.dot_general(a, b, (((1,), (1,)), ((), ())), preferred_element_type=jnp.float32)


def halo_pieces(rows):
    pieces = []
    left = HALO
    while left > 0:
        take = min(rows, left)
        pieces.append((len(pieces) + 1, take))
        left -= take
    return pieces


def by_segment(index, counts, first, number):
    out = jnp.zeros(index.shape, jnp.int32)
    for s in range(number):
        out = jnp.where(index == s, counts[first + s], out)
    return out


def iota(shape, dimension):
    return lax.broadcasted_iota(jnp.int32, shape, dimension)


def layer_kernel(cfg, *refs):
    rows, width, section, chunk, sections, shards, segs_row, pieces = cfg
    refs = list(refs)
    info = refs[0]
    wk, wv, wq, wo, wp, taps = refs[1:7]
    refs = refs[7:]
    count_p = len(pieces)
    halos, source, refs = refs[:count_p][::-1], refs[count_p], refs[count_p + 1 :]
    if section == 0:
        befores = [halo.at[max(chunk - 1, 0)] for halo in halos]
        halos = [halo.at[chunk] for halo in halos]
    elif chunk > 0:
        befores, refs = refs[:count_p], refs[count_p:]
    if section + chunk > 0:
        refs = refs[1:]
    outputs, refs = refs[0], refs[1:]
    with_relay = section < sections - 1
    relays = []
    if with_relay:
        number = 1 + sum(1 for _, take in pieces if take < rows)
        relays, refs = refs[:number], refs[number:]
    (xe, normed, ke, ve, qe, ctx, res, cin, depth, gated, result, bias, mem_bias,
     xsem, osem) = refs

    ext = HALO + rows
    segs = ext // SEG
    q_rows = rows + SEG
    q_seg = HALO_SEGS - 1
    mem_first = q_seg - NMEM
    mems = segs - 1 - mem_first
    mem_pad = ke.shape[0] - ext
    key_seg = q_seg - BACK
    key_row = key_seg * SEG
    keys = ke.shape[0] - key_row
    win = ext - key_row
    head_dim = width // HEADS
    sum_rows = qe.shape[0] - q_rows
    phase, shard = info[0], info[1]

    @pl.when(phase == section)
    def _():
        own = xe.at[pl.ds(HALO, rows)]
        spots = []
        for distance, take in pieces:
            top = HALO - (distance - 1) * rows - take
            spots.append((distance, xe.at[pl.ds(top, take)]))
        own_copy = pltpu.make_async_copy(
            source.at[chunk] if section == 0 else source, own, xsem.at[0]
        )
        own_copy.start()
        for n, (distance, spot) in enumerate(spots):
            @pl.when(shard >= distance)
            def _():
                pltpu.make_async_copy(halos[n], spot, xsem.at[1 + n]).start()
            if chunk > 0:
                @pl.when(shard < distance)
                def _():
                    pltpu.make_async_copy(befores[n], spot, xsem.at[1 + n]).start()
        if chunk == 0:
            for distance, spot in spots:
                @pl.when(shard < distance)
                def _():
                    spot[...] = jnp.zeros(spot.shape, jnp.bfloat16)

        first = chunk * segs_row + shard * (rows // SEG) - HALO_SEGS
        counts = []
        for s in range(segs):
            g = first + s
            value = info[2 + jnp.maximum(g, 0)]
            counts.append(jnp.where(g >= 0, value, 0))

        row_seg = q_seg + (iota((q_rows, keys), 0) >> SHIFT)
        col = iota((q_rows, keys), 1)
        line = iota((1, keys), 1)
        kvalid = (line & (SEG - 1)) < by_segment(line >> SHIFT, counts, key_seg, win // SEG)
        mvalid = by_segment(line - win, counts, mem_first, mems) > 0
        live = (kvalid & (line < win)) | (mvalid & (line >= win))
        lows = jnp.where(line < win, key_seg + (line >> SHIFT), mem_first + 1 + line - win)
        highs = jnp.where(line < win, lows + BACK, lows + NMEM - 1)
        lows = jnp.where(live, lows, segs)
        good = (row_seg >= lows) & (row_seg <= highs)
        bias[...] = jnp.where(good, OPEN, FAR)

        mem_keys = mem_bias.shape[1]
        mseg = mem_first + (iota((mems * HEADS, mem_keys), 0) >> HEAD_SHIFT)
        mline = iota((1, mem_keys), 1)
        mlow = mline >> SHIFT
        mlive = (mline & (SEG - 1)) < by_segment(mlow, counts, 0, mem_keys // SEG)
        mhigh = mlow + BACK
        mlow = jnp.where(mlive, mlow, segs)
        mem_bias[...] = jnp.where((mseg >= mlow) & (mseg <= mhigh), OPEN, FAR)

        own_copy.wait()
        for n, (distance, spot) in enumerate(spots):
            if chunk > 0:
                pltpu.make_async_copy(halos[n], spot, xsem.at[1 + n]).wait()
            else:
                @pl.when(shard >= distance)
                def _():
                    pltpu.make_async_copy(halos[n], spot, xsem.at[1 + n]).wait()
        def set_normed(s, value):
            normed[pl.ds(s * SEG, SEG), :] = value.astype(jnp.bfloat16)

        layer_norms(segs, lambda s: xe[pl.ds(s * SEG, SEG), :].astype(jnp.float32), set_normed)

        def columns(n):
            return pl.ds(pl.multiple_of(n * TILE, TILE), TILE)

        def tiles(unroll):
            return pl.loop(0, width // TILE, unroll=unroll)

        sseg = iota((sum_rows, ext), 0) + mem_first
        sline = iota((1, ext), 1)
        smine = sline >> SHIFT
        slive = (sline & (SEG - 1)) < by_segment(smine, counts, 0, segs)
        smine = jnp.where(slive, smine, -1)
        pick = jnp.where(sseg == smine, 1.0, 0.0).astype(jnp.bfloat16)
        scount = by_segment(iota((sum_rows, 1), 0), counts, mem_first, mems)
        divisor = jnp.maximum(scount, 1).astype(jnp.float32)
        normed[pl.ds(ext, sum_rows), :] = (dot(pick, normed[pl.ds(0, ext), :]) / divisor).astype(
            jnp.bfloat16
        )

        scale = 1.0 / math.sqrt(head_dim)

        @tiles(2)
        def _(n):
            at = columns(n)
            block = normed[pl.ds(0, ext), :]
            ke[pl.ds(0, ext), at] = dot(block, wk[:, at]).astype(jnp.bfloat16)
            ve[pl.ds(0, ext), at] = dot(block, wv[:, at]).astype(jnp.bfloat16)
            askers = normed[pl.ds(ext - q_rows, q_rows + sum_rows), :]
            qe[:, at] = (dot(askers, wq[:, at]) * scale).astype(jnp.bfloat16)

        own_head = (iota((HEADS, width), 1) // head_dim) == iota((HEADS, width), 0)
        sq = qe[pl.ds(q_rows, sum_rows), :].astype(jnp.float32)
        spread_q = []
        for m in range(mems):
            line_q = jnp.broadcast_to(sq[m : m + 1, :], (HEADS, width))
            spread_q.append(jnp.where(own_head, line_q, 0.0).astype(jnp.bfloat16))
        spread_q = jnp.concatenate(spread_q)
        ms = jnp.minimum(dot_nt(spread_q, ke[pl.ds(0, mem_keys), :]), mem_bias[...])
        me = jnp.exp(ms - jnp.max(ms, axis=-1, keepdims=True))
        mw = me * (1.0 / jnp.sum(me, axis=-1, keepdims=True))
        mo = dot(mw.astype(jnp.bfloat16), ve[pl.ds(0, mem_keys), :])
        lines = []
        for m in range(mems):
            part = jnp.where(own_head, mo[m * HEADS : (m + 1) * HEADS, :], 0.0)
            lines.append(jnp.sum(part, axis=0, keepdims=True))
        lines.append(jnp.zeros((mem_pad - mems, width), jnp.float32))
        memory = jnp.concatenate(lines).astype(jnp.bfloat16)

        @tiles(4)
        def _(n):
            at = columns(n)
            ke[pl.ds(ext, mem_pad), at] = dot(memory, wk[:, at]).astype(jnp.bfloat16)
            ve[pl.ds(ext, mem_pad), at] = dot(memory, wv[:, at]).astype(jnp.bfloat16)

        even = iota((q_rows, PAIR), 1) < head_dim

        @pl.loop(0, width // PAIR, unroll=4)
        def _(n):
            at = pl.ds(pl.multiple_of(n * PAIR, PAIR), PAIR)
            qp = qe[pl.ds(0, q_rows), at]
            zero = jnp.zeros_like(qp)
            q_both = jnp.concatenate([jnp.where(even, qp, zero), jnp.where(even, zero, qp)])
            raw = dot_nt(q_both, ke[pl.ds(key_row, keys), at])
            edge = bias[...]
            scores = jnp.minimum(raw, jnp.concatenate([edge, edge]))
            weight = jnp.exp(scores - jnp.max(scores, axis=-1, keepdims=True))
            inverse = 1.0 / jnp.sum(weight, axis=-1, keepdims=True)
            both = dot(weight.astype(jnp.bfloat16), ve[pl.ds(key_row, keys), at]) * inverse
            ctx[:, at] = jnp.where(even, both[:q_rows], both[q_rows:]).astype(jnp.bfloat16)

        @tiles(4)
        def _(n):
            at = columns(n)
            x_part = xe[pl.ds(ext - q_rows, q_rows), at].astype(jnp.float32)
            res[:, at] = (x_part + dot(ctx[...], wo[:, at])).astype(jnp.bfloat16)

        inner = iota((SEG, 1), 0)

        def set_cin(s, value):
            mask = (inner < counts[q_seg + s]).astype(jnp.float32)
            value = (value * mask).astype(jnp.bfloat16)
            cin[pl.ds(s * SEG, SEG), :] = value.astype(jnp.float32)

        layer_norms(
            q_rows // SEG, lambda s: res[pl.ds(s * SEG, SEG), :].astype(jnp.float32), set_cin
        )

        @pl.loop(0, width // PAIR)
        def _(n):
            at = pl.ds(pl.multiple_of(n * PAIR, PAIR), PAIR)
            total = jnp.zeros((rows, PAIR), jnp.float32)
            block = cin[:, at]
            start = SEG - (KW - 1)
            for residue in range(8):
                size = rows + (8 if residue else 0)
                part = None
                for o in range(start, start + KW):
                    if o % 8 == residue:
                        base = o - residue
                        term = taps[pl.ds(o - start, 1), at] * block[base : base + size]
                        part = term if part is None else part + term
                if residue:
                    part = pltpu.roll(part, size - residue, 0)[:rows]
                total = total + part
            depth[:, at] = total

        def set_gated(s, value):
            value = value * (1.0 / (1.0 + jnp.exp(-value)))
            gated[pl.ds(s * SEG, SEG), :] = value.astype(jnp.bfloat16)

        layer_norms(rows // SEG, lambda s: depth[pl.ds(s * SEG, SEG), :], set_gated)

        frame = iota((rows, 1), 0)
        frame_count = by_segment(frame >> SHIFT, counts, HALO_SEGS, rows // SEG)
        row_mask = ((frame & (SEG - 1)) < frame_count).astype(jnp.float32)

        @tiles(4)
        def _(n):
            at = columns(n)
            mixed = res[pl.ds(SEG, rows), at].astype(jnp.float32) + dot(gated[...], wp[:, at])
            result[:, at] = (mixed * row_mask).astype(jnp.bfloat16)

        copies = []
        if with_relay:
            copies.append(pltpu.make_async_copy(result, relays[0], osem.at[1]))
            spot = 1
            for _, take in pieces:
                if take < rows:
                    tail = result.at[pl.ds(rows - take, take)]
                    copies.append(pltpu.make_async_copy(tail, relays[spot], osem.at[1 + spot]))
                    spot += 1
        copies.append(pltpu.make_async_copy(result, outputs.at[chunk], osem.at[0]))
        for copy in copies:
            copy.start()
        for copy in copies:
            copy.wait()


def load_kernel(*refs):
    sources, kernel, targets, taps, sem = refs[:5], refs[5], refs[6:11], refs[11], refs[12]
    copies = [
        pltpu.make_async_copy(source, target, sem.at[n])
        for n, (source, target) in enumerate(zip(sources, targets))
    ]
    for copy in copies:
        copy.start()
    taps[pl.ds(0, KW), :] = kernel[...].astype(jnp.float32)
    for copy in copies:
        copy.wait()


def per_device(frames, frame_counts, w_query, w_key, w_value, w_out, conv_kernel, w_point):
    micro, rows, width = frames.shape
    sections = lax.axis_size("phase")
    shards = lax.axis_size("tm")
    segs_row = frame_counts.shape[1]
    pieces = halo_pieces(rows)
    ext = HALO + rows
    q_rows = rows + SEG
    mems = ext // SEG - 1 - (HALO_SEGS - 1 - NMEM)
    mem_pad = -(-mems // SEG) * SEG
    sum_rows = -(-mems // 16) * 16
    mem_keys = (mems + BACK) * SEG
    keys = ext + mem_pad - (HALO_SEGS - 1 - BACK) * SEG

    def send(block, distance, source, target):
        route = [
            (s * sections + source, (s + distance) % shards * sections + target)
            for s in range(shards)
        ]
        return lax.ppermute(block, ("tm", "phase"), route)

    frame_halos = [
        send(frames[:, rows - take :, :], distance, distance % sections, 0)
        for distance, take in pieces
    ]
    inbox = [[None, *frame_halos] for _ in range(micro)]

    where = jnp.stack([lax.axis_index("phase"), lax.axis_index("tm")]).astype(jnp.int32)
    info = jnp.concatenate([where, frame_counts.reshape(-1)])

    def vmem(*shape, dtype=jnp.bfloat16):
        return pltpu.VMEM(shape, dtype)

    scratch = [
        vmem(ext, width), vmem(ext + sum_rows, width), vmem(ext + mem_pad, width), vmem(ext + mem_pad, width),
        vmem(q_rows + sum_rows, width), vmem(q_rows, width), vmem(q_rows, width),
        vmem(q_rows, width, dtype=jnp.float32), vmem(rows, width, dtype=jnp.float32),
        vmem(rows, width), vmem(rows, width),
        vmem(q_rows, keys, dtype=jnp.float32), vmem(mems * HEADS, mem_keys, dtype=jnp.float32),
        pltpu.SemaphoreType.DMA((1 + len(pieces),)),
        pltpu.SemaphoreType.DMA((2 + len(pieces),)),
    ]
    smem = pl.BlockSpec(memory_space=pltpu.SMEM)
    any_space = pl.BlockSpec(memory_space=pl.ANY)
    hbm = pl.BlockSpec(memory_space=pltpu.HBM)
    in_vmem = pl.BlockSpec(memory_space=pltpu.VMEM)
    weights = pl.pallas_call(
        load_kernel,
        out_shape=[vmem(width, width)] * 5 + [vmem(32, width, dtype=jnp.float32)],
        in_specs=[hbm] * 5 + [in_vmem],
        out_specs=[in_vmem] * 6,
        scratch_shapes=[pltpu.SemaphoreType.DMA((5,))],
        cost_estimate=pl.CostEstimate(flops=0, bytes_accessed=10**7, transcendentals=0),
        compiler_params=pltpu.CompilerParams(vmem_limit_bytes=4 * 1024 * 1024),
        name="load",
    )(
        *[
            pltpu.with_memory_space_constraint(w[0], pltpu.HBM)
            for w in (w_key, w_value, w_query, w_out, w_point)
        ],
        conv_kernel[0],
    )
    weights = [pltpu.with_memory_space_constraint(w, pltpu.VMEM) for w in weights]
    frames_kept = pltpu.with_memory_space_constraint(frames, pltpu.HBM)
    block = jax.ShapeDtypeStruct((rows, width), jnp.bfloat16)
    tails = [
        jax.ShapeDtypeStruct((take, width), jnp.bfloat16) for _, take in pieces if take < rows
    ]
    whole = jax.ShapeDtypeStruct((micro, rows, width), jnp.bfloat16)
    cost = pl.CostEstimate(flops=6 * 10**9, bytes_accessed=12 * 10**6, transcendentals=10**6)

    outputs = None
    for section in range(sections):
        outbox = []
        for chunk in range(micro):
            source = frames_kept if section == 0 else inbox[chunk][0]
            args = [info, *weights, *inbox[chunk][:0:-1], source]
            if chunk > 0 and section > 0:
                args += inbox[chunk - 1][1:]
            in_specs = [smem] + [in_vmem] * 6 + [any_space] * (len(args) - 7)
            if section == 0:
                in_specs[7 + len(pieces)] = hbm
            aliases = {}
            if outputs is not None:
                aliases = {len(args): 0}
                args.append(outputs)
                in_specs.append(hbm)
            last = section == sections - 1
            outs = [whole] if last else [whole, block, *tails]
            cfg = (rows, width, section, chunk, sections, shards, segs_row, pieces)
            made = pl.pallas_call(
                functools.partial(layer_kernel, cfg),
                out_shape=outs,
                in_specs=in_specs,
                out_specs=[hbm] + [any_space] * (len(outs) - 1),
                scratch_shapes=scratch,
                input_output_aliases=aliases,
                cost_estimate=cost,
                compiler_params=pltpu.CompilerParams(vmem_limit_bytes=VMEM_BYTES),
                name="layer",
            )(*args)
            outputs = made[0]
            if not last:
                whole_block, tails_out = made[1], iter(made[2:])
                got = {0: whole_block}
                for distance, take in pieces:
                    got[distance] = next(tails_out) if take < rows else whole_block
                far = max(got)
                if outbox and far > 0:
                    near = outbox[-1][0]
                    got[far], outbox[-1][0] = lax.optimization_barrier((got[far], near))
                sent = {d: send(got[d], d, section, section + 1) for d in got}
                outbox.append([sent[d] for d in sorted(got)])
        inbox = outbox
    return outputs[None]


def solution(mesh):
    in_specs = (
        P(None, "tm", None),
        P(),
        P("phase", None, None),
        P("phase", None, None),
        P("phase", None, None),
        P("phase", None, None),
        P("phase", None, None),
        P("phase", None, None),
    )
    out_specs = P("phase", None, "tm", None)
    return jax.shard_map(
        per_device, mesh=mesh, in_specs=in_specs, out_specs=out_specs, check_vma=False
    )
```

```python
import functools
import math

import jax
import jax.numpy as jnp
from jax import lax
from jax.experimental import pallas as pl
from jax.experimental.pallas import tpu as pltpu
from jax.sharding import PartitionSpec as P

HEADS = 16
SEG = 32
LC = 64
NMEM = 4
KW = 31

EPSILON = 1e-05
BACK = LC // SEG
HALO_SEGS = 1 + NMEM + BACK
HALO = HALO_SEGS * SEG
FAR = -1e30
OPEN = 3e38
TILE = 256
PAIR = 128
SHIFT = 5
HEAD_SHIFT = 4
VMEM_BYTES = 32 * 1024 * 1024


def layer_norms(number, load, store):
    means = [jnp.mean(load(s), axis=-1, keepdims=True) for s in range(number)]
    scales = []
    for s in range(number):
        center = load(s) - means[s]
        scales.append(lax.rsqrt(jnp.mean(center * center, axis=-1, keepdims=True) + EPSILON))
    for s in range(number):
        store(s, (load(s) - means[s]) * scales[s])


def dot(a, b):
    return jnp.dot(a, b, preferred_element_type=jnp.float32)


def dot_nt(a, b):
    return lax.dot_general(a, b, (((1,), (1,)), ((), ())), preferred_element_type=jnp.float32)


def halo_pieces(rows):
    pieces = []
    left = HALO
    while left > 0:
        take = min(rows, left)
        pieces.append((len(pieces) + 1, take))
        left -= take
    return pieces


def by_segment(index, counts, first, number):
    out = jnp.zeros(index.shape, jnp.int32)
    for s in range(number):
        out = jnp.where(index == s, counts[first + s], out)
    return out


def iota(shape, dimension):
    return lax.broadcasted_iota(jnp.int32, shape, dimension)


def layer_kernel(cfg, *refs):
    rows, width, section, chunk, sections, shards, segs_row, pieces = cfg
    refs = list(refs)
    info = refs[0]
    wk, wv, wq, wo, wp, taps = refs[1:7]
    refs = refs[7:]
    count_p = len(pieces)
    halos, own, refs = refs[:count_p][::-1], refs[count_p], refs[count_p + 1 :]
    if section == 0:
        own = own.at[chunk]
        befores = [halo.at[max(chunk - 1, 0)] for halo in halos]
        halos = [halo.at[chunk] for halo in halos]
    else:
        if chunk > 0:
            befores, refs = refs[:count_p], refs[count_p:]
        earlier, refs = refs[0], refs[1:]
    if section + chunk > 0:
        refs = refs[1:]
    outputs, refs = refs[0], refs[1:]
    last = section == sections - 1
    if not last:
        result, refs = refs[0], refs[1:]
        number = sum(1 for _, take in pieces if take < rows)
        tails, refs = refs[:number], refs[number:]
    (xe, normed, ke, ve, qe, ctx, res, cin, depth, gated, staged, bias, mem_bias, osem) = refs
    if last:
        result = staged

    ext = HALO + rows
    segs = ext // SEG
    q_rows = rows + SEG
    q_seg = HALO_SEGS - 1
    mem_first = q_seg - NMEM
    mems = segs - 1 - mem_first
    mem_pad = ke.shape[0] - ext
    key_seg = q_seg - BACK
    key_row = key_seg * SEG
    keys = ke.shape[0] - key_row
    win = ext - key_row
    head_dim = width // HEADS
    sum_rows = qe.shape[0] - q_rows
    phase, shard = info[0], info[1]

    if section > 0:
        @pl.when(phase == section - 1)
        def _():
            copy = pltpu.make_async_copy(earlier, outputs.at[chunk], osem.at[0])
            copy.start()
            copy.wait()

    @pl.when(phase == section)
    def _():
        for n, (distance, take) in enumerate(pieces):
            spot = pl.ds(HALO - (distance - 1) * rows - take, take)

            @pl.when(shard >= distance)
            def _():
                xe[spot, :] = halos[n][...]

            @pl.when(shard < distance)
            def _():
                if chunk > 0:
                    xe[spot, :] = befores[n][...]
                else:
                    xe[spot, :] = jnp.zeros((take, width), jnp.bfloat16)

        first = chunk * segs_row + shard * (rows // SEG) - HALO_SEGS
        counts = []
        for s in range(segs):
            g = first + s
            value = info[2 + jnp.maximum(g, 0)]
            counts.append(jnp.where(g >= 0, value, 0))

        row_seg = q_seg + (iota((q_rows, keys), 0) >> SHIFT)
        col = iota((q_rows, keys), 1)
        line = iota((1, keys), 1)
        kvalid = (line & (SEG - 1)) < by_segment(line >> SHIFT, counts, key_seg, win // SEG)
        mvalid = by_segment(line - win, counts, mem_first, mems) > 0
        live = (kvalid & (line < win)) | (mvalid & (line >= win))
        lows = jnp.where(line < win, key_seg + (line >> SHIFT), mem_first + 1 + line - win)
        highs = jnp.where(line < win, lows + BACK, lows + NMEM - 1)
        lows = jnp.where(live, lows, segs)
        good = (row_seg >= lows) & (row_seg <= highs)
        bias[...] = jnp.where(good, OPEN, FAR)

        mem_keys = mem_bias.shape[1]
        mseg = mem_first + (iota((mems * HEADS, mem_keys), 0) >> HEAD_SHIFT)
        mline = iota((1, mem_keys), 1)
        mlow = mline >> SHIFT
        mlive = (mline & (SEG - 1)) < by_segment(mlow, counts, 0, mem_keys // SEG)
        mhigh = mlow + BACK
        mlow = jnp.where(mlive, mlow, segs)
        mem_bias[...] = jnp.where((mseg >= mlow) & (mseg <= mhigh), OPEN, FAR)

        def load_x(s):
            if s < HALO_SEGS:
                part = xe[pl.ds(s * SEG, SEG), :]
            else:
                part = own[pl.ds((s - HALO_SEGS) * SEG, SEG), :]
            return part.astype(jnp.float32)

        def set_normed(s, value):
            normed[pl.ds(s * SEG, SEG), :] = value.astype(jnp.bfloat16)

        layer_norms(segs, load_x, set_normed)

        def columns(n):
            return pl.ds(pl.multiple_of(n * TILE, TILE), TILE)

        def tiles(unroll):
            return pl.loop(0, width // TILE, unroll=unroll)

        sseg = iota((sum_rows, ext), 0) + mem_first
        sline = iota((1, ext), 1)
        smine = sline >> SHIFT
        slive = (sline & (SEG - 1)) < by_segment(smine, counts, 0, segs)
        smine = jnp.where(slive, smine, -1)
        pick = jnp.where(sseg == smine, 1.0, 0.0).astype(jnp.bfloat16)
        scount = by_segment(iota((sum_rows, 1), 0), counts, mem_first, mems)
        divisor = jnp.maximum(scount, 1).astype(jnp.float32)
        normed[pl.ds(ext, sum_rows), :] = (dot(pick, normed[pl.ds(0, ext), :]) / divisor).astype(
            jnp.bfloat16
        )

        scale = 1.0 / math.sqrt(head_dim)

        @tiles(2)
        def _(n):
            at = columns(n)
            block = normed[pl.ds(0, ext), :]
            ke[pl.ds(0, ext), at] = dot(block, wk[:, at]).astype(jnp.bfloat16)
            ve[pl.ds(0, ext), at] = dot(block, wv[:, at]).astype(jnp.bfloat16)
            askers = normed[pl.ds(ext - q_rows, q_rows + sum_rows), :]
            qe[:, at] = (dot(askers, wq[:, at]) * scale).astype(jnp.bfloat16)

        own_head = (iota((HEADS, width), 1) // head_dim) == iota((HEADS, width), 0)
        sq = qe[pl.ds(q_rows, sum_rows), :].astype(jnp.float32)
        spread_q = []
        for m in range(mems):
            line_q = jnp.broadcast_to(sq[m : m + 1, :], (HEADS, width))
            spread_q.append(jnp.where(own_head, line_q, 0.0).astype(jnp.bfloat16))
        spread_q = jnp.concatenate(spread_q)
        ms = jnp.minimum(dot_nt(spread_q, ke[pl.ds(0, mem_keys), :]), mem_bias[...])
        me = jnp.exp(ms - jnp.max(ms, axis=-1, keepdims=True))
        mw = me * (1.0 / jnp.sum(me, axis=-1, keepdims=True))
        mo = dot(mw.astype(jnp.bfloat16), ve[pl.ds(0, mem_keys), :])
        lines = []
        for m in range(mems):
            part = jnp.where(own_head, mo[m * HEADS : (m + 1) * HEADS, :], 0.0)
            lines.append(jnp.sum(part, axis=0, keepdims=True))
        lines.append(jnp.zeros((mem_pad - mems, width), jnp.float32))
        memory = jnp.concatenate(lines).astype(jnp.bfloat16)

        @tiles(4)
        def _(n):
            at = columns(n)
            ke[pl.ds(ext, mem_pad), at] = dot(memory, wk[:, at]).astype(jnp.bfloat16)
            ve[pl.ds(ext, mem_pad), at] = dot(memory, wv[:, at]).astype(jnp.bfloat16)

        even = iota((q_rows, PAIR), 1) < head_dim

        @pl.loop(0, width // PAIR, unroll=4)
        def _(n):
            at = pl.ds(pl.multiple_of(n * PAIR, PAIR), PAIR)
            qp = qe[pl.ds(0, q_rows), at]
            zero = jnp.zeros_like(qp)
            q_both = jnp.concatenate([jnp.where(even, qp, zero), jnp.where(even, zero, qp)])
            raw = dot_nt(q_both, ke[pl.ds(key_row, keys), at])
            edge = bias[...]
            scores = jnp.minimum(raw, jnp.concatenate([edge, edge]))
            weight = jnp.exp(scores - jnp.max(scores, axis=-1, keepdims=True))
            inverse = 1.0 / jnp.sum(weight, axis=-1, keepdims=True)
            both = dot(weight.astype(jnp.bfloat16), ve[pl.ds(key_row, keys), at]) * inverse
            ctx[:, at] = jnp.where(even, both[:q_rows], both[q_rows:]).astype(jnp.bfloat16)

        @tiles(4)
        def _(n):
            at = columns(n)
            x_part = jnp.concatenate([xe[pl.ds(HALO - SEG, SEG), at], own[:, at]])
            mixed = x_part.astype(jnp.float32) + dot(ctx[...], wo[:, at])
            res[:, at] = mixed.astype(jnp.bfloat16)

        inner = iota((SEG, 1), 0)

        def set_cin(s, value):
            mask = (inner < counts[q_seg + s]).astype(jnp.float32)
            value = (value * mask).astype(jnp.bfloat16)
            cin[pl.ds(s * SEG, SEG), :] = value.astype(jnp.float32)

        layer_norms(
            q_rows // SEG, lambda s: res[pl.ds(s * SEG, SEG), :].astype(jnp.float32), set_cin
        )

        @pl.loop(0, width // PAIR)
        def _(n):
            at = pl.ds(pl.multiple_of(n * PAIR, PAIR), PAIR)
            total = jnp.zeros((rows, PAIR), jnp.float32)
            block = cin[:, at]
            start = SEG - (KW - 1)
            for residue in range(8):
                size = rows + (8 if residue else 0)
                part = None
                for o in range(start, start + KW):
                    if o % 8 == residue:
                        base = o - residue
                        term = taps[pl.ds(o - start, 1), at] * block[base : base + size]
                        part = term if part is None else part + term
                if residue:
                    part = pltpu.roll(part, size - residue, 0)[:rows]
                total = total + part
            depth[:, at] = total

        def set_gated(s, value):
            value = value * (1.0 / (1.0 + jnp.exp(-value)))
            gated[pl.ds(s * SEG, SEG), :] = value.astype(jnp.bfloat16)

        layer_norms(rows // SEG, lambda s: depth[pl.ds(s * SEG, SEG), :], set_gated)

        frame = iota((rows, 1), 0)
        frame_count = by_segment(frame >> SHIFT, counts, HALO_SEGS, rows // SEG)
        row_mask = ((frame & (SEG - 1)) < frame_count).astype(jnp.float32)

        @tiles(4)
        def _(n):
            at = columns(n)
            mixed = res[pl.ds(SEG, rows), at].astype(jnp.float32) + dot(gated[...], wp[:, at])
            made = (mixed * row_mask).astype(jnp.bfloat16)
            result[:, at] = made
            if last:
                pltpu.make_async_copy(
                    result.at[:, at], outputs.at[chunk, :, at], osem.at[n]
                ).start()
            else:
                for tail in tails:
                    tail[:, at] = made[rows - tail.shape[0] :]

        if last:
            for n in range(width // TILE):
                at = pl.ds(n * TILE, TILE)
                pltpu.make_async_copy(
                    result.at[:, at], outputs.at[chunk, :, at], osem.at[n]
                ).wait()


def load_kernel(*refs):
    sources, kernel, targets, taps, sem = refs[:6], refs[6], refs[7:13], refs[13], refs[14]
    copies = [
        pltpu.make_async_copy(source, target, sem.at[n])
        for n, (source, target) in enumerate(zip(sources, targets))
    ]
    for copy in copies:
        copy.start()
    taps[pl.ds(0, KW), :] = kernel[...].astype(jnp.float32)
    for copy in copies:
        copy.wait()


def per_device(frames, frame_counts, w_query, w_key, w_value, w_out, conv_kernel, w_point):
    micro, rows, width = frames.shape
    sections = lax.axis_size("phase")
    shards = lax.axis_size("tm")
    segs_row = frame_counts.shape[1]
    pieces = halo_pieces(rows)
    ext = HALO + rows
    q_rows = rows + SEG
    mems = ext // SEG - 1 - (HALO_SEGS - 1 - NMEM)
    mem_pad = -(-mems // SEG) * SEG
    sum_rows = -(-mems // 16) * 16
    mem_keys = (mems + BACK) * SEG
    keys = ext + mem_pad - (HALO_SEGS - 1 - BACK) * SEG

    def send(block, distance, source, target):
        route = [
            (s * sections + source, (s + distance) % shards * sections + target)
            for s in range(shards)
        ]
        return lax.ppermute(block, ("tm", "phase"), route)

    frame_halos = [
        send(frames[:, rows - take :, :], distance, distance % sections, 0)
        for distance, take in pieces
    ]
    inbox = [[None, *frame_halos] for _ in range(micro)]

    where = jnp.stack([lax.axis_index("phase"), lax.axis_index("tm")]).astype(jnp.int32)
    info = jnp.concatenate([where, frame_counts.reshape(-1)])

    def vmem(*shape, dtype=jnp.bfloat16):
        return pltpu.VMEM(shape, dtype)

    scratch = [
        vmem(HALO, width), vmem(ext + sum_rows, width),
        vmem(ext + mem_pad, width), vmem(ext + mem_pad, width),
        vmem(q_rows + sum_rows, width), vmem(q_rows, width), vmem(q_rows, width),
        vmem(q_rows, width, dtype=jnp.float32), vmem(rows, width, dtype=jnp.float32),
        vmem(rows, width), vmem(rows, width),
        vmem(q_rows, keys, dtype=jnp.float32), vmem(mems * HEADS, mem_keys, dtype=jnp.float32),
        pltpu.SemaphoreType.DMA((width // TILE,)),
    ]
    smem = pl.BlockSpec(memory_space=pltpu.SMEM)
    hbm = pl.BlockSpec(memory_space=pltpu.HBM)
    in_vmem = pl.BlockSpec(memory_space=pltpu.VMEM)
    def kept(array, space):
        return pltpu.with_memory_space_constraint(array, space)

    *weights, frames_near, taps = pl.pallas_call(
        load_kernel,
        out_shape=[vmem(width, width)] * 5
        + [vmem(micro, rows, width), vmem(32, width, dtype=jnp.float32)],
        in_specs=[hbm] * 6 + [in_vmem],
        out_specs=[in_vmem] * 7,
        scratch_shapes=[pltpu.SemaphoreType.DMA((6,))],
        cost_estimate=pl.CostEstimate(flops=0, bytes_accessed=10**7, transcendentals=0),
        compiler_params=pltpu.CompilerParams(vmem_limit_bytes=4 * 1024 * 1024),
        name="load",
    )(
        *[kept(w[0], pltpu.HBM) for w in (w_key, w_value, w_query, w_out, w_point)],
        kept(frames, pltpu.HBM),
        conv_kernel[0],
    )
    weights = [kept(w, pltpu.VMEM) for w in (*weights, taps)]
    frames_near = kept(frames_near, pltpu.VMEM)
    block = vmem(rows, width)
    tails = [vmem(take, width) for _, take in pieces if take < rows]
    whole = pltpu.HBM((micro, rows, width), jnp.bfloat16)
    cost = pl.CostEstimate(flops=6 * 10**9, bytes_accessed=12 * 10**6, transcendentals=10**6)

    outputs = None
    results = {}
    for section in range(sections):
        outbox = []
        for chunk in range(micro):
            own = inbox[chunk][0] if section > 0 else frames_near
            near = [*inbox[chunk][:0:-1], own]
            if section > 0:
                if chunk > 0:
                    near += inbox[chunk - 1][1:]
                near.append(results[section - 1, chunk])
            args = [info, *weights, *[kept(array, pltpu.VMEM) for array in near]]
            in_specs = [smem] + [in_vmem] * (len(args) - 1)
            aliases = {}
            if outputs is not None:
                aliases = {len(args): 0}
                args.append(kept(outputs, pltpu.HBM))
                in_specs.append(hbm)
            last = section == sections - 1
            outs = [whole] if last else [whole, block, *tails]
            cfg = (rows, width, section, chunk, sections, shards, segs_row, pieces)
            made = pl.pallas_call(
                functools.partial(layer_kernel, cfg),
                out_shape=outs,
                in_specs=in_specs,
                out_specs=[hbm] + [in_vmem] * (len(outs) - 1),
                scratch_shapes=scratch,
                input_output_aliases=aliases,
                cost_estimate=cost,
                compiler_params=pltpu.CompilerParams(vmem_limit_bytes=VMEM_BYTES),
                name="layer",
            )(*args)
            outputs = made[0]
            if not last:
                results[section, chunk] = made[1]
                whole_block, tails_out = made[1], iter(made[2:])
                got = {0: whole_block}
                for distance, take in pieces:
                    got[distance] = next(tails_out) if take < rows else whole_block
                far = max(got)
                if outbox and far > 0:
                    near = outbox[-1][0]
                    got[far], outbox[-1][0] = lax.optimization_barrier((got[far], near))
                sent = {d: send(got[d], d, section, section + 1) for d in got}
                outbox.append([sent[d] for d in sorted(got)])
        inbox = outbox
    return outputs[None]


def solution(mesh):
    in_specs = (
        P(None, "tm", None),
        P(),
        P("phase", None, None),
        P("phase", None, None),
        P("phase", None, None),
        P("phase", None, None),
        P("phase", None, None),
        P("phase", None, None),
    )
    out_specs = P("phase", None, "tm", None)
    return jax.shard_map(
        per_device, mesh=mesh, in_specs=in_specs, out_specs=out_specs, check_vma=False
    )
```

```python
import functools
import math

import jax
import jax.numpy as jnp
from jax import lax
from jax.experimental import pallas as pl
from jax.experimental.pallas import tpu as pltpu
from jax.sharding import PartitionSpec as P

HEADS = 16
SEG = 32
LC = 64
NMEM = 4
KW = 31

EPSILON = 1e-05
BACK = LC // SEG
HALO_SEGS = 1 + NMEM + BACK
HALO = HALO_SEGS * SEG
FAR = -1e30
OPEN = 3e38
TILE = 256
PAIR = 128
PAD = 16
SHIFT = 5
HEAD_SHIFT = 4
VMEM_BYTES = 32 * 1024 * 1024


def layer_norms(number, load, store):
    means = [jnp.mean(load(s), axis=-1, keepdims=True) for s in range(number)]
    scales = []
    for s in range(number):
        center = load(s) - means[s]
        scales.append(lax.rsqrt(jnp.mean(center * center, axis=-1, keepdims=True) + EPSILON))
    for s in range(number):
        store(s, (load(s) - means[s]) * scales[s])


def dot(a, b):
    return jnp.dot(a, b, preferred_element_type=jnp.float32)


def dot_nt(a, b):
    return lax.dot_general(a, b, (((1,), (1,)), ((), ())), preferred_element_type=jnp.float32)


def halo_pieces(rows):
    pieces = []
    left = HALO
    while left > 0:
        take = min(rows, left)
        pieces.append((len(pieces) + 1, take))
        left -= take
    return pieces


def by_segment(index, counts, first, number):
    out = jnp.zeros(index.shape, jnp.int32)
    for s in range(number):
        out = jnp.where(index == s, counts[first + s], out)
    return out


def iota(shape, dimension):
    return lax.broadcasted_iota(jnp.int32, shape, dimension)


def layer_kernel(cfg, *refs):
    rows, width, section, chunk, sections, shards, segs_row, pieces = cfg
    refs = list(refs)
    info = refs[0]
    wk, wv, wq, wo, wp, taps = refs[1:7]
    bias, mem_bias, pick, divisor, frame_mask = [ref.at[chunk] for ref in refs[7:12]]
    refs = refs[12:]
    count_p = len(pieces)
    own, halos, refs = refs[0], refs[1 : 1 + count_p], refs[1 + count_p :]
    if section == 0:
        own = own.at[chunk]
        befores = [halo.at[max(chunk - 1, 0)] for halo in halos]
        halos = [halo.at[chunk] for halo in halos]
    else:
        if chunk > 0:
            befores, refs = refs[:count_p], refs[count_p:]
        earlier, refs = refs[0], refs[1:]
    if section + chunk > 0:
        refs = refs[1:]
    outputs, refs = refs[0], refs[1:]
    last = section == sections - 1
    if not last:
        result, refs = refs[0], refs[1:]
        if section % 2 == 0:
            padded, refs = refs[0], refs[1:]
        number = sum(1 for _, take in pieces if take < rows)
        tails, refs = refs[:number], refs[number:]
    (xe, normed, ke, ve, qe, ctx, res, cin, depth, gated, staged, osem) = refs
    if last:
        result = staged

    ext = HALO + rows
    segs = ext // SEG
    q_rows = rows + SEG
    q_seg = HALO_SEGS - 1
    mems = segs - 1 - (q_seg - NMEM)
    mem_pad = ke.shape[0] - ext
    key_row = (q_seg - BACK) * SEG
    keys = ke.shape[0] - key_row
    mem_keys = mem_bias.shape[1]
    head_dim = width // HEADS
    sum_rows = qe.shape[0] - q_rows
    phase, shard = info[0], info[1]

    if section > 0:
        @pl.when(phase == section - 1)
        def _():
            copy = pltpu.make_async_copy(earlier, outputs.at[chunk], osem.at[0])
            copy.start()
            copy.wait()

    @pl.when(phase == section)
    def _():
        for n, (distance, take) in enumerate(pieces):
            spot = pl.ds(HALO - (distance - 1) * rows - take, take)

            @pl.when(shard >= distance)
            def _():
                xe[spot, :] = halos[n][...]

            @pl.when(shard < distance)
            def _():
                if chunk > 0:
                    xe[spot, :] = befores[n][...]
                else:
                    xe[spot, :] = jnp.zeros((take, width), jnp.bfloat16)

        def load_x(s):
            if s < HALO_SEGS:
                part = xe[pl.ds(s * SEG, SEG), :]
            else:
                part = own[pl.ds((s - HALO_SEGS) * SEG, SEG), :]
            return part.astype(jnp.float32)

        def set_normed(s, value):
            normed[pl.ds(s * SEG, SEG), :] = value.astype(jnp.bfloat16)

        layer_norms(segs, load_x, set_normed)

        def columns(n):
            return pl.ds(pl.multiple_of(n * TILE, TILE), TILE)

        def tiles(unroll):
            return pl.loop(0, width // TILE, unroll=unroll)

        sums = dot(pick[...], normed[pl.ds(0, ext), :])
        normed[pl.ds(ext, sum_rows), :] = (sums / divisor[...]).astype(jnp.bfloat16)

        scale = 1.0 / math.sqrt(head_dim)

        @tiles(2)
        def _(n):
            at = columns(n)
            block = normed[pl.ds(0, ext), :]
            ke[pl.ds(0, ext), at] = dot(block, wk[:, at]).astype(jnp.bfloat16)
            ve[pl.ds(0, ext), at] = dot(block, wv[:, at]).astype(jnp.bfloat16)
            askers = normed[pl.ds(ext - q_rows, q_rows + sum_rows), :]
            qe[:, at] = (dot(askers, wq[:, at]) * scale).astype(jnp.bfloat16)

        own_head = (iota((HEADS, width), 1) // head_dim) == iota((HEADS, width), 0)
        sq = qe[pl.ds(q_rows, sum_rows), :].astype(jnp.float32)
        spread_q = []
        for m in range(mems):
            line_q = jnp.broadcast_to(sq[m : m + 1, :], (HEADS, width))
            spread_q.append(jnp.where(own_head, line_q, 0.0).astype(jnp.bfloat16))
        spread_q = jnp.concatenate(spread_q)
        ms = jnp.minimum(dot_nt(spread_q, ke[pl.ds(0, mem_keys), :]), mem_bias[...])
        me = jnp.exp(ms - jnp.max(ms, axis=-1, keepdims=True))
        mw = me * (1.0 / jnp.sum(me, axis=-1, keepdims=True))
        mo = dot(mw.astype(jnp.bfloat16), ve[pl.ds(0, mem_keys), :])
        lines = []
        for m in range(mems):
            part = jnp.where(own_head, mo[m * HEADS : (m + 1) * HEADS, :], 0.0)
            lines.append(jnp.sum(part, axis=0, keepdims=True))
        lines.append(jnp.zeros((mem_pad - mems, width), jnp.float32))
        memory = jnp.concatenate(lines).astype(jnp.bfloat16)

        @tiles(4)
        def _(n):
            at = columns(n)
            ke[pl.ds(ext, mem_pad), at] = dot(memory, wk[:, at]).astype(jnp.bfloat16)
            ve[pl.ds(ext, mem_pad), at] = dot(memory, wv[:, at]).astype(jnp.bfloat16)

        even = iota((q_rows, PAIR), 1) < head_dim

        @pl.loop(0, width // PAIR, unroll=4)
        def _(n):
            at = pl.ds(pl.multiple_of(n * PAIR, PAIR), PAIR)
            qp = qe[pl.ds(0, q_rows), at]
            zero = jnp.zeros_like(qp)
            q_both = jnp.concatenate([jnp.where(even, qp, zero), jnp.where(even, zero, qp)])
            raw = dot_nt(q_both, ke[pl.ds(key_row, keys), at])
            edge = bias[...]
            scores = jnp.minimum(raw, jnp.concatenate([edge, edge]))
            weight = jnp.exp(scores - jnp.max(scores, axis=-1, keepdims=True))
            inverse = 1.0 / jnp.sum(weight, axis=-1, keepdims=True)
            both = dot(weight.astype(jnp.bfloat16), ve[pl.ds(key_row, keys), at]) * inverse
            ctx[:, at] = jnp.where(even, both[:q_rows], both[q_rows:]).astype(jnp.bfloat16)

        @tiles(4)
        def _(n):
            at = columns(n)
            x_part = jnp.concatenate([xe[pl.ds(HALO - SEG, SEG), at], own[pl.ds(0, rows), at]])
            mixed = x_part.astype(jnp.float32) + dot(ctx[...], wo[:, at])
            res[:, at] = mixed.astype(jnp.bfloat16)

        def set_cin(s, value):
            mask = frame_mask[pl.ds(s * SEG, SEG), :]
            value = (value * mask).astype(jnp.bfloat16)
            cin[pl.ds(s * SEG, SEG), :] = value.astype(jnp.float32)

        layer_norms(
            q_rows // SEG, lambda s: res[pl.ds(s * SEG, SEG), :].astype(jnp.float32), set_cin
        )

        @pl.loop(0, width // PAIR)
        def _(n):
            at = pl.ds(pl.multiple_of(n * PAIR, PAIR), PAIR)
            total = jnp.zeros((rows, PAIR), jnp.float32)
            block = cin[:, at]
            start = SEG - (KW - 1)
            for residue in range(8):
                size = rows + (8 if residue else 0)
                part = None
                for o in range(start, start + KW):
                    if o % 8 == residue:
                        base = o - residue
                        term = taps[pl.ds(o - start, 1), at] * block[base : base + size]
                        part = term if part is None else part + term
                if residue:
                    part = pltpu.roll(part, size - residue, 0)[:rows]
                total = total + part
            depth[:, at] = total

        def set_gated(s, value):
            value = value * (1.0 / (1.0 + jnp.exp(-value)))
            gated[pl.ds(s * SEG, SEG), :] = value.astype(jnp.bfloat16)

        layer_norms(rows // SEG, lambda s: depth[pl.ds(s * SEG, SEG), :], set_gated)

        row_mask = frame_mask[pl.ds(SEG, rows), :]

        @tiles(4)
        def _(n):
            at = columns(n)
            mixed = res[pl.ds(SEG, rows), at].astype(jnp.float32) + dot(gated[...], wp[:, at])
            made = (mixed * row_mask).astype(jnp.bfloat16)
            result[:, at] = made
            if last:
                pltpu.make_async_copy(
                    result.at[:, at], outputs.at[chunk, :, at], osem.at[n]
                ).start()
            else:
                if section % 2 == 0:
                    padded[pl.ds(0, rows), at] = made
                    padded[pl.ds(rows, PAD), at] = jnp.zeros((PAD, TILE), jnp.bfloat16)
                for tail in tails:
                    tail[:, at] = made[rows - tail.shape[0] :]

        if last:
            for n in range(width // TILE):
                at = pl.ds(n * TILE, TILE)
                pltpu.make_async_copy(
                    result.at[:, at], outputs.at[chunk, :, at], osem.at[n]
                ).wait()


def load_kernel(cfg, info, *refs):
    rows, segs_row, micro = cfg
    sources, kernel, targets, taps, masks, sem = (
        refs[:6], refs[6], refs[7:13], refs[13], refs[14:19], refs[19],
    )
    copies = [
        pltpu.make_async_copy(source, target, sem.at[n])
        for n, (source, target) in enumerate(zip(sources, targets))
    ]
    for copy in copies:
        copy.start()
    taps[pl.ds(0, KW), :] = kernel[...].astype(jnp.float32)
    bias, mem_bias, pick, divisor, frame_mask = masks
    q_rows, keys = bias.shape[1:]
    mem_keys = mem_bias.shape[2]
    sum_rows, ext = pick.shape[1:]
    segs = ext // SEG
    q_seg = HALO_SEGS - 1
    mem_first = q_seg - NMEM
    mems = segs - 1 - mem_first
    key_seg = q_seg - BACK
    win = ext - key_seg * SEG
    for chunk in range(micro):
        first = chunk * segs_row + info[1] * (rows // SEG) - HALO_SEGS
        counts = []
        for s in range(segs):
            value = info[2 + jnp.maximum(first + s, 0)]
            counts.append(jnp.where(first + s >= 0, value, 0))

        row_seg = q_seg + (iota((q_rows, keys), 0) >> SHIFT)
        line = iota((1, keys), 1)
        kvalid = (line & (SEG - 1)) < by_segment(line >> SHIFT, counts, key_seg, win // SEG)
        mvalid = by_segment(line - win, counts, mem_first, mems) > 0
        live = (kvalid & (line < win)) | (mvalid & (line >= win))
        lows = jnp.where(line < win, key_seg + (line >> SHIFT), mem_first + 1 + line - win)
        highs = jnp.where(line < win, lows + BACK, lows + NMEM - 1)
        lows = jnp.where(live, lows, segs)
        good = (row_seg >= lows) & (row_seg <= highs)
        bias[chunk] = jnp.where(good, OPEN, FAR)

        mseg = mem_first + (iota((mems * HEADS, mem_keys), 0) >> HEAD_SHIFT)
        mline = iota((1, mem_keys), 1)
        mlow = mline >> SHIFT
        mlive = (mline & (SEG - 1)) < by_segment(mlow, counts, 0, mem_keys // SEG)
        mhigh = mlow + BACK
        mlow = jnp.where(mlive, mlow, segs)
        mem_bias[chunk] = jnp.where((mseg >= mlow) & (mseg <= mhigh), OPEN, FAR)

        sseg = iota((sum_rows, ext), 0) + mem_first
        sline = iota((1, ext), 1)
        smine = sline >> SHIFT
        slive = (sline & (SEG - 1)) < by_segment(smine, counts, 0, segs)
        smine = jnp.where(slive, smine, -1)
        pick[chunk] = jnp.where(sseg == smine, 1.0, 0.0).astype(jnp.bfloat16)
        scount = by_segment(iota((sum_rows, 1), 0), counts, mem_first, mems)
        divisor[chunk] = jnp.maximum(scount, 1).astype(jnp.float32)

        frame = iota((q_rows, 1), 0)
        frame_count = by_segment(frame >> SHIFT, counts, q_seg, q_rows // SEG)
        frame_mask[chunk] = ((frame & (SEG - 1)) < frame_count).astype(jnp.float32)
    for copy in copies:
        copy.wait()


def per_device(frames, frame_counts, w_query, w_key, w_value, w_out, conv_kernel, w_point):
    micro, rows, width = frames.shape
    sections = lax.axis_size("phase")
    shards = lax.axis_size("tm")
    segs_row = frame_counts.shape[1]
    pieces = halo_pieces(rows)
    ext = HALO + rows
    q_rows = rows + SEG
    mems = ext // SEG - 1 - (HALO_SEGS - 1 - NMEM)
    mem_pad = -(-mems // SEG) * SEG
    sum_rows = -(-mems // 16) * 16
    mem_keys = (mems + BACK) * SEG
    keys = ext + mem_pad - (HALO_SEGS - 1 - BACK) * SEG

    def send(block, distance, source, target):
        route = [
            (s * sections + source, (s + distance) % shards * sections + target)
            for s in range(shards)
        ]
        return lax.ppermute(block, ("tm", "phase"), route)

    frame_halos = [
        send(frames[:, rows - take :, :], distance, distance % sections, 0)
        for distance, take in pieces
    ]
    inbox = [[None, *frame_halos] for _ in range(micro)]

    where = jnp.stack([lax.axis_index("phase"), lax.axis_index("tm")]).astype(jnp.int32)
    info = jnp.concatenate([where, frame_counts.reshape(-1)])

    def vmem(*shape, dtype=jnp.bfloat16):
        return pltpu.VMEM(shape, dtype)

    scratch = [
        vmem(HALO, width), vmem(ext + sum_rows, width),
        vmem(ext + mem_pad, width), vmem(ext + mem_pad, width),
        vmem(q_rows + sum_rows, width), vmem(q_rows, width), vmem(q_rows, width),
        vmem(q_rows, width, dtype=jnp.float32), vmem(rows, width, dtype=jnp.float32),
        vmem(rows, width), vmem(rows, width),
        pltpu.SemaphoreType.DMA((width // TILE,)),
    ]
    smem = pl.BlockSpec(memory_space=pltpu.SMEM)
    hbm = pl.BlockSpec(memory_space=pltpu.HBM)
    in_vmem = pl.BlockSpec(memory_space=pltpu.VMEM)
    def kept(array, space):
        return pltpu.with_memory_space_constraint(array, space)

    near_by = pl.pallas_call(
        functools.partial(load_kernel, (rows, segs_row, micro)),
        out_shape=[vmem(width, width)] * 5
        + [
            vmem(micro, rows, width),
            vmem(32, width, dtype=jnp.float32),
            vmem(micro, q_rows, keys, dtype=jnp.float32),
            vmem(micro, mems * HEADS, mem_keys, dtype=jnp.float32),
            vmem(micro, sum_rows, ext),
            vmem(micro, sum_rows, 1, dtype=jnp.float32),
            vmem(micro, q_rows, 1, dtype=jnp.float32),
        ],
        in_specs=[smem] + [hbm] * 6 + [in_vmem],
        out_specs=[in_vmem] * 12,
        scratch_shapes=[pltpu.SemaphoreType.DMA((6,))],
        cost_estimate=pl.CostEstimate(flops=0, bytes_accessed=10**7, transcendentals=0),
        compiler_params=pltpu.CompilerParams(vmem_limit_bytes=4 * 1024 * 1024),
        name="load",
    )(
        info,
        *[kept(w[0], pltpu.HBM) for w in (w_key, w_value, w_query, w_out, w_point)],
        kept(frames, pltpu.HBM),
        conv_kernel[0],
    )
    near_by = [kept(w, pltpu.VMEM) for w in near_by]
    frames_near = near_by.pop(5)
    block = vmem(rows, width)
    tails = [vmem(take, width) for _, take in pieces if take < rows]
    whole = pltpu.HBM((micro, rows, width), jnp.bfloat16)
    cost = pl.CostEstimate(flops=6 * 10**9, bytes_accessed=12 * 10**6, transcendentals=10**6)

    outputs = None
    results = {}
    for section in range(sections):
        outbox = []
        for chunk in range(micro):
            own = inbox[chunk][0] if section > 0 else frames_near
            near = [own, *inbox[chunk][1:]]
            if section > 0:
                if chunk > 0:
                    near += inbox[chunk - 1][1:]
                near.append(results[section - 1, chunk])
            args = [info, *near_by, *[kept(array, pltpu.VMEM) for array in near]]
            in_specs = [smem] + [in_vmem] * (len(args) - 1)
            aliases = {}
            if outputs is not None:
                aliases = {len(args): 0}
                args.append(kept(outputs, pltpu.HBM))
                in_specs.append(hbm)
            last = section == sections - 1
            padded = [vmem(rows + PAD, width)] if section % 2 == 0 else []
            outs = [whole] if last else [whole, block, *padded, *tails]
            cfg = (rows, width, section, chunk, sections, shards, segs_row, pieces)
            made = pl.pallas_call(
                functools.partial(layer_kernel, cfg),
                out_shape=outs,
                in_specs=in_specs,
                out_specs=[hbm] + [in_vmem] * (len(outs) - 1),
                scratch_shapes=scratch,
                input_output_aliases=aliases,
                cost_estimate=cost,
                compiler_params=pltpu.CompilerParams(vmem_limit_bytes=VMEM_BYTES),
                name="layer",
            )(*args)
            outputs = made[0]
            if not last:
                results[section, chunk] = made[1]
                whole_block, tails_out = made[1], iter(made[2:])
                got = {0: next(tails_out) if section % 2 == 0 else whole_block}
                for distance, take in pieces:
                    got[distance] = next(tails_out) if take < rows else whole_block
                far = max(got)
                if outbox and far > 0:
                    near = outbox[-1][0]
                    got[far], outbox[-1][0] = lax.optimization_barrier((got[far], near))
                sent = {d: send(got[d], d, section, section + 1) for d in got}
                outbox.append([sent[d] for d in sorted(got)])
        inbox = outbox
    return outputs[None]


def solution(mesh):
    in_specs = (
        P(None, "tm", None),
        P(),
        P("phase", None, None),
        P("phase", None, None),
        P("phase", None, None),
        P("phase", None, None),
        P("phase", None, None),
        P("phase", None, None),
    )
    out_specs = P("phase", None, "tm", None)
    return jax.shard_map(
        per_device, mesh=mesh, in_specs=in_specs, out_specs=out_specs, check_vma=False
    )
```

```python
import functools
import math

import jax
import jax.numpy as jnp
from jax import lax
from jax.experimental import pallas as pl
from jax.experimental.pallas import tpu as pltpu
from jax.sharding import PartitionSpec as P

HEADS = 16
SEG = 32
LC = 64
NMEM = 4
KW = 31

EPSILON = 1e-05
BACK = LC // SEG
HALO_SEGS = 1 + NMEM + BACK
HALO = HALO_SEGS * SEG
FAR = -1e30
OPEN = 3e38
TILE = 256
PAIR = 128
PAD = 16
SHIFT = 5
HEAD_SHIFT = 4
VMEM_BYTES = 32 * 1024 * 1024


def layer_norms(number, load, store):
    means = [jnp.mean(load(s), axis=-1, keepdims=True) for s in range(number)]
    scales = []
    for s in range(number):
        center = load(s) - means[s]
        scales.append(lax.rsqrt(jnp.mean(center * center, axis=-1, keepdims=True) + EPSILON))
    for s in range(number):
        store(s, (load(s) - means[s]) * scales[s])


def dot(a, b):
    return jnp.dot(a, b, preferred_element_type=jnp.float32)


def dot_nt(a, b):
    return lax.dot_general(a, b, (((1,), (1,)), ((), ())), preferred_element_type=jnp.float32)


def halo_pieces(rows):
    pieces = []
    left = HALO
    while left > 0:
        take = min(rows, left)
        pieces.append((len(pieces) + 1, take))
        left -= take
    return pieces


def by_segment(index, counts, first, number):
    out = jnp.zeros(index.shape, jnp.int32)
    for s in range(number):
        out = jnp.where(index == s, counts[first + s], out)
    return out


def iota(shape, dimension):
    return lax.broadcasted_iota(jnp.int32, shape, dimension)


def layer_kernel(cfg, *refs):
    rows, width, section, chunk, sections, shards, segs_row, pieces = cfg
    refs = list(refs)
    info = refs[0]
    wk, wv, wq, wo, wp, taps = refs[1:7]
    bias, mem_bias, pick, divisor, frame_mask = [ref.at[chunk] for ref in refs[7:12]]
    refs = refs[12:]
    count_p = len(pieces)
    own, halos, refs = refs[0], refs[1 : 1 + count_p], refs[1 + count_p :]
    if section == 0:
        own = own.at[chunk]
        befores = [halo.at[max(chunk - 1, 0)] for halo in halos]
        halos = [halo.at[chunk] for halo in halos]
    else:
        if chunk > 0:
            befores, refs = refs[:count_p], refs[count_p:]
        earlier, refs = refs[0], refs[1:]
    if section + chunk > 0:
        refs = refs[1:]
    outputs, refs = refs[0], refs[1:]
    last = section == sections - 1
    if not last:
        result, refs = refs[0], refs[1:]
        if section % 2 == 0:
            padded, refs = refs[0], refs[1:]
        number = sum(1 for _, take in pieces if take < rows)
        tails, refs = refs[:number], refs[number:]
    (xe, normed, ke, ve, qe, ctx, res, cin, depth, gated, staged, osem) = refs
    if last:
        result = staged

    ext = HALO + rows
    segs = ext // SEG
    q_rows = rows + SEG
    q_seg = HALO_SEGS - 1
    mems = segs - 1 - (q_seg - NMEM)
    mem_pad = ke.shape[0] - ext
    key_row = (q_seg - BACK) * SEG
    keys = ke.shape[0] - key_row
    mem_keys = mem_bias.shape[1]
    head_dim = width // HEADS
    sum_rows = qe.shape[0] - q_rows
    phase, shard = info[0], info[1]

    if section > 0:
        @pl.when(phase == section - 1)
        def _():
            copy = pltpu.make_async_copy(earlier, outputs.at[chunk], osem.at[0])
            copy.start()
            copy.wait()

    @pl.when(phase == section)
    def _():
        for n, (distance, take) in enumerate(pieces):
            spot = pl.ds(HALO - (distance - 1) * rows - take, take)

            @pl.when(shard >= distance)
            def _():
                xe[spot, :] = halos[n][...]

            @pl.when(shard < distance)
            def _():
                if chunk > 0:
                    xe[spot, :] = befores[n][...]
                else:
                    xe[spot, :] = jnp.zeros((take, width), jnp.bfloat16)

        def load_x(s):
            if s < HALO_SEGS:
                part = xe[pl.ds(s * SEG, SEG), :]
            else:
                part = own[pl.ds((s - HALO_SEGS) * SEG, SEG), :]
            return part.astype(jnp.float32)

        def set_normed(s, value):
            normed[pl.ds(s * SEG, SEG), :] = value.astype(jnp.bfloat16)

        layer_norms(segs, load_x, set_normed)

        def columns(n):
            return pl.ds(pl.multiple_of(n * TILE, TILE), TILE)

        def tiles(unroll):
            return pl.loop(0, width // TILE, unroll=unroll)

        sums = dot(pick[...], normed[pl.ds(0, ext), :])
        normed[pl.ds(ext, sum_rows), :] = (sums / divisor[...]).astype(jnp.bfloat16)

        scale = 1.0 / math.sqrt(head_dim)

        @tiles(4)
        def _(n):
            at = columns(n)
            block = normed[pl.ds(0, ext), :]
            ke[pl.ds(0, ext), at] = dot(block, wk[:, at]).astype(jnp.bfloat16)
            ve[pl.ds(0, ext), at] = dot(block, wv[:, at]).astype(jnp.bfloat16)
            askers = normed[pl.ds(ext - q_rows, q_rows + sum_rows), :]
            qe[:, at] = (dot(askers, wq[:, at]) * scale).astype(jnp.bfloat16)

        own_head = (iota((HEADS, width), 1) // head_dim) == iota((HEADS, width), 0)
        sq = qe[pl.ds(q_rows, sum_rows), :].astype(jnp.float32)
        spread_q = []
        for m in range(mems):
            line_q = jnp.broadcast_to(sq[m : m + 1, :], (HEADS, width))
            spread_q.append(jnp.where(own_head, line_q, 0.0).astype(jnp.bfloat16))
        spread_q = jnp.concatenate(spread_q)
        ms = jnp.minimum(dot_nt(spread_q, ke[pl.ds(0, mem_keys), :]), mem_bias[...])
        me = jnp.exp(ms - jnp.max(ms, axis=-1, keepdims=True))
        mw = me * (1.0 / jnp.sum(me, axis=-1, keepdims=True))
        mo = dot(mw.astype(jnp.bfloat16), ve[pl.ds(0, mem_keys), :])
        lines = []
        for m in range(mems):
            part = jnp.where(own_head, mo[m * HEADS : (m + 1) * HEADS, :], 0.0)
            lines.append(jnp.sum(part, axis=0, keepdims=True))
        lines.append(jnp.zeros((mem_pad - mems, width), jnp.float32))
        memory = jnp.concatenate(lines).astype(jnp.bfloat16)

        @tiles(4)
        def _(n):
            at = columns(n)
            ke[pl.ds(ext, mem_pad), at] = dot(memory, wk[:, at]).astype(jnp.bfloat16)
            ve[pl.ds(ext, mem_pad), at] = dot(memory, wv[:, at]).astype(jnp.bfloat16)

        even = iota((q_rows, PAIR), 1) < head_dim

        @pl.loop(0, width // PAIR, unroll=8)
        def _(n):
            at = pl.ds(pl.multiple_of(n * PAIR, PAIR), PAIR)
            qp = qe[pl.ds(0, q_rows), at]
            zero = jnp.zeros_like(qp)
            q_both = jnp.concatenate([jnp.where(even, qp, zero), jnp.where(even, zero, qp)])
            raw = dot_nt(q_both, ke[pl.ds(key_row, keys), at])
            edge = bias[...]
            scores = jnp.minimum(raw, jnp.concatenate([edge, edge]))
            weight = jnp.exp(scores - jnp.max(scores, axis=-1, keepdims=True))
            inverse = 1.0 / jnp.sum(weight, axis=-1, keepdims=True)
            both = dot(weight.astype(jnp.bfloat16), ve[pl.ds(key_row, keys), at]) * inverse
            ctx[:, at] = jnp.where(even, both[:q_rows], both[q_rows:]).astype(jnp.bfloat16)

        @tiles(4)
        def _(n):
            at = columns(n)
            x_part = jnp.concatenate([xe[pl.ds(HALO - SEG, SEG), at], own[pl.ds(0, rows), at]])
            mixed = x_part.astype(jnp.float32) + dot(ctx[...], wo[:, at])
            res[:, at] = mixed.astype(jnp.bfloat16)

        def set_cin(s, value):
            mask = frame_mask[pl.ds(s * SEG, SEG), :]
            value = (value * mask).astype(jnp.bfloat16)
            cin[pl.ds(s * SEG, SEG), :] = value.astype(jnp.float32)

        layer_norms(
            q_rows // SEG, lambda s: res[pl.ds(s * SEG, SEG), :].astype(jnp.float32), set_cin
        )

        @pl.loop(0, width // PAIR, unroll=2)
        def _(n):
            at = pl.ds(pl.multiple_of(n * PAIR, PAIR), PAIR)
            total = jnp.zeros((rows, PAIR), jnp.float32)
            block = cin[:, at]
            start = SEG - (KW - 1)
            for residue in range(8):
                size = rows + (8 if residue else 0)
                part = None
                for o in range(start, start + KW):
                    if o % 8 == residue:
                        base = o - residue
                        term = taps[pl.ds(o - start, 1), at] * block[base : base + size]
                        part = term if part is None else part + term
                if residue:
                    part = pltpu.roll(part, size - residue, 0)[:rows]
                total = total + part
            depth[:, at] = total

        def set_gated(s, value):
            value = value * (1.0 / (1.0 + jnp.exp(-value)))
            gated[pl.ds(s * SEG, SEG), :] = value.astype(jnp.bfloat16)

        layer_norms(rows // SEG, lambda s: depth[pl.ds(s * SEG, SEG), :], set_gated)

        row_mask = frame_mask[pl.ds(SEG, rows), :]

        @tiles(4)
        def _(n):
            at = columns(n)
            mixed = res[pl.ds(SEG, rows), at].astype(jnp.float32) + dot(gated[...], wp[:, at])
            made = (mixed * row_mask).astype(jnp.bfloat16)
            result[:, at] = made
            if last:
                pltpu.make_async_copy(
                    result.at[:, at], outputs.at[chunk, :, at], osem.at[n]
                ).start()
            else:
                if section % 2 == 0:
                    padded[pl.ds(0, rows), at] = made
                    padded[pl.ds(rows, PAD), at] = jnp.zeros((PAD, TILE), jnp.bfloat16)
                for tail in tails:
                    tail[:, at] = made[rows - tail.shape[0] :]

        if last:
            for n in range(width // TILE):
                at = pl.ds(n * TILE, TILE)
                pltpu.make_async_copy(
                    result.at[:, at], outputs.at[chunk, :, at], osem.at[n]
                ).wait()


def load_kernel(cfg, info, *refs):
    rows, segs_row, micro = cfg
    sources, kernel, targets, taps, masks, sem = (
        refs[:6], refs[6], refs[7:13], refs[13], refs[14:19], refs[19],
    )
    copies = [
        pltpu.make_async_copy(source, target, sem.at[n])
        for n, (source, target) in enumerate(zip(sources, targets))
    ]
    for copy in copies:
        copy.start()
    taps[pl.ds(0, KW), :] = kernel[...].astype(jnp.float32)
    bias, mem_bias, pick, divisor, frame_mask = masks
    q_rows, keys = bias.shape[1:]
    mem_keys = mem_bias.shape[2]
    sum_rows, ext = pick.shape[1:]
    segs = ext // SEG
    q_seg = HALO_SEGS - 1
    mem_first = q_seg - NMEM
    mems = segs - 1 - mem_first
    key_seg = q_seg - BACK
    win = ext - key_seg * SEG
    for chunk in range(micro):
        first = chunk * segs_row + info[1] * (rows // SEG) - HALO_SEGS
        counts = []
        for s in range(segs):
            value = info[2 + jnp.maximum(first + s, 0)]
            counts.append(jnp.where(first + s >= 0, value, 0))

        row_seg = q_seg + (iota((q_rows, keys), 0) >> SHIFT)
        line = iota((1, keys), 1)
        kvalid = (line & (SEG - 1)) < by_segment(line >> SHIFT, counts, key_seg, win // SEG)
        mvalid = by_segment(line - win, counts, mem_first, mems) > 0
        live = (kvalid & (line < win)) | (mvalid & (line >= win))
        lows = jnp.where(line < win, key_seg + (line >> SHIFT), mem_first + 1 + line - win)
        highs = jnp.where(line < win, lows + BACK, lows + NMEM - 1)
        lows = jnp.where(live, lows, segs)
        good = (row_seg >= lows) & (row_seg <= highs)
        bias[chunk] = jnp.where(good, OPEN, FAR)

        mseg = mem_first + (iota((mems * HEADS, mem_keys), 0) >> HEAD_SHIFT)
        mline = iota((1, mem_keys), 1)
        mlow = mline >> SHIFT
        mlive = (mline & (SEG - 1)) < by_segment(mlow, counts, 0, mem_keys // SEG)
        mhigh = mlow + BACK
        mlow = jnp.where(mlive, mlow, segs)
        mem_bias[chunk] = jnp.where((mseg >= mlow) & (mseg <= mhigh), OPEN, FAR)

        sseg = iota((sum_rows, ext), 0) + mem_first
        sline = iota((1, ext), 1)
        smine = sline >> SHIFT
        slive = (sline & (SEG - 1)) < by_segment(smine, counts, 0, segs)
        smine = jnp.where(slive, smine, -1)
        pick[chunk] = jnp.where(sseg == smine, 1.0, 0.0).astype(jnp.bfloat16)
        scount = by_segment(iota((sum_rows, 1), 0), counts, mem_first, mems)
        divisor[chunk] = jnp.maximum(scount, 1).astype(jnp.float32)

        frame = iota((q_rows, 1), 0)
        frame_count = by_segment(frame >> SHIFT, counts, q_seg, q_rows // SEG)
        frame_mask[chunk] = ((frame & (SEG - 1)) < frame_count).astype(jnp.float32)
    for copy in copies:
        copy.wait()


def per_device(frames, frame_counts, w_query, w_key, w_value, w_out, conv_kernel, w_point):
    micro, rows, width = frames.shape
    sections = lax.axis_size("phase")
    shards = lax.axis_size("tm")
    segs_row = frame_counts.shape[1]
    pieces = halo_pieces(rows)
    ext = HALO + rows
    q_rows = rows + SEG
    mems = ext // SEG - 1 - (HALO_SEGS - 1 - NMEM)
    mem_pad = -(-mems // SEG) * SEG
    sum_rows = -(-mems // 16) * 16
    mem_keys = (mems + BACK) * SEG
    keys = ext + mem_pad - (HALO_SEGS - 1 - BACK) * SEG

    def send(block, distance, source, target):
        route = [
            (s * sections + source, (s + distance) % shards * sections + target)
            for s in range(shards)
        ]
        return lax.ppermute(block, ("tm", "phase"), route)

    frame_halos = [
        send(frames[:, rows - take :, :], distance, distance % sections, 0)
        for distance, take in pieces
    ]
    inbox = [[None, *frame_halos] for _ in range(micro)]

    where = jnp.stack([lax.axis_index("phase"), lax.axis_index("tm")]).astype(jnp.int32)
    info = jnp.concatenate([where, frame_counts.reshape(-1)])

    def vmem(*shape, dtype=jnp.bfloat16):
        return pltpu.VMEM(shape, dtype)

    scratch = [
        vmem(HALO, width), vmem(ext + sum_rows, width),
        vmem(ext + mem_pad, width), vmem(ext + mem_pad, width),
        vmem(q_rows + sum_rows, width), vmem(q_rows, width), vmem(q_rows, width),
        vmem(q_rows, width, dtype=jnp.float32), vmem(rows, width, dtype=jnp.float32),
        vmem(rows, width), vmem(rows, width),
        pltpu.SemaphoreType.DMA((width // TILE,)),
    ]
    smem = pl.BlockSpec(memory_space=pltpu.SMEM)
    hbm = pl.BlockSpec(memory_space=pltpu.HBM)
    in_vmem = pl.BlockSpec(memory_space=pltpu.VMEM)
    def kept(array, space):
        return pltpu.with_memory_space_constraint(array, space)

    near_by = pl.pallas_call(
        functools.partial(load_kernel, (rows, segs_row, micro)),
        out_shape=[vmem(width, width)] * 5
        + [
            vmem(micro, rows, width),
            vmem(32, width, dtype=jnp.float32),
            vmem(micro, q_rows, keys, dtype=jnp.float32),
            vmem(micro, mems * HEADS, mem_keys, dtype=jnp.float32),
            vmem(micro, sum_rows, ext),
            vmem(micro, sum_rows, 1, dtype=jnp.float32),
            vmem(micro, q_rows, 1, dtype=jnp.float32),
        ],
        in_specs=[smem] + [hbm] * 6 + [in_vmem],
        out_specs=[in_vmem] * 12,
        scratch_shapes=[pltpu.SemaphoreType.DMA((6,))],
        cost_estimate=pl.CostEstimate(flops=0, bytes_accessed=10**7, transcendentals=0),
        compiler_params=pltpu.CompilerParams(vmem_limit_bytes=4 * 1024 * 1024),
        name="load",
    )(
        info,
        *[kept(w[0], pltpu.HBM) for w in (w_key, w_value, w_query, w_out, w_point)],
        kept(frames, pltpu.HBM),
        conv_kernel[0],
    )
    near_by = [kept(w, pltpu.VMEM) for w in near_by]
    frames_near = near_by.pop(5)
    block = vmem(rows, width)
    tails = [vmem(take, width) for _, take in pieces if take < rows]
    whole = pltpu.HBM((micro, rows, width), jnp.bfloat16)
    cost = pl.CostEstimate(flops=6 * 10**9, bytes_accessed=12 * 10**6, transcendentals=10**6)

    outputs = None
    results = {}
    for section in range(sections):
        outbox = []
        for chunk in range(micro):
            own = inbox[chunk][0] if section > 0 else frames_near
            near = [own, *inbox[chunk][1:]]
            if section > 0:
                if chunk > 0:
                    near += inbox[chunk - 1][1:]
                near.append(results[section - 1, chunk])
            args = [info, *near_by, *[kept(array, pltpu.VMEM) for array in near]]
            in_specs = [smem] + [in_vmem] * (len(args) - 1)
            aliases = {}
            if outputs is not None:
                aliases = {len(args): 0}
                args.append(kept(outputs, pltpu.HBM))
                in_specs.append(hbm)
            last = section == sections - 1
            padded = [vmem(rows + PAD, width)] if section % 2 == 0 else []
            outs = [whole] if last else [whole, block, *padded, *tails]
            cfg = (rows, width, section, chunk, sections, shards, segs_row, pieces)
            made = pl.pallas_call(
                functools.partial(layer_kernel, cfg),
                out_shape=outs,
                in_specs=in_specs,
                out_specs=[hbm] + [in_vmem] * (len(outs) - 1),
                scratch_shapes=scratch,
                input_output_aliases=aliases,
                cost_estimate=cost,
                compiler_params=pltpu.CompilerParams(vmem_limit_bytes=VMEM_BYTES),
                name="layer",
            )(*args)
            outputs = made[0]
            if not last:
                results[section, chunk] = made[1]
                whole_block, tails_out = made[1], iter(made[2:])
                got = {0: next(tails_out) if section % 2 == 0 else whole_block}
                for distance, take in pieces:
                    got[distance] = next(tails_out) if take < rows else whole_block
                far = max(got)
                if outbox and far > 0:
                    near = outbox[-1][0]
                    got[far], outbox[-1][0] = lax.optimization_barrier((got[far], near))
                sent = {d: send(got[d], d, section, section + 1) for d in got}
                outbox.append([sent[d] for d in sorted(got)])
        inbox = outbox
    return outputs[None]


def solution(mesh):
    in_specs = (
        P(None, "tm", None),
        P(),
        P("phase", None, None),
        P("phase", None, None),
        P("phase", None, None),
        P("phase", None, None),
        P("phase", None, None),
        P("phase", None, None),
    )
    out_specs = P("phase", None, "tm", None)
    return jax.shard_map(
        per_device, mesh=mesh, in_specs=in_specs, out_specs=out_specs, check_vma=False
    )
```

```python
import functools
import math

import jax
import jax.numpy as jnp
from jax import lax
from jax.experimental import pallas as pl
from jax.experimental.pallas import tpu as pltpu
from jax.sharding import PartitionSpec as P

HEADS = 16
SEG = 32
LC = 64
NMEM = 4
KW = 31

EPSILON = 1e-05
BACK = LC // SEG
HALO_SEGS = 1 + NMEM + BACK
HALO = HALO_SEGS * SEG
FAR = -1e30
OPEN = 3e38
TILE = 256
PAIR = 128
PAD = 16
SHIFT = 5
HEAD_SHIFT = 4
VMEM_BYTES = 32 * 1024 * 1024


def layer_norms(number, load, store):
    means = [jnp.mean(load(s), axis=-1, keepdims=True) for s in range(number)]
    scales = []
    for s in range(number):
        center = load(s) - means[s]
        scales.append(lax.rsqrt(jnp.mean(center * center, axis=-1, keepdims=True) + EPSILON))
    for s in range(number):
        store(s, (load(s) - means[s]) * scales[s])


def dot(a, b):
    return jnp.dot(a, b, preferred_element_type=jnp.float32)


def dot_nt(a, b):
    return lax.dot_general(a, b, (((1,), (1,)), ((), ())), preferred_element_type=jnp.float32)


def halo_pieces(rows):
    pieces = []
    left = HALO
    while left > 0:
        take = min(rows, left)
        pieces.append((len(pieces) + 1, take))
        left -= take
    return pieces


def by_segment(index, counts, first, number):
    out = jnp.zeros(index.shape, jnp.int32)
    for s in range(number):
        out = jnp.where(index == s, counts[first + s], out)
    return out


def iota(shape, dimension):
    return lax.broadcasted_iota(jnp.int32, shape, dimension)


def layer_kernel(cfg, *refs):
    rows, width, section, chunk, sections, shards, segs_row, pieces = cfg
    refs = list(refs)
    where = refs[0]
    wk, wv, wq, wo, wp, taps = refs[1:7]
    bias, mem_bias, pick, divisor, frame_mask = [ref.at[chunk] for ref in refs[7:12]]
    refs = refs[12:]
    count_p = len(pieces)
    own, halos, refs = refs[0], refs[1 : 1 + count_p], refs[1 + count_p :]
    if section == 0:
        own = own.at[chunk]
    if chunk > 0:
        befores, refs = refs[:count_p], refs[count_p:]
    if section > 0:
        earlier, refs = refs[0], refs[1:]
    if section + chunk > 0:
        refs = refs[1:]
    outputs, refs = refs[0], refs[1:]
    last = section == sections - 1
    if not last:
        result, refs = refs[0], refs[1:]
        if section % 2 == 0:
            padded, refs = refs[0], refs[1:]
        number = sum(1 for _, take in pieces if take < rows)
        tails, refs = refs[:number], refs[number:]
    (xe, normed, ke, ve, qe, ctx, res, cin, depth, gated, staged, osem) = refs
    if last:
        result = staged

    ext = HALO + rows
    segs = ext // SEG
    q_rows = rows + SEG
    q_seg = HALO_SEGS - 1
    mems = segs - 1 - (q_seg - NMEM)
    mem_pad = ke.shape[0] - ext
    key_row = (q_seg - BACK) * SEG
    keys = ke.shape[0] - key_row
    mem_keys = mem_bias.shape[1]
    head_dim = width // HEADS
    sum_rows = qe.shape[0] - q_rows
    phase, shard = where[0], where[1]

    if section > 0:
        @pl.when(phase == section - 1)
        def _():
            copy = pltpu.make_async_copy(earlier, outputs.at[chunk], osem.at[0])
            copy.start()
            copy.wait()

    @pl.when(phase == section)
    def _():
        for n, (distance, take) in enumerate(pieces):
            spot = pl.ds(HALO - (distance - 1) * rows - take, take)

            @pl.when(shard >= distance)
            def _():
                xe[spot, :] = halos[n][...]

            @pl.when(shard < distance)
            def _():
                if chunk > 0:
                    xe[spot, :] = befores[n][...]
                else:
                    xe[spot, :] = jnp.zeros((take, width), jnp.bfloat16)

        def load_x(s):
            if s < HALO_SEGS:
                part = xe[pl.ds(s * SEG, SEG), :]
            else:
                part = own[pl.ds((s - HALO_SEGS) * SEG, SEG), :]
            return part.astype(jnp.float32)

        def set_normed(s, value):
            normed[pl.ds(s * SEG, SEG), :] = value.astype(jnp.bfloat16)

        layer_norms(segs, load_x, set_normed)

        def columns(n):
            return pl.ds(pl.multiple_of(n * TILE, TILE), TILE)

        def tiles(unroll):
            return pl.loop(0, width // TILE, unroll=unroll)

        sums = dot(pick[...], normed[pl.ds(0, ext), :])
        normed[pl.ds(ext, sum_rows), :] = (sums / divisor[...]).astype(jnp.bfloat16)

        scale = 1.0 / math.sqrt(head_dim)

        @tiles(4)
        def _(n):
            at = columns(n)
            block = normed[pl.ds(0, ext), :]
            ke[pl.ds(0, ext), at] = dot(block, wk[:, at]).astype(jnp.bfloat16)
            ve[pl.ds(0, ext), at] = dot(block, wv[:, at]).astype(jnp.bfloat16)
            askers = normed[pl.ds(ext - q_rows, q_rows + sum_rows), :]
            qe[:, at] = (dot(askers, wq[:, at]) * scale).astype(jnp.bfloat16)

        own_head = (iota((HEADS, width), 1) // head_dim) == iota((HEADS, width), 0)
        sq = qe[pl.ds(q_rows, sum_rows), :].astype(jnp.float32)
        spread_q = []
        for m in range(mems):
            line_q = jnp.broadcast_to(sq[m : m + 1, :], (HEADS, width))
            spread_q.append(jnp.where(own_head, line_q, 0.0).astype(jnp.bfloat16))
        spread_q = jnp.concatenate(spread_q)
        ms = jnp.minimum(dot_nt(spread_q, ke[pl.ds(0, mem_keys), :]), mem_bias[...])
        me = jnp.exp(ms - jnp.max(ms, axis=-1, keepdims=True))
        mw = me * (1.0 / jnp.sum(me, axis=-1, keepdims=True))
        mo = dot(mw.astype(jnp.bfloat16), ve[pl.ds(0, mem_keys), :])
        lines = []
        for m in range(mems):
            part = jnp.where(own_head, mo[m * HEADS : (m + 1) * HEADS, :], 0.0)
            lines.append(jnp.sum(part, axis=0, keepdims=True))
        lines.append(jnp.zeros((mem_pad - mems, width), jnp.float32))
        memory = jnp.concatenate(lines).astype(jnp.bfloat16)

        @tiles(4)
        def _(n):
            at = columns(n)
            ke[pl.ds(ext, mem_pad), at] = dot(memory, wk[:, at]).astype(jnp.bfloat16)
            ve[pl.ds(ext, mem_pad), at] = dot(memory, wv[:, at]).astype(jnp.bfloat16)

        even = iota((q_rows, PAIR), 1) < head_dim

        @pl.loop(0, width // PAIR, unroll=8)
        def _(n):
            at = pl.ds(pl.multiple_of(n * PAIR, PAIR), PAIR)
            qp = qe[pl.ds(0, q_rows), at]
            zero = jnp.zeros_like(qp)
            q_both = jnp.concatenate([jnp.where(even, qp, zero), jnp.where(even, zero, qp)])
            raw = dot_nt(q_both, ke[pl.ds(key_row, keys), at])
            edge = bias[...]
            scores = jnp.minimum(raw, jnp.concatenate([edge, edge]))
            weight = jnp.exp(scores - jnp.max(scores, axis=-1, keepdims=True))
            inverse = 1.0 / jnp.sum(weight, axis=-1, keepdims=True)
            both = dot(weight.astype(jnp.bfloat16), ve[pl.ds(key_row, keys), at]) * inverse
            ctx[:, at] = jnp.where(even, both[:q_rows], both[q_rows:]).astype(jnp.bfloat16)

        @tiles(4)
        def _(n):
            at = columns(n)
            x_part = jnp.concatenate([xe[pl.ds(HALO - SEG, SEG), at], own[pl.ds(0, rows), at]])
            mixed = x_part.astype(jnp.float32) + dot(ctx[...], wo[:, at])
            res[:, at] = mixed.astype(jnp.bfloat16)

        def set_cin(s, value):
            mask = frame_mask[pl.ds(s * SEG, SEG), :]
            value = (value * mask).astype(jnp.bfloat16)
            cin[pl.ds(s * SEG, SEG), :] = value.astype(jnp.float32)

        layer_norms(
            q_rows // SEG, lambda s: res[pl.ds(s * SEG, SEG), :].astype(jnp.float32), set_cin
        )

        @pl.loop(0, width // PAIR, unroll=2)
        def _(n):
            at = pl.ds(pl.multiple_of(n * PAIR, PAIR), PAIR)
            total = jnp.zeros((rows, PAIR), jnp.float32)
            block = cin[:, at]
            start = SEG - (KW - 1)
            for residue in range(8):
                size = rows + (8 if residue else 0)
                part = None
                for o in range(start, start + KW):
                    if o % 8 == residue:
                        base = o - residue
                        term = taps[pl.ds(o - start, 1), at] * block[base : base + size]
                        part = term if part is None else part + term
                if residue:
                    part = pltpu.roll(part, size - residue, 0)[:rows]
                total = total + part
            depth[:, at] = total

        def set_gated(s, value):
            value = value * (1.0 / (1.0 + jnp.exp(-value)))
            gated[pl.ds(s * SEG, SEG), :] = value.astype(jnp.bfloat16)

        layer_norms(rows // SEG, lambda s: depth[pl.ds(s * SEG, SEG), :], set_gated)

        row_mask = frame_mask[pl.ds(SEG, rows), :]

        @tiles(4)
        def _(n):
            at = columns(n)
            mixed = res[pl.ds(SEG, rows), at].astype(jnp.float32) + dot(gated[...], wp[:, at])
            made = (mixed * row_mask).astype(jnp.bfloat16)
            result[:, at] = made
            if last:
                pltpu.make_async_copy(
                    result.at[:, at], outputs.at[chunk, :, at], osem.at[n]
                ).start()
            else:
                if section % 2 == 0:
                    padded[pl.ds(0, rows), at] = made
                    padded[pl.ds(rows, PAD), at] = jnp.zeros((PAD, TILE), jnp.bfloat16)
                for tail in tails:
                    tail[:, at] = made[rows - tail.shape[0] :]

        if last:
            for n in range(width // TILE):
                at = pl.ds(n * TILE, TILE)
                pltpu.make_async_copy(
                    result.at[:, at], outputs.at[chunk, :, at], osem.at[n]
                ).wait()


def load_kernel(cfg, where, frame_counts, *refs):
    rows, segs_row, micro = cfg
    sources, targets, taps, masks = refs[:7], refs[7:13], refs[13], refs[14:19]
    narrow_taps, sem = refs[19:]
    targets = [*targets, narrow_taps]
    copies = [
        pltpu.make_async_copy(source, target, sem.at[n])
        for n, (source, target) in enumerate(zip(sources, targets))
    ]
    for copy in copies:
        copy.start()
    bias, mem_bias, pick, divisor, frame_mask = masks
    q_rows, keys = bias.shape[1:]
    mem_keys = mem_bias.shape[2]
    sum_rows, ext = pick.shape[1:]
    segs = ext // SEG
    q_seg = HALO_SEGS - 1
    mem_first = q_seg - NMEM
    mems = segs - 1 - mem_first
    key_seg = q_seg - BACK
    win = ext - key_seg * SEG
    for chunk in range(micro):
        first = chunk * segs_row + where[1] * (rows // SEG) - HALO_SEGS
        counts = []
        for s in range(segs):
            safe = jnp.maximum(first + s, 0)
            value = frame_counts[safe // segs_row, safe % segs_row]
            counts.append(jnp.where(first + s >= 0, value, 0))

        row_seg = q_seg + (iota((q_rows, keys), 0) >> SHIFT)
        line = iota((1, keys), 1)
        kvalid = (line & (SEG - 1)) < by_segment(line >> SHIFT, counts, key_seg, win // SEG)
        mvalid = by_segment(line - win, counts, mem_first, mems) > 0
        live = (kvalid & (line < win)) | (mvalid & (line >= win))
        lows = jnp.where(line < win, key_seg + (line >> SHIFT), mem_first + 1 + line - win)
        highs = jnp.where(line < win, lows + BACK, lows + NMEM - 1)
        lows = jnp.where(live, lows, segs)
        good = (row_seg >= lows) & (row_seg <= highs)
        bias[chunk] = jnp.where(good, OPEN, FAR)

        mseg = mem_first + (iota((mems * HEADS, mem_keys), 0) >> HEAD_SHIFT)
        mline = iota((1, mem_keys), 1)
        mlow = mline >> SHIFT
        mlive = (mline & (SEG - 1)) < by_segment(mlow, counts, 0, mem_keys // SEG)
        mhigh = mlow + BACK
        mlow = jnp.where(mlive, mlow, segs)
        mem_bias[chunk] = jnp.where((mseg >= mlow) & (mseg <= mhigh), OPEN, FAR)

        sseg = iota((sum_rows, ext), 0) + mem_first
        sline = iota((1, ext), 1)
        smine = sline >> SHIFT
        slive = (sline & (SEG - 1)) < by_segment(smine, counts, 0, segs)
        smine = jnp.where(slive, smine, -1)
        pick[chunk] = jnp.where(sseg == smine, 1.0, 0.0).astype(jnp.bfloat16)
        scount = by_segment(iota((sum_rows, 1), 0), counts, mem_first, mems)
        divisor[chunk] = jnp.maximum(scount, 1).astype(jnp.float32)

        frame = iota((q_rows, 1), 0)
        frame_count = by_segment(frame >> SHIFT, counts, q_seg, q_rows // SEG)
        frame_mask[chunk] = ((frame & (SEG - 1)) < frame_count).astype(jnp.float32)
    for copy in copies:
        copy.wait()
    taps[pl.ds(0, KW), :] = narrow_taps[...].astype(jnp.float32)


def per_device(frames, frame_counts, w_query, w_key, w_value, w_out, conv_kernel, w_point):
    micro, rows, width = frames.shape
    sections = lax.axis_size("phase")
    shards = lax.axis_size("tm")
    segs_row = frame_counts.shape[1]
    pieces = halo_pieces(rows)
    ext = HALO + rows
    q_rows = rows + SEG
    mems = ext // SEG - 1 - (HALO_SEGS - 1 - NMEM)
    mem_pad = -(-mems // SEG) * SEG
    sum_rows = -(-mems // 16) * 16
    mem_keys = (mems + BACK) * SEG
    keys = ext + mem_pad - (HALO_SEGS - 1 - BACK) * SEG

    def send(block, distance, source, target):
        route = [
            (s * sections + source, (s + distance) % shards * sections + target)
            for s in range(shards)
        ]
        return lax.ppermute(block, ("tm", "phase"), route)

    inbox = [
        [None]
        + [
            send(frames[chunk, rows - take :, :], distance, distance % sections, 0)
            for distance, take in pieces
        ]
        for chunk in range(micro)
    ]

    where = jnp.stack([lax.axis_index("phase"), lax.axis_index("tm")]).astype(jnp.int32)

    def vmem(*shape, dtype=jnp.bfloat16):
        return pltpu.VMEM(shape, dtype)

    scratch = [
        vmem(HALO, width), vmem(ext + sum_rows, width),
        vmem(ext + mem_pad, width), vmem(ext + mem_pad, width),
        vmem(q_rows + sum_rows, width), vmem(q_rows, width), vmem(q_rows, width),
        vmem(q_rows, width, dtype=jnp.float32), vmem(rows, width, dtype=jnp.float32),
        vmem(rows, width), vmem(rows, width),
        pltpu.SemaphoreType.DMA((width // TILE,)),
    ]
    smem = pl.BlockSpec(memory_space=pltpu.SMEM)
    hbm = pl.BlockSpec(memory_space=pltpu.HBM)
    in_vmem = pl.BlockSpec(memory_space=pltpu.VMEM)
    def kept(array, space):
        return pltpu.with_memory_space_constraint(array, space)

    near_by = pl.pallas_call(
        functools.partial(load_kernel, (rows, segs_row, micro)),
        out_shape=[vmem(width, width)] * 5
        + [
            vmem(micro, rows, width),
            vmem(32, width, dtype=jnp.float32),
            vmem(micro, q_rows, keys, dtype=jnp.float32),
            vmem(micro, mems * HEADS, mem_keys, dtype=jnp.float32),
            vmem(micro, sum_rows, ext),
            vmem(micro, sum_rows, 1, dtype=jnp.float32),
            vmem(micro, q_rows, 1, dtype=jnp.float32),
        ],
        in_specs=[smem] * 2 + [hbm] * 7,
        out_specs=[in_vmem] * 12,
        scratch_shapes=[vmem(KW, width), pltpu.SemaphoreType.DMA((7,))],
        cost_estimate=pl.CostEstimate(flops=0, bytes_accessed=10**7, transcendentals=0),
        compiler_params=pltpu.CompilerParams(vmem_limit_bytes=4 * 1024 * 1024),
        name="load",
    )(
        where,
        kept(frame_counts, pltpu.HBM),
        *[kept(w[0], pltpu.HBM) for w in (w_key, w_value, w_query, w_out, w_point)],
        kept(frames, pltpu.HBM),
        kept(conv_kernel[0], pltpu.HBM),
    )
    near_by = [kept(w, pltpu.VMEM) for w in near_by]
    frames_near = near_by.pop(5)
    block = vmem(rows, width)
    tails = [vmem(take, width) for _, take in pieces if take < rows]
    whole = pltpu.HBM((micro, rows, width), jnp.bfloat16)
    cost = pl.CostEstimate(flops=6 * 10**9, bytes_accessed=12 * 10**6, transcendentals=10**6)

    outputs = None
    results = {}
    for section in range(sections):
        outbox = []
        for chunk in range(micro):
            own = inbox[chunk][0] if section > 0 else frames_near
            near = [own, *inbox[chunk][1:]]
            if chunk > 0:
                near += inbox[chunk - 1][1:]
            if section > 0:
                near.append(results[section - 1, chunk])
            args = [where, *near_by, *[kept(array, pltpu.VMEM) for array in near]]
            in_specs = [smem] + [in_vmem] * (len(args) - 1)
            aliases = {}
            if outputs is not None:
                aliases = {len(args): 0}
                args.append(kept(outputs, pltpu.HBM))
                in_specs.append(hbm)
            last = section == sections - 1
            padded = [vmem(rows + PAD, width)] if section % 2 == 0 else []
            outs = [whole] if last else [whole, block, *padded, *tails]
            cfg = (rows, width, section, chunk, sections, shards, segs_row, pieces)
            made = pl.pallas_call(
                functools.partial(layer_kernel, cfg),
                out_shape=outs,
                in_specs=in_specs,
                out_specs=[hbm] + [in_vmem] * (len(outs) - 1),
                scratch_shapes=scratch,
                input_output_aliases=aliases,
                cost_estimate=cost,
                compiler_params=pltpu.CompilerParams(vmem_limit_bytes=VMEM_BYTES),
                name="layer",
            )(*args)
            outputs = made[0]
            if not last:
                results[section, chunk] = made[1]
                whole_block, tails_out = made[1], iter(made[2:])
                got = {0: next(tails_out) if section % 2 == 0 else whole_block}
                for distance, take in pieces:
                    got[distance] = next(tails_out) if take < rows else whole_block
                far = max(got)
                if outbox and far > 0:
                    near = outbox[-1][0]
                    got[far], outbox[-1][0] = lax.optimization_barrier((got[far], near))
                sent = {d: send(got[d], d, section, section + 1) for d in got}
                outbox.append([sent[d] for d in sorted(got)])
        inbox = outbox
    return outputs[None]


def solution(mesh):
    in_specs = (
        P(None, "tm", None),
        P(),
        P("phase", None, None),
        P("phase", None, None),
        P("phase", None, None),
        P("phase", None, None),
        P("phase", None, None),
        P("phase", None, None),
    )
    out_specs = P("phase", None, "tm", None)
    return jax.shard_map(
        per_device, mesh=mesh, in_specs=in_specs, out_specs=out_specs, check_vma=False
    )
```

```python
import functools
import math

import jax
import jax.numpy as jnp
from jax import lax
from jax.experimental import pallas as pl
from jax.experimental.pallas import tpu as pltpu
from jax.sharding import PartitionSpec as P

HEADS = 16
SEG = 32
LC = 64
NMEM = 4
KW = 31

EPSILON = 1e-05
BACK = LC // SEG
HALO_SEGS = 1 + NMEM + BACK
HALO = HALO_SEGS * SEG
FAR = -1e30
OPEN = 3e38
TILE = 256
PAIR = 128
PAD = 16
SHIFT = 5
HEAD_SHIFT = 4
VMEM_BYTES = 32 * 1024 * 1024


def layer_norms(number, load, store):
    means = [jnp.mean(load(s), axis=-1, keepdims=True) for s in range(number)]
    scales = []
    for s in range(number):
        center = load(s) - means[s]
        scales.append(lax.rsqrt(jnp.mean(center * center, axis=-1, keepdims=True) + EPSILON))
    for s in range(number):
        store(s, (load(s) - means[s]) * scales[s])


def dot(a, b):
    return jnp.dot(a, b, preferred_element_type=jnp.float32)


def dot_nt(a, b):
    return lax.dot_general(a, b, (((1,), (1,)), ((), ())), preferred_element_type=jnp.float32)


def halo_pieces(rows):
    pieces = []
    left = HALO
    while left > 0:
        take = min(rows, left)
        pieces.append((len(pieces) + 1, take))
        left -= take
    return pieces


def passed_on(section, chunk):
    return section > 0 and chunk == 0


def tail_of(ref, rows):
    return ref.at[pl.ds(ref.shape[0] - rows, rows)]


def by_segment(index, counts, first, number):
    out = jnp.zeros(index.shape, jnp.int32)
    for s in range(number):
        out = jnp.where(index == s, counts[first + s], out)
    return out


def iota(shape, dimension):
    return lax.broadcasted_iota(jnp.int32, shape, dimension)


def layer_kernel(cfg, *refs):
    rows, width, section, chunk, sections, shards, segs_row, pieces = cfg
    refs = list(refs)
    where = refs[0]
    wk, wv, wq, wo, wp, taps = refs[1:7]
    bias, mem_bias, pick, divisor, frame_mask = [ref.at[chunk] for ref in refs[7:12]]
    refs = refs[12:]
    count_p = len(pieces)
    own, halos, refs = refs[0], refs[1 : 1 + count_p], refs[1 + count_p :]
    if section == 0:
        own = own.at[chunk]
    if chunk > 0:
        befores, refs = refs[:count_p], refs[count_p:]
    halos = [tail_of(halo, take) for halo, (_, take) in zip(halos, pieces)]
    if chunk > 0:
        befores = [tail_of(halo, take) for halo, (_, take) in zip(befores, pieces)]
    if section > 0:
        earlier, refs = refs[0], refs[1:]
    if section + chunk > 0:
        refs = refs[1:]
    outputs, refs = refs[0], refs[1:]
    last = section == sections - 1
    if not last:
        result, refs = refs[0], refs[1:]
        direct = not passed_on(section, chunk)
        if direct and section % 2 == 0:
            padded, refs = refs[0], refs[1:]
        number = sum(1 for _, take in pieces if take < rows) if direct else 0
        tails, refs = refs[:number], refs[number:]
    (xe, normed, ke, ve, qe, ctx, res, cin, depth, gated, staged, osem) = refs
    if last:
        result = staged

    ext = HALO + rows
    segs = ext // SEG
    q_rows = rows + SEG
    q_seg = HALO_SEGS - 1
    mems = segs - 1 - (q_seg - NMEM)
    mem_pad = ke.shape[0] - ext
    key_row = (q_seg - BACK) * SEG
    keys = ke.shape[0] - key_row
    mem_keys = mem_bias.shape[1]
    head_dim = width // HEADS
    sum_rows = qe.shape[0] - q_rows
    phase, shard = where[0], where[1]

    if section > 0:
        @pl.when(phase == section - 1)
        def _():
            copy = pltpu.make_async_copy(earlier, outputs.at[chunk], osem.at[0])
            copy.start()
            copy.wait()

    @pl.when(phase == section)
    def _():
        for n, (distance, take) in enumerate(pieces):
            spot = pl.ds(HALO - (distance - 1) * rows - take, take)

            @pl.when(shard >= distance)
            def _():
                xe[spot, :] = halos[n][...]

            @pl.when(shard < distance)
            def _():
                if chunk > 0:
                    xe[spot, :] = befores[n][...]
                else:
                    xe[spot, :] = jnp.zeros((take, width), jnp.bfloat16)

        def load_x(s):
            if s < HALO_SEGS:
                part = xe[pl.ds(s * SEG, SEG), :]
            else:
                part = own[pl.ds((s - HALO_SEGS) * SEG, SEG), :]
            return part.astype(jnp.float32)

        def set_normed(s, value):
            normed[pl.ds(s * SEG, SEG), :] = value.astype(jnp.bfloat16)

        layer_norms(segs, load_x, set_normed)

        def columns(n):
            return pl.ds(pl.multiple_of(n * TILE, TILE), TILE)

        def tiles(unroll):
            return pl.loop(0, width // TILE, unroll=unroll)

        sums = dot(pick[...], normed[pl.ds(0, ext), :])
        normed[pl.ds(ext, sum_rows), :] = (sums / divisor[...]).astype(jnp.bfloat16)

        scale = 1.0 / math.sqrt(head_dim)

        @tiles(4)
        def _(n):
            at = columns(n)
            block = normed[pl.ds(0, ext), :]
            ke[pl.ds(0, ext), at] = dot(block, wk[:, at]).astype(jnp.bfloat16)
            ve[pl.ds(0, ext), at] = dot(block, wv[:, at]).astype(jnp.bfloat16)
            askers = normed[pl.ds(ext - q_rows, q_rows + sum_rows), :]
            qe[:, at] = (dot(askers, wq[:, at]) * scale).astype(jnp.bfloat16)

        own_head = (iota((HEADS, width), 1) // head_dim) == iota((HEADS, width), 0)
        sq = qe[pl.ds(q_rows, sum_rows), :].astype(jnp.float32)
        spread_q = []
        for m in range(mems):
            line_q = jnp.broadcast_to(sq[m : m + 1, :], (HEADS, width))
            spread_q.append(jnp.where(own_head, line_q, 0.0).astype(jnp.bfloat16))
        spread_q = jnp.concatenate(spread_q)
        ms = jnp.minimum(dot_nt(spread_q, ke[pl.ds(0, mem_keys), :]), mem_bias[...])
        me = jnp.exp(ms - jnp.max(ms, axis=-1, keepdims=True))
        mw = me * (1.0 / jnp.sum(me, axis=-1, keepdims=True))
        mo = dot(mw.astype(jnp.bfloat16), ve[pl.ds(0, mem_keys), :])
        lines = []
        for m in range(mems):
            part = jnp.where(own_head, mo[m * HEADS : (m + 1) * HEADS, :], 0.0)
            lines.append(jnp.sum(part, axis=0, keepdims=True))
        lines.append(jnp.zeros((mem_pad - mems, width), jnp.float32))
        memory = jnp.concatenate(lines).astype(jnp.bfloat16)

        @tiles(4)
        def _(n):
            at = columns(n)
            ke[pl.ds(ext, mem_pad), at] = dot(memory, wk[:, at]).astype(jnp.bfloat16)
            ve[pl.ds(ext, mem_pad), at] = dot(memory, wv[:, at]).astype(jnp.bfloat16)

        even = iota((q_rows, PAIR), 1) < head_dim

        @pl.loop(0, width // PAIR, unroll=8)
        def _(n):
            at = pl.ds(pl.multiple_of(n * PAIR, PAIR), PAIR)
            qp = qe[pl.ds(0, q_rows), at]
            zero = jnp.zeros_like(qp)
            q_both = jnp.concatenate([jnp.where(even, qp, zero), jnp.where(even, zero, qp)])
            raw = dot_nt(q_both, ke[pl.ds(key_row, keys), at])
            edge = bias[...]
            scores = jnp.minimum(raw, jnp.concatenate([edge, edge]))
            weight = jnp.exp(scores - jnp.max(scores, axis=-1, keepdims=True))
            inverse = 1.0 / jnp.sum(weight, axis=-1, keepdims=True)
            both = dot(weight.astype(jnp.bfloat16), ve[pl.ds(key_row, keys), at]) * inverse
            ctx[:, at] = jnp.where(even, both[:q_rows], both[q_rows:]).astype(jnp.bfloat16)

        @tiles(4)
        def _(n):
            at = columns(n)
            x_part = jnp.concatenate([xe[pl.ds(HALO - SEG, SEG), at], own[pl.ds(0, rows), at]])
            mixed = x_part.astype(jnp.float32) + dot(ctx[...], wo[:, at])
            res[:, at] = mixed.astype(jnp.bfloat16)

        def set_cin(s, value):
            mask = frame_mask[pl.ds(s * SEG, SEG), :]
            value = (value * mask).astype(jnp.bfloat16)
            cin[pl.ds(s * SEG, SEG), :] = value.astype(jnp.float32)

        layer_norms(
            q_rows // SEG, lambda s: res[pl.ds(s * SEG, SEG), :].astype(jnp.float32), set_cin
        )

        @pl.loop(0, width // PAIR, unroll=2)
        def _(n):
            at = pl.ds(pl.multiple_of(n * PAIR, PAIR), PAIR)
            total = jnp.zeros((rows, PAIR), jnp.float32)
            block = cin[:, at]
            start = SEG - (KW - 1)
            for residue in range(8):
                size = rows + (8 if residue else 0)
                part = None
                for o in range(start, start + KW):
                    if o % 8 == residue:
                        base = o - residue
                        term = taps[pl.ds(o - start, 1), at] * block[base : base + size]
                        part = term if part is None else part + term
                if residue:
                    part = pltpu.roll(part, size - residue, 0)[:rows]
                total = total + part
            depth[:, at] = total

        def set_gated(s, value):
            value = value * (1.0 / (1.0 + jnp.exp(-value)))
            gated[pl.ds(s * SEG, SEG), :] = value.astype(jnp.bfloat16)

        layer_norms(rows // SEG, lambda s: depth[pl.ds(s * SEG, SEG), :], set_gated)

        row_mask = frame_mask[pl.ds(SEG, rows), :]

        @tiles(4)
        def _(n):
            at = columns(n)
            mixed = res[pl.ds(SEG, rows), at].astype(jnp.float32) + dot(gated[...], wp[:, at])
            made = (mixed * row_mask).astype(jnp.bfloat16)
            result[:, at] = made
            if last:
                pltpu.make_async_copy(
                    result.at[:, at], outputs.at[chunk, :, at], osem.at[n]
                ).start()
            else:
                if direct and section % 2 == 0:
                    padded[pl.ds(0, rows), at] = made
                    padded[pl.ds(rows, PAD), at] = jnp.zeros((PAD, TILE), jnp.bfloat16)
                for tail in tails:
                    tail[:, at] = made[rows - tail.shape[0] :]

        if last:
            for n in range(width // TILE):
                at = pl.ds(n * TILE, TILE)
                pltpu.make_async_copy(
                    result.at[:, at], outputs.at[chunk, :, at], osem.at[n]
                ).wait()


def load_kernel(cfg, where, frame_counts, *refs):
    rows, segs_row, micro = cfg
    sources, targets, taps, masks = refs[:7], refs[7:13], refs[13], refs[14:19]
    narrow_taps, sem = refs[19:]
    targets = [*targets, narrow_taps]
    copies = [
        pltpu.make_async_copy(source, target, sem.at[n])
        for n, (source, target) in enumerate(zip(sources, targets))
    ]
    for copy in copies:
        copy.start()
    bias, mem_bias, pick, divisor, frame_mask = masks
    q_rows, keys = bias.shape[1:]
    mem_keys = mem_bias.shape[2]
    sum_rows, ext = pick.shape[1:]
    segs = ext // SEG
    q_seg = HALO_SEGS - 1
    mem_first = q_seg - NMEM
    mems = segs - 1 - mem_first
    key_seg = q_seg - BACK
    win = ext - key_seg * SEG
    for chunk in range(micro):
        first = chunk * segs_row + where[1] * (rows // SEG) - HALO_SEGS
        counts = []
        for s in range(segs):
            safe = jnp.maximum(first + s, 0)
            value = frame_counts[safe // segs_row, safe % segs_row]
            counts.append(jnp.where(first + s >= 0, value, 0))

        row_seg = q_seg + (iota((q_rows, keys), 0) >> SHIFT)
        line = iota((1, keys), 1)
        kvalid = (line & (SEG - 1)) < by_segment(line >> SHIFT, counts, key_seg, win // SEG)
        mvalid = by_segment(line - win, counts, mem_first, mems) > 0
        live = (kvalid & (line < win)) | (mvalid & (line >= win))
        lows = jnp.where(line < win, key_seg + (line >> SHIFT), mem_first + 1 + line - win)
        highs = jnp.where(line < win, lows + BACK, lows + NMEM - 1)
        lows = jnp.where(live, lows, segs)
        good = (row_seg >= lows) & (row_seg <= highs)
        bias[chunk] = jnp.where(good, OPEN, FAR)

        mseg = mem_first + (iota((mems * HEADS, mem_keys), 0) >> HEAD_SHIFT)
        mline = iota((1, mem_keys), 1)
        mlow = mline >> SHIFT
        mlive = (mline & (SEG - 1)) < by_segment(mlow, counts, 0, mem_keys // SEG)
        mhigh = mlow + BACK
        mlow = jnp.where(mlive, mlow, segs)
        mem_bias[chunk] = jnp.where((mseg >= mlow) & (mseg <= mhigh), OPEN, FAR)

        sseg = iota((sum_rows, ext), 0) + mem_first
        sline = iota((1, ext), 1)
        smine = sline >> SHIFT
        slive = (sline & (SEG - 1)) < by_segment(smine, counts, 0, segs)
        smine = jnp.where(slive, smine, -1)
        pick[chunk] = jnp.where(sseg == smine, 1.0, 0.0).astype(jnp.bfloat16)
        scount = by_segment(iota((sum_rows, 1), 0), counts, mem_first, mems)
        divisor[chunk] = jnp.maximum(scount, 1).astype(jnp.float32)

        frame = iota((q_rows, 1), 0)
        frame_count = by_segment(frame >> SHIFT, counts, q_seg, q_rows // SEG)
        frame_mask[chunk] = ((frame & (SEG - 1)) < frame_count).astype(jnp.float32)
    for copy in copies:
        copy.wait()
    taps[pl.ds(0, KW), :] = narrow_taps[...].astype(jnp.float32)


def per_device(frames, frame_counts, w_query, w_key, w_value, w_out, conv_kernel, w_point):
    micro, rows, width = frames.shape
    sections = lax.axis_size("phase")
    shards = lax.axis_size("tm")
    segs_row = frame_counts.shape[1]
    pieces = halo_pieces(rows)
    ext = HALO + rows
    q_rows = rows + SEG
    mems = ext // SEG - 1 - (HALO_SEGS - 1 - NMEM)
    mem_pad = -(-mems // SEG) * SEG
    sum_rows = -(-mems // 16) * 16
    mem_keys = (mems + BACK) * SEG
    keys = ext + mem_pad - (HALO_SEGS - 1 - BACK) * SEG

    def send(block, distance, source, target):
        route = [
            (s * sections + source, (s + distance) % shards * sections + target)
            for s in range(shards)
        ]
        return lax.ppermute(block, ("tm", "phase"), route)

    inbox = [
        [None]
        + [
            send(frames[chunk, rows - take :, :], distance, distance % sections, 0)
            for distance, take in pieces
        ]
        for chunk in range(micro)
    ]

    where = jnp.stack([lax.axis_index("phase"), lax.axis_index("tm")]).astype(jnp.int32)

    def vmem(*shape, dtype=jnp.bfloat16):
        return pltpu.VMEM(shape, dtype)

    scratch = [
        vmem(HALO, width), vmem(ext + sum_rows, width),
        vmem(ext + mem_pad, width), vmem(ext + mem_pad, width),
        vmem(q_rows + sum_rows, width), vmem(q_rows, width), vmem(q_rows, width),
        vmem(q_rows, width, dtype=jnp.float32), vmem(rows, width, dtype=jnp.float32),
        vmem(rows, width), vmem(rows, width),
        pltpu.SemaphoreType.DMA((width // TILE,)),
    ]
    smem = pl.BlockSpec(memory_space=pltpu.SMEM)
    hbm = pl.BlockSpec(memory_space=pltpu.HBM)
    in_vmem = pl.BlockSpec(memory_space=pltpu.VMEM)
    def kept(array, space):
        return pltpu.with_memory_space_constraint(array, space)

    near_by = pl.pallas_call(
        functools.partial(load_kernel, (rows, segs_row, micro)),
        out_shape=[vmem(width, width)] * 5
        + [
            vmem(micro, rows, width),
            vmem(32, width, dtype=jnp.float32),
            vmem(micro, q_rows, keys, dtype=jnp.float32),
            vmem(micro, mems * HEADS, mem_keys, dtype=jnp.float32),
            vmem(micro, sum_rows, ext),
            vmem(micro, sum_rows, 1, dtype=jnp.float32),
            vmem(micro, q_rows, 1, dtype=jnp.float32),
        ],
        in_specs=[smem] * 2 + [hbm] * 7,
        out_specs=[in_vmem] * 12,
        scratch_shapes=[vmem(KW, width), pltpu.SemaphoreType.DMA((7,))],
        cost_estimate=pl.CostEstimate(flops=0, bytes_accessed=10**7, transcendentals=0),
        compiler_params=pltpu.CompilerParams(vmem_limit_bytes=4 * 1024 * 1024),
        name="load",
    )(
        where,
        kept(frame_counts, pltpu.HBM),
        *[kept(w[0], pltpu.HBM) for w in (w_key, w_value, w_query, w_out, w_point)],
        kept(frames, pltpu.HBM),
        kept(conv_kernel[0], pltpu.HBM),
    )
    near_by = [kept(w, pltpu.VMEM) for w in near_by]
    frames_near = near_by.pop(5)
    block = vmem(rows, width)
    tails = [vmem(take, width) for _, take in pieces if take < rows]
    whole = pltpu.HBM((micro, rows, width), jnp.bfloat16)
    cost = pl.CostEstimate(flops=6 * 10**9, bytes_accessed=12 * 10**6, transcendentals=10**6)

    outputs = None
    results = {}
    for section in range(sections):
        outbox = []
        for chunk in range(micro):
            own = inbox[chunk][0] if section > 0 else frames_near
            near = [own, *inbox[chunk][1:]]
            if chunk > 0:
                near += inbox[chunk - 1][1:]
            if section > 0:
                near.append(results[section - 1, chunk])
            args = [where, *near_by, *[kept(array, pltpu.VMEM) for array in near]]
            in_specs = [smem] + [in_vmem] * (len(args) - 1)
            aliases = {}
            if outputs is not None:
                aliases = {len(args): 0}
                args.append(kept(outputs, pltpu.HBM))
                in_specs.append(hbm)
            last = section == sections - 1
            direct = not passed_on(section, chunk)
            padded = [vmem(rows + PAD, width)] if direct and section % 2 == 0 else []
            outs = [whole] if last else [whole, block, *padded, *(tails if direct else [])]
            cfg = (rows, width, section, chunk, sections, shards, segs_row, pieces)
            made = pl.pallas_call(
                functools.partial(layer_kernel, cfg),
                out_shape=outs,
                in_specs=in_specs,
                out_specs=[hbm] + [in_vmem] * (len(outs) - 1),
                scratch_shapes=scratch,
                input_output_aliases=aliases,
                cost_estimate=cost,
                compiler_params=pltpu.CompilerParams(vmem_limit_bytes=VMEM_BYTES),
                name="layer",
            )(*args)
            outputs = made[0]
            if not last:
                results[section, chunk] = made[1]
                whole_block, tails_out = made[1], list(made[2:])
                own_out = tails_out.pop(0) if padded else whole_block
                if passed_on(section, chunk):
                    outbox.append([send(own_out, 0, section, section + 1)])
                    continue
                got = {0: own_out}
                for distance, take in pieces:
                    got[distance] = tails_out.pop(0) if take < rows else whole_block
                far = max(got)
                if outbox and len(outbox[-1]) > 1 and far > 0:
                    near = outbox[-1][0]
                    got[far], outbox[-1][0] = lax.optimization_barrier((got[far], near))
                sent = {d: send(got[d], d, section, section + 1) for d in got}
                outbox.append([sent[d] for d in sorted(got)])
        if outbox and passed_on(section, 0):
            first = outbox[0]
            first[0], _ = lax.optimization_barrier((first[0], results[section, micro - 1]))
            first += [send(first[0], distance, section + 1, section + 1) for distance, _ in pieces]
        inbox = outbox
    return outputs[None]


def solution(mesh):
    in_specs = (
        P(None, "tm", None),
        P(),
        P("phase", None, None),
        P("phase", None, None),
        P("phase", None, None),
        P("phase", None, None),
        P("phase", None, None),
        P("phase", None, None),
    )
    out_specs = P("phase", None, "tm", None)
    return jax.shard_map(
        per_device, mesh=mesh, in_specs=in_specs, out_specs=out_specs, check_vma=False
    )
```

```python
import functools
import math

import jax
import jax.numpy as jnp
from jax import lax
from jax.experimental import pallas as pl
from jax.experimental.pallas import tpu as pltpu
from jax.sharding import PartitionSpec as P

HEADS = 16
SEG = 32
LC = 64
NMEM = 4
KW = 31

EPSILON = 1e-05
BACK = LC // SEG
HALO_SEGS = 1 + NMEM + BACK
HALO = HALO_SEGS * SEG
FAR = -1e30
OPEN = 3e38
TILE = 256
PAIR = 128
PAD = 16
SHIFT = 5
HEAD_SHIFT = 4
VMEM_BYTES = 32 * 1024 * 1024


def layer_norms(number, load, store):
    means = [jnp.mean(load(s), axis=-1, keepdims=True) for s in range(number)]
    scales = []
    for s in range(number):
        center = load(s) - means[s]
        scales.append(lax.rsqrt(jnp.mean(center * center, axis=-1, keepdims=True) + EPSILON))
    for s in range(number):
        store(s, (load(s) - means[s]) * scales[s])


def dot(a, b):
    return jnp.dot(a, b, preferred_element_type=jnp.float32)


def dot_nt(a, b):
    return lax.dot_general(a, b, (((1,), (1,)), ((), ())), preferred_element_type=jnp.float32)


def halo_pieces(rows):
    pieces = []
    left = HALO
    while left > 0:
        take = min(rows, left)
        pieces.append((len(pieces) + 1, take))
        left -= take
    return pieces


def halo_sent(chunk, rows, pieces):
    return [(distance, take) for distance, take in pieces if chunk > 0 or take < rows]


def by_segment(index, counts, first, number):
    out = jnp.zeros(index.shape, jnp.int32)
    for s in range(number):
        out = jnp.where(index == s, counts[first + s], out)
    return out


def iota(shape, dimension):
    return lax.broadcasted_iota(jnp.int32, shape, dimension)


def layer_kernel(cfg, *refs):
    rows, width, section, chunk, sections, shards, segs_row, pieces = cfg
    refs = list(refs)
    where = refs[0]
    wk, wv, wq, wo, wp, taps = refs[1:7]
    bias, mem_bias, pick, divisor, frame_mask = [ref.at[chunk] for ref in refs[7:12]]
    refs = refs[12:]
    count_p = len(pieces)
    own, halos, refs = refs[0], refs[1 : 1 + count_p], refs[1 + count_p :]
    if section == 0:
        own = own.at[chunk]
    if section > 0:
        earlier, refs = refs[0], refs[1:]
    if chunk > 0 and section < sections - 1:
        prior, refs = refs[0], refs[1:]
    if section + chunk > 0:
        refs = refs[1:]
    outputs, refs = refs[0], refs[1:]
    last = section == sections - 1
    if not last:
        result, refs = refs[0], refs[1:]
        if section % 2 == 0:
            padded, refs = refs[0], refs[1:]
        sent = halo_sent(chunk, rows, pieces)
        tails, refs = refs[: len(sent)], refs[len(sent) :]
    (xe, normed, ke, ve, qe, ctx, res, cin, depth, gated, staged, osem) = refs
    if last:
        result = staged

    ext = HALO + rows
    segs = ext // SEG
    q_rows = rows + SEG
    q_seg = HALO_SEGS - 1
    mems = segs - 1 - (q_seg - NMEM)
    mem_pad = ke.shape[0] - ext
    key_row = (q_seg - BACK) * SEG
    keys = ke.shape[0] - key_row
    mem_keys = mem_bias.shape[1]
    head_dim = width // HEADS
    sum_rows = qe.shape[0] - q_rows
    phase, shard = where[0], where[1]

    if section > 0:
        @pl.when(phase == section - 1)
        def _():
            copy = pltpu.make_async_copy(earlier, outputs.at[chunk], osem.at[0])
            copy.start()
            copy.wait()

    @pl.when(phase == section)
    def _():
        for n, (distance, take) in enumerate(pieces):
            spot = pl.ds(HALO - (distance - 1) * rows - take, take)

            if chunk > 0:
                xe[spot, :] = halos[n][...]
            else:
                @pl.when(shard >= distance)
                def _():
                    xe[spot, :] = halos[n][...]

                @pl.when(shard < distance)
                def _():
                    xe[spot, :] = jnp.zeros((take, width), jnp.bfloat16)

        def load_x(s):
            if s < HALO_SEGS:
                part = xe[pl.ds(s * SEG, SEG), :]
            else:
                part = own[pl.ds((s - HALO_SEGS) * SEG, SEG), :]
            return part.astype(jnp.float32)

        def set_normed(s, value):
            normed[pl.ds(s * SEG, SEG), :] = value.astype(jnp.bfloat16)

        layer_norms(segs, load_x, set_normed)

        def columns(n):
            return pl.ds(pl.multiple_of(n * TILE, TILE), TILE)

        def tiles(unroll):
            return pl.loop(0, width // TILE, unroll=unroll)

        sums = dot(pick[...], normed[pl.ds(0, ext), :])
        normed[pl.ds(ext, sum_rows), :] = (sums / divisor[...]).astype(jnp.bfloat16)

        scale = 1.0 / math.sqrt(head_dim)

        @tiles(4)
        def _(n):
            at = columns(n)
            block = normed[pl.ds(0, ext), :]
            ke[pl.ds(0, ext), at] = dot(block, wk[:, at]).astype(jnp.bfloat16)
            ve[pl.ds(0, ext), at] = dot(block, wv[:, at]).astype(jnp.bfloat16)
            askers = normed[pl.ds(ext - q_rows, q_rows + sum_rows), :]
            qe[:, at] = (dot(askers, wq[:, at]) * scale).astype(jnp.bfloat16)

        own_head = (iota((HEADS, width), 1) // head_dim) == iota((HEADS, width), 0)
        sq = qe[pl.ds(q_rows, sum_rows), :].astype(jnp.float32)
        spread_q = []
        for m in range(mems):
            line_q = jnp.broadcast_to(sq[m : m + 1, :], (HEADS, width))
            spread_q.append(jnp.where(own_head, line_q, 0.0).astype(jnp.bfloat16))
        spread_q = jnp.concatenate(spread_q)
        ms = jnp.minimum(dot_nt(spread_q, ke[pl.ds(0, mem_keys), :]), mem_bias[...])
        me = jnp.exp(ms - jnp.max(ms, axis=-1, keepdims=True))
        mw = me * (1.0 / jnp.sum(me, axis=-1, keepdims=True))
        mo = dot(mw.astype(jnp.bfloat16), ve[pl.ds(0, mem_keys), :])
        lines = []
        for m in range(mems):
            part = jnp.where(own_head, mo[m * HEADS : (m + 1) * HEADS, :], 0.0)
            lines.append(jnp.sum(part, axis=0, keepdims=True))
        lines.append(jnp.zeros((mem_pad - mems, width), jnp.float32))
        memory = jnp.concatenate(lines).astype(jnp.bfloat16)

        @tiles(4)
        def _(n):
            at = columns(n)
            ke[pl.ds(ext, mem_pad), at] = dot(memory, wk[:, at]).astype(jnp.bfloat16)
            ve[pl.ds(ext, mem_pad), at] = dot(memory, wv[:, at]).astype(jnp.bfloat16)

        even = iota((q_rows, PAIR), 1) < head_dim

        @pl.loop(0, width // PAIR, unroll=8)
        def _(n):
            at = pl.ds(pl.multiple_of(n * PAIR, PAIR), PAIR)
            qp = qe[pl.ds(0, q_rows), at]
            zero = jnp.zeros_like(qp)
            q_both = jnp.concatenate([jnp.where(even, qp, zero), jnp.where(even, zero, qp)])
            raw = dot_nt(q_both, ke[pl.ds(key_row, keys), at])
            edge = bias[...]
            scores = jnp.minimum(raw, jnp.concatenate([edge, edge]))
            weight = jnp.exp(scores - jnp.max(scores, axis=-1, keepdims=True))
            inverse = 1.0 / jnp.sum(weight, axis=-1, keepdims=True)
            both = dot(weight.astype(jnp.bfloat16), ve[pl.ds(key_row, keys), at]) * inverse
            ctx[:, at] = jnp.where(even, both[:q_rows], both[q_rows:]).astype(jnp.bfloat16)

        @tiles(4)
        def _(n):
            at = columns(n)
            x_part = jnp.concatenate([xe[pl.ds(HALO - SEG, SEG), at], own[pl.ds(0, rows), at]])
            mixed = x_part.astype(jnp.float32) + dot(ctx[...], wo[:, at])
            res[:, at] = mixed.astype(jnp.bfloat16)

        def set_cin(s, value):
            mask = frame_mask[pl.ds(s * SEG, SEG), :]
            value = (value * mask).astype(jnp.bfloat16)
            cin[pl.ds(s * SEG, SEG), :] = value.astype(jnp.float32)

        layer_norms(
            q_rows // SEG, lambda s: res[pl.ds(s * SEG, SEG), :].astype(jnp.float32), set_cin
        )

        @pl.loop(0, width // PAIR, unroll=2)
        def _(n):
            at = pl.ds(pl.multiple_of(n * PAIR, PAIR), PAIR)
            total = jnp.zeros((rows, PAIR), jnp.float32)
            block = cin[:, at]
            start = SEG - (KW - 1)
            for residue in range(8):
                size = rows + (8 if residue else 0)
                part = None
                for o in range(start, start + KW):
                    if o % 8 == residue:
                        base = o - residue
                        term = taps[pl.ds(o - start, 1), at] * block[base : base + size]
                        part = term if part is None else part + term
                if residue:
                    part = pltpu.roll(part, size - residue, 0)[:rows]
                total = total + part
            depth[:, at] = total

        def set_gated(s, value):
            value = value * (1.0 / (1.0 + jnp.exp(-value)))
            gated[pl.ds(s * SEG, SEG), :] = value.astype(jnp.bfloat16)

        layer_norms(rows // SEG, lambda s: depth[pl.ds(s * SEG, SEG), :], set_gated)

        row_mask = frame_mask[pl.ds(SEG, rows), :]

        @tiles(4)
        def _(n):
            at = columns(n)
            mixed = res[pl.ds(SEG, rows), at].astype(jnp.float32) + dot(gated[...], wp[:, at])
            made = (mixed * row_mask).astype(jnp.bfloat16)
            result[:, at] = made
            if last:
                pltpu.make_async_copy(
                    result.at[:, at], outputs.at[chunk, :, at], osem.at[n]
                ).start()
            else:
                if section % 2 == 0:
                    padded[pl.ds(0, rows), at] = made
                    padded[pl.ds(rows, PAD), at] = jnp.zeros((PAD, TILE), jnp.bfloat16)
                for tail in tails:
                    tail[:, at] = made[rows - tail.shape[0] :]

        if not last and chunk > 0:
            for tail, (distance, take) in zip(tails, sent):
                @pl.when(shard + distance >= shards)
                def _():
                    tail[...] = prior[pl.ds(rows - take, take), :]

        if last:
            for n in range(width // TILE):
                at = pl.ds(n * TILE, TILE)
                pltpu.make_async_copy(
                    result.at[:, at], outputs.at[chunk, :, at], osem.at[n]
                ).wait()


def load_kernel(cfg, where, frame_counts, *refs):
    rows, segs_row, micro = cfg
    sources, targets, taps, masks = refs[:7], refs[7:13], refs[13], refs[14:19]
    narrow_taps, sem = refs[19:]
    targets = [*targets, narrow_taps]
    copies = [
        pltpu.make_async_copy(source, target, sem.at[n])
        for n, (source, target) in enumerate(zip(sources, targets))
    ]
    for copy in copies:
        copy.start()
    bias, mem_bias, pick, divisor, frame_mask = masks
    q_rows, keys = bias.shape[1:]
    mem_keys = mem_bias.shape[2]
    sum_rows, ext = pick.shape[1:]
    segs = ext // SEG
    q_seg = HALO_SEGS - 1
    mem_first = q_seg - NMEM
    mems = segs - 1 - mem_first
    key_seg = q_seg - BACK
    win = ext - key_seg * SEG
    for chunk in range(micro):
        first = chunk * segs_row + where[1] * (rows // SEG) - HALO_SEGS
        counts = []
        for s in range(segs):
            safe = jnp.maximum(first + s, 0)
            value = frame_counts[safe // segs_row, safe % segs_row]
            counts.append(jnp.where(first + s >= 0, value, 0))

        row_seg = q_seg + (iota((q_rows, keys), 0) >> SHIFT)
        line = iota((1, keys), 1)
        kvalid = (line & (SEG - 1)) < by_segment(line >> SHIFT, counts, key_seg, win // SEG)
        mvalid = by_segment(line - win, counts, mem_first, mems) > 0
        live = (kvalid & (line < win)) | (mvalid & (line >= win))
        lows = jnp.where(line < win, key_seg + (line >> SHIFT), mem_first + 1 + line - win)
        highs = jnp.where(line < win, lows + BACK, lows + NMEM - 1)
        lows = jnp.where(live, lows, segs)
        good = (row_seg >= lows) & (row_seg <= highs)
        bias[chunk] = jnp.where(good, OPEN, FAR)

        mseg = mem_first + (iota((mems * HEADS, mem_keys), 0) >> HEAD_SHIFT)
        mline = iota((1, mem_keys), 1)
        mlow = mline >> SHIFT
        mlive = (mline & (SEG - 1)) < by_segment(mlow, counts, 0, mem_keys // SEG)
        mhigh = mlow + BACK
        mlow = jnp.where(mlive, mlow, segs)
        mem_bias[chunk] = jnp.where((mseg >= mlow) & (mseg <= mhigh), OPEN, FAR)

        sseg = iota((sum_rows, ext), 0) + mem_first
        sline = iota((1, ext), 1)
        smine = sline >> SHIFT
        slive = (sline & (SEG - 1)) < by_segment(smine, counts, 0, segs)
        smine = jnp.where(slive, smine, -1)
        pick[chunk] = jnp.where(sseg == smine, 1.0, 0.0).astype(jnp.bfloat16)
        scount = by_segment(iota((sum_rows, 1), 0), counts, mem_first, mems)
        divisor[chunk] = jnp.maximum(scount, 1).astype(jnp.float32)

        frame = iota((q_rows, 1), 0)
        frame_count = by_segment(frame >> SHIFT, counts, q_seg, q_rows // SEG)
        frame_mask[chunk] = ((frame & (SEG - 1)) < frame_count).astype(jnp.float32)
    for copy in copies:
        copy.wait()
    taps[pl.ds(0, KW), :] = narrow_taps[...].astype(jnp.float32)


def per_device(frames, frame_counts, w_query, w_key, w_value, w_out, conv_kernel, w_point):
    micro, rows, width = frames.shape
    sections = lax.axis_size("phase")
    shards = lax.axis_size("tm")
    segs_row = frame_counts.shape[1]
    pieces = halo_pieces(rows)
    ext = HALO + rows
    q_rows = rows + SEG
    mems = ext // SEG - 1 - (HALO_SEGS - 1 - NMEM)
    mem_pad = -(-mems // SEG) * SEG
    sum_rows = -(-mems // 16) * 16
    mem_keys = (mems + BACK) * SEG
    keys = ext + mem_pad - (HALO_SEGS - 1 - BACK) * SEG

    def send(block, distance, source, target, around):
        route = [
            (s * sections + source, (s + distance) % shards * sections + target)
            for s in range(shards)
            if around or s + distance < shards
        ]
        return lax.ppermute(block, ("tm", "phase"), route)

    def frame_halos(frames, chunk):
        halos = []
        for distance, take in pieces:
            block = frames[chunk]
            if chunk > 0:
                wraps = lax.axis_index("tm") + distance >= shards
                block = jnp.where(wraps, frames[chunk - 1], block)
            halos.append(send(block[rows - take :], distance, distance % sections, 0, chunk))
        return halos

    inbox = [[None, *frame_halos(frames, 0)]]

    where = jnp.stack([lax.axis_index("phase"), lax.axis_index("tm")]).astype(jnp.int32)

    def vmem(*shape, dtype=jnp.bfloat16):
        return pltpu.VMEM(shape, dtype)

    scratch = [
        vmem(HALO, width), vmem(ext + sum_rows, width),
        vmem(ext + mem_pad, width), vmem(ext + mem_pad, width),
        vmem(q_rows + sum_rows, width), vmem(q_rows, width), vmem(q_rows, width),
        vmem(q_rows, width, dtype=jnp.float32), vmem(rows, width, dtype=jnp.float32),
        vmem(rows, width), vmem(rows, width),
        pltpu.SemaphoreType.DMA((width // TILE,)),
    ]
    smem = pl.BlockSpec(memory_space=pltpu.SMEM)
    hbm = pl.BlockSpec(memory_space=pltpu.HBM)
    in_vmem = pl.BlockSpec(memory_space=pltpu.VMEM)
    def kept(array, space):
        return pltpu.with_memory_space_constraint(array, space)

    near_by = pl.pallas_call(
        functools.partial(load_kernel, (rows, segs_row, micro)),
        out_shape=[vmem(width, width)] * 5
        + [
            vmem(micro, rows, width),
            vmem(32, width, dtype=jnp.float32),
            vmem(micro, q_rows, keys, dtype=jnp.float32),
            vmem(micro, mems * HEADS, mem_keys, dtype=jnp.float32),
            vmem(micro, sum_rows, ext),
            vmem(micro, sum_rows, 1, dtype=jnp.float32),
            vmem(micro, q_rows, 1, dtype=jnp.float32),
        ],
        in_specs=[smem] * 2 + [hbm] * 7,
        out_specs=[in_vmem] * 12,
        scratch_shapes=[vmem(KW, width), pltpu.SemaphoreType.DMA((7,))],
        cost_estimate=pl.CostEstimate(flops=0, bytes_accessed=10**7, transcendentals=0),
        compiler_params=pltpu.CompilerParams(vmem_limit_bytes=4 * 1024 * 1024),
        name="load",
    )(
        where,
        kept(frame_counts, pltpu.HBM),
        *[kept(w[0], pltpu.HBM) for w in (w_key, w_value, w_query, w_out, w_point)],
        kept(frames, pltpu.HBM),
        kept(conv_kernel[0], pltpu.HBM),
    )
    inbox += [[None, *frame_halos(near_by[5], chunk)] for chunk in range(1, micro)]
    near_by = [kept(w, pltpu.VMEM) for w in near_by]
    frames_near = near_by.pop(5)
    block = vmem(rows, width)
    whole = pltpu.HBM((micro, rows, width), jnp.bfloat16)
    cost = pl.CostEstimate(flops=6 * 10**9, bytes_accessed=12 * 10**6, transcendentals=10**6)

    outputs = None
    results = {}
    for section in range(sections):
        outbox = []
        for chunk in range(micro):
            own = inbox[chunk][0] if section > 0 else frames_near
            near = [own, *inbox[chunk][1:]]
            if section > 0:
                near.append(results[section - 1, chunk])
            if chunk > 0 and section < sections - 1:
                near.append(results[section, chunk - 1])
            args = [where, *near_by, *[kept(array, pltpu.VMEM) for array in near]]
            in_specs = [smem] + [in_vmem] * (len(args) - 1)
            aliases = {}
            if outputs is not None:
                aliases = {len(args): 0}
                args.append(kept(outputs, pltpu.HBM))
                in_specs.append(hbm)
            last = section == sections - 1
            padded = [vmem(rows + PAD, width)] if section % 2 == 0 else []
            tails = [vmem(take, width) for _, take in halo_sent(chunk, rows, pieces)]
            outs = [whole] if last else [whole, block, *padded, *tails]
            cfg = (rows, width, section, chunk, sections, shards, segs_row, pieces)
            made = pl.pallas_call(
                functools.partial(layer_kernel, cfg),
                out_shape=outs,
                in_specs=in_specs,
                out_specs=[hbm] + [in_vmem] * (len(outs) - 1),
                scratch_shapes=scratch,
                input_output_aliases=aliases,
                cost_estimate=cost,
                compiler_params=pltpu.CompilerParams(vmem_limit_bytes=VMEM_BYTES),
                name="layer",
            )(*args)
            outputs = made[0]
            if not last:
                results[section, chunk] = made[1]
                whole_block, tails_out = made[1], iter(made[2:])
                got = {0: next(tails_out) if section % 2 == 0 else whole_block}
                for distance, take in pieces:
                    own_array = (distance, take) in halo_sent(chunk, rows, pieces)
                    got[distance] = next(tails_out) if own_array else whole_block
                far = max(got)
                if outbox and far > 0:
                    near = outbox[-1][0]
                    got[far], outbox[-1][0] = lax.optimization_barrier((got[far], near))
                sent = {d: send(got[d], d, section, section + 1, chunk) for d in got}
                outbox.append([sent[d] for d in sorted(got)])
        inbox = outbox
    return outputs[None]


def solution(mesh):
    in_specs = (
        P(None, "tm", None),
        P(),
        P("phase", None, None),
        P("phase", None, None),
        P("phase", None, None),
        P("phase", None, None),
        P("phase", None, None),
        P("phase", None, None),
    )
    out_specs = P("phase", None, "tm", None)
    return jax.shard_map(
        per_device, mesh=mesh, in_specs=in_specs, out_specs=out_specs, check_vma=False
    )
```

```python
import functools
import math

import jax
import jax.numpy as jnp
from jax import lax
from jax.experimental import pallas as pl
from jax.experimental.pallas import tpu as pltpu
from jax.sharding import PartitionSpec as P

HEADS = 16
SEG = 32
LC = 64
NMEM = 4
KW = 31

EPSILON = 1e-05
BACK = LC // SEG
HALO_SEGS = 1 + NMEM + BACK
HALO = HALO_SEGS * SEG
FAR = -1e30
OPEN = 3e38
TILE = 256
PAIR = 128
PAD = 16
SHIFT = 5
HEAD_SHIFT = 4
VMEM_BYTES = 32 * 1024 * 1024


def layer_norms(number, load, store):
    means = [jnp.mean(load(s), axis=-1, keepdims=True) for s in range(number)]
    scales = []
    for s in range(number):
        center = load(s) - means[s]
        scales.append(lax.rsqrt(jnp.mean(center * center, axis=-1, keepdims=True) + EPSILON))
    for s in range(number):
        store(s, (load(s) - means[s]) * scales[s])


def dot(a, b):
    return jnp.dot(a, b, preferred_element_type=jnp.float32)


def dot_nt(a, b):
    return lax.dot_general(a, b, (((1,), (1,)), ((), ())), preferred_element_type=jnp.float32)


def halo_pieces(rows):
    pieces = []
    left = HALO
    while left > 0:
        take = min(rows, left)
        pieces.append((len(pieces) + 1, take))
        left -= take
    return pieces


def by_segment(index, counts, first, number):
    out = jnp.zeros(index.shape, jnp.int32)
    for s in range(number):
        out = jnp.where(index == s, counts[first + s], out)
    return out


def iota(shape, dimension):
    return lax.broadcasted_iota(jnp.int32, shape, dimension)


def layer_kernel(cfg, *refs):
    rows, width, section, chunk, sections, shards, segs_row, pieces = cfg
    refs = list(refs)
    where = refs[0]
    wk, wv, wq, wo, wp, taps = refs[1:7]
    bias, mem_bias, pick, divisor, frame_mask = [ref.at[chunk] for ref in refs[7:12]]
    refs = refs[12:]
    count_p = len(pieces)
    own, halos, refs = refs[0], refs[1 : 1 + count_p], refs[1 + count_p :]
    if section == 0:
        own = own.at[chunk]
    if chunk > 0:
        befores, refs = refs[:count_p], refs[count_p:]
    if section > 0:
        earlier, refs = refs[0], refs[1:]
    if section + chunk > 0:
        refs = refs[1:]
    outputs, refs = refs[0], refs[1:]
    last = section == sections - 1
    if not last:
        result, refs = refs[0], refs[1:]
        if section % 2 == 0:
            padded, refs = refs[0], refs[1:]
        number = sum(1 for _, take in pieces if take < rows)
        tails, refs = refs[:number], refs[number:]
    (xe, normed, ke, ve, qe, ctx, res, cin, depth, gated, staged, osem) = refs
    if last:
        result = staged

    ext = HALO + rows
    segs = ext // SEG
    q_rows = rows + SEG
    q_seg = HALO_SEGS - 1
    mems = segs - 1 - (q_seg - NMEM)
    mem_pad = ke.shape[0] - ext
    key_row = (q_seg - BACK) * SEG
    keys = ke.shape[0] - key_row
    mem_keys = mem_bias.shape[1]
    head_dim = width // HEADS
    sum_rows = qe.shape[0] - q_rows
    phase, shard = where[0], where[1]

    if section > 0:
        @pl.when(phase == section - 1)
        def _():
            copy = pltpu.make_async_copy(earlier, outputs.at[chunk], osem.at[0])
            copy.start()
            copy.wait()

    @pl.when(phase == section)
    def _():
        for n, (distance, take) in enumerate(pieces):
            spot = pl.ds(HALO - (distance - 1) * rows - take, take)

            @pl.when(shard >= distance)
            def _():
                xe[spot, :] = halos[n][...]

            @pl.when(shard < distance)
            def _():
                if chunk > 0:
                    xe[spot, :] = befores[n][...]
                else:
                    xe[spot, :] = jnp.zeros((take, width), jnp.bfloat16)

        def load_x(s):
            if s < HALO_SEGS:
                part = xe[pl.ds(s * SEG, SEG), :]
            else:
                part = own[pl.ds((s - HALO_SEGS) * SEG, SEG), :]
            return part.astype(jnp.float32)

        def set_normed(s, value):
            normed[pl.ds(s * SEG, SEG), :] = value.astype(jnp.bfloat16)

        layer_norms(segs, load_x, set_normed)

        def columns(n):
            return pl.ds(pl.multiple_of(n * TILE, TILE), TILE)

        def tiles(unroll):
            return pl.loop(0, width // TILE, unroll=unroll)

        sums = dot(pick[...], normed[pl.ds(0, ext), :])
        normed[pl.ds(ext, sum_rows), :] = (sums / divisor[...]).astype(jnp.bfloat16)

        scale = 1.0 / math.sqrt(head_dim)

        @tiles(4)
        def _(n):
            at = columns(n)
            block = normed[pl.ds(0, ext), :]
            ke[pl.ds(0, ext), at] = dot(block, wk[:, at]).astype(jnp.bfloat16)
            ve[pl.ds(0, ext), at] = dot(block, wv[:, at]).astype(jnp.bfloat16)
            askers = normed[pl.ds(ext - q_rows, q_rows + sum_rows), :]
            qe[:, at] = (dot(askers, wq[:, at]) * scale).astype(jnp.bfloat16)

        own_head = (iota((HEADS, width), 1) // head_dim) == iota((HEADS, width), 0)
        sq = qe[pl.ds(q_rows, sum_rows), :].astype(jnp.float32)
        spread_q = []
        for m in range(mems):
            line_q = jnp.broadcast_to(sq[m : m + 1, :], (HEADS, width))
            spread_q.append(jnp.where(own_head, line_q, 0.0).astype(jnp.bfloat16))
        spread_q = jnp.concatenate(spread_q)
        ms = jnp.minimum(dot_nt(spread_q, ke[pl.ds(0, mem_keys), :]), mem_bias[...])
        me = jnp.exp(ms - jnp.max(ms, axis=-1, keepdims=True))
        mw = me * (1.0 / jnp.sum(me, axis=-1, keepdims=True))
        mo = dot(mw.astype(jnp.bfloat16), ve[pl.ds(0, mem_keys), :])
        lines = []
        for m in range(mems):
            part = jnp.where(own_head, mo[m * HEADS : (m + 1) * HEADS, :], 0.0)
            lines.append(jnp.sum(part, axis=0, keepdims=True))
        lines.append(jnp.zeros((mem_pad - mems, width), jnp.float32))
        memory = jnp.concatenate(lines).astype(jnp.bfloat16)

        @tiles(4)
        def _(n):
            at = columns(n)
            ke[pl.ds(ext, mem_pad), at] = dot(memory, wk[:, at]).astype(jnp.bfloat16)
            ve[pl.ds(ext, mem_pad), at] = dot(memory, wv[:, at]).astype(jnp.bfloat16)

        even = iota((q_rows, PAIR), 1) < head_dim

        @pl.loop(0, width // PAIR, unroll=4)
        def _(n):
            at = pl.ds(pl.multiple_of(n * PAIR, PAIR), PAIR)
            qp = qe[pl.ds(0, q_rows), at]
            zero = jnp.zeros_like(qp)
            q_both = jnp.concatenate([jnp.where(even, qp, zero), jnp.where(even, zero, qp)])
            raw = dot_nt(q_both, ke[pl.ds(key_row, keys), at])
            edge = bias[...]
            scores = jnp.minimum(raw, jnp.concatenate([edge, edge]))
            weight = jnp.exp(scores - jnp.max(scores, axis=-1, keepdims=True))
            inverse = 1.0 / jnp.sum(weight, axis=-1, keepdims=True)
            both = dot(weight.astype(jnp.bfloat16), ve[pl.ds(key_row, keys), at]) * inverse
            ctx[:, at] = jnp.where(even, both[:q_rows], both[q_rows:]).astype(jnp.bfloat16)

        @tiles(4)
        def _(n):
            at = columns(n)
            x_part = jnp.concatenate([xe[pl.ds(HALO - SEG, SEG), at], own[pl.ds(0, rows), at]])
            mixed = x_part.astype(jnp.float32) + dot(ctx[...], wo[:, at])
            res[:, at] = mixed.astype(jnp.bfloat16)

        def set_cin(s, value):
            mask = frame_mask[pl.ds(s * SEG, SEG), :]
            value = (value * mask).astype(jnp.bfloat16)
            cin[pl.ds(s * SEG, SEG), :] = value.astype(jnp.float32)

        layer_norms(
            q_rows // SEG, lambda s: res[pl.ds(s * SEG, SEG), :].astype(jnp.float32), set_cin
        )

        @pl.loop(0, width // PAIR, unroll=2)
        def _(n):
            at = pl.ds(pl.multiple_of(n * PAIR, PAIR), PAIR)
            total = jnp.zeros((rows, PAIR), jnp.float32)
            block = cin[:, at]
            start = SEG - (KW - 1)
            for residue in range(8):
                size = rows + (8 if residue else 0)
                part = None
                for o in range(start, start + KW):
                    if o % 8 == residue:
                        base = o - residue
                        term = taps[pl.ds(o - start, 1), at] * block[base : base + size]
                        part = term if part is None else part + term
                if residue:
                    part = pltpu.roll(part, size - residue, 0)[:rows]
                total = total + part
            depth[:, at] = total

        def set_gated(s, value):
            value = value * (1.0 / (1.0 + jnp.exp(-value)))
            gated[pl.ds(s * SEG, SEG), :] = value.astype(jnp.bfloat16)

        layer_norms(rows // SEG, lambda s: depth[pl.ds(s * SEG, SEG), :], set_gated)

        row_mask = frame_mask[pl.ds(SEG, rows), :]

        @tiles(4)
        def _(n):
            at = columns(n)
            mixed = res[pl.ds(SEG, rows), at].astype(jnp.float32) + dot(gated[...], wp[:, at])
            made = (mixed * row_mask).astype(jnp.bfloat16)
            result[:, at] = made
            if last:
                pltpu.make_async_copy(
                    result.at[:, at], outputs.at[chunk, :, at], osem.at[n]
                ).start()
            else:
                if section % 2 == 0:
                    padded[pl.ds(0, rows), at] = made
                    padded[pl.ds(rows, PAD), at] = jnp.zeros((PAD, TILE), jnp.bfloat16)
                for tail in tails:
                    tail[:, at] = made[rows - tail.shape[0] :]

        if last:
            for n in range(width // TILE):
                at = pl.ds(n * TILE, TILE)
                pltpu.make_async_copy(
                    result.at[:, at], outputs.at[chunk, :, at], osem.at[n]
                ).wait()


def load_kernel(cfg, where, frame_counts, *refs):
    rows, segs_row, micro = cfg
    sources, targets, taps, masks = refs[:7], refs[7:13], refs[13], refs[14:19]
    narrow_taps, sem = refs[19:]
    targets = [*targets, narrow_taps]
    copies = [
        pltpu.make_async_copy(source, target, sem.at[n])
        for n, (source, target) in enumerate(zip(sources, targets))
    ]
    for copy in copies:
        copy.start()
    bias, mem_bias, pick, divisor, frame_mask = masks
    q_rows, keys = bias.shape[1:]
    mem_keys = mem_bias.shape[2]
    sum_rows, ext = pick.shape[1:]
    segs = ext // SEG
    q_seg = HALO_SEGS - 1
    mem_first = q_seg - NMEM
    mems = segs - 1 - mem_first
    key_seg = q_seg - BACK
    win = ext - key_seg * SEG
    for chunk in range(micro):
        first = chunk * segs_row + where[1] * (rows // SEG) - HALO_SEGS
        counts = []
        for s in range(segs):
            safe = jnp.maximum(first + s, 0)
            value = frame_counts[safe // segs_row, safe % segs_row]
            counts.append(jnp.where(first + s >= 0, value, 0))

        row_seg = q_seg + (iota((q_rows, keys), 0) >> SHIFT)
        line = iota((1, keys), 1)
        kvalid = (line & (SEG - 1)) < by_segment(line >> SHIFT, counts, key_seg, win // SEG)
        mvalid = by_segment(line - win, counts, mem_first, mems) > 0
        live = (kvalid & (line < win)) | (mvalid & (line >= win))
        lows = jnp.where(line < win, key_seg + (line >> SHIFT), mem_first + 1 + line - win)
        highs = jnp.where(line < win, lows + BACK, lows + NMEM - 1)
        lows = jnp.where(live, lows, segs)
        good = (row_seg >= lows) & (row_seg <= highs)
        bias[chunk] = jnp.where(good, OPEN, FAR)

        mseg = mem_first + (iota((mems * HEADS, mem_keys), 0) >> HEAD_SHIFT)
        mline = iota((1, mem_keys), 1)
        mlow = mline >> SHIFT
        mlive = (mline & (SEG - 1)) < by_segment(mlow, counts, 0, mem_keys // SEG)
        mhigh = mlow + BACK
        mlow = jnp.where(mlive, mlow, segs)
        mem_bias[chunk] = jnp.where((mseg >= mlow) & (mseg <= mhigh), OPEN, FAR)

        sseg = iota((sum_rows, ext), 0) + mem_first
        sline = iota((1, ext), 1)
        smine = sline >> SHIFT
        slive = (sline & (SEG - 1)) < by_segment(smine, counts, 0, segs)
        smine = jnp.where(slive, smine, -1)
        pick[chunk] = jnp.where(sseg == smine, 1.0, 0.0).astype(jnp.bfloat16)
        scount = by_segment(iota((sum_rows, 1), 0), counts, mem_first, mems)
        divisor[chunk] = jnp.maximum(scount, 1).astype(jnp.float32)

        frame = iota((q_rows, 1), 0)
        frame_count = by_segment(frame >> SHIFT, counts, q_seg, q_rows // SEG)
        frame_mask[chunk] = ((frame & (SEG - 1)) < frame_count).astype(jnp.float32)
    for copy in copies:
        copy.wait()
    taps[pl.ds(0, KW), :] = narrow_taps[...].astype(jnp.float32)


def per_device(frames, frame_counts, w_query, w_key, w_value, w_out, conv_kernel, w_point):
    micro, rows, width = frames.shape
    sections = lax.axis_size("phase")
    shards = lax.axis_size("tm")
    segs_row = frame_counts.shape[1]
    pieces = halo_pieces(rows)
    ext = HALO + rows
    q_rows = rows + SEG
    mems = ext // SEG - 1 - (HALO_SEGS - 1 - NMEM)
    mem_pad = -(-mems // SEG) * SEG
    sum_rows = -(-mems // 16) * 16
    mem_keys = (mems + BACK) * SEG
    keys = ext + mem_pad - (HALO_SEGS - 1 - BACK) * SEG

    def send(block, distance, source, target):
        route = [
            (s * sections + source, (s + distance) % shards * sections + target)
            for s in range(shards)
        ]
        return lax.ppermute(block, ("tm", "phase"), route)

    inbox = [
        [None]
        + [
            send(frames[chunk, rows - take :, :], distance, distance % sections, 0)
            for distance, take in pieces
        ]
        for chunk in range(micro)
    ]

    where = jnp.stack([lax.axis_index("phase"), lax.axis_index("tm")]).astype(jnp.int32)

    def vmem(*shape, dtype=jnp.bfloat16):
        return pltpu.VMEM(shape, dtype)

    scratch = [
        vmem(HALO, width), vmem(ext + sum_rows, width),
        vmem(ext + mem_pad, width), vmem(ext + mem_pad, width),
        vmem(q_rows + sum_rows, width), vmem(q_rows, width), vmem(q_rows, width),
        vmem(q_rows, width, dtype=jnp.float32), vmem(rows, width, dtype=jnp.float32),
        vmem(rows, width), vmem(rows, width),
        pltpu.SemaphoreType.DMA((width // TILE,)),
    ]
    smem = pl.BlockSpec(memory_space=pltpu.SMEM)
    hbm = pl.BlockSpec(memory_space=pltpu.HBM)
    in_vmem = pl.BlockSpec(memory_space=pltpu.VMEM)
    def kept(array, space):
        return pltpu.with_memory_space_constraint(array, space)

    near_by = pl.pallas_call(
        functools.partial(load_kernel, (rows, segs_row, micro)),
        out_shape=[vmem(width, width)] * 5
        + [
            vmem(micro, rows, width),
            vmem(32, width, dtype=jnp.float32),
            vmem(micro, q_rows, keys, dtype=jnp.float32),
            vmem(micro, mems * HEADS, mem_keys, dtype=jnp.float32),
            vmem(micro, sum_rows, ext),
            vmem(micro, sum_rows, 1, dtype=jnp.float32),
            vmem(micro, q_rows, 1, dtype=jnp.float32),
        ],
        in_specs=[smem] * 2 + [hbm] * 7,
        out_specs=[in_vmem] * 12,
        scratch_shapes=[vmem(KW, width), pltpu.SemaphoreType.DMA((7,))],
        cost_estimate=pl.CostEstimate(flops=0, bytes_accessed=10**7, transcendentals=0),
        compiler_params=pltpu.CompilerParams(vmem_limit_bytes=4 * 1024 * 1024),
        name="load",
    )(
        where,
        kept(frame_counts, pltpu.HBM),
        *[kept(w[0], pltpu.HBM) for w in (w_key, w_value, w_query, w_out, w_point)],
        kept(frames, pltpu.HBM),
        kept(conv_kernel[0], pltpu.HBM),
    )
    near_by = [kept(w, pltpu.VMEM) for w in near_by]
    frames_near = near_by.pop(5)
    block = vmem(rows, width)
    tails = [vmem(take, width) for _, take in pieces if take < rows]
    whole = pltpu.HBM((micro, rows, width), jnp.bfloat16)
    cost = pl.CostEstimate(flops=6 * 10**9, bytes_accessed=12 * 10**6, transcendentals=10**6)

    outputs = None
    results = {}
    for section in range(sections):
        outbox = []
        for chunk in range(micro):
            own = inbox[chunk][0] if section > 0 else frames_near
            near = [own, *inbox[chunk][1:]]
            if chunk > 0:
                near += inbox[chunk - 1][1:]
            if section > 0:
                near.append(results[section - 1, chunk])
            args = [where, *near_by, *[kept(array, pltpu.VMEM) for array in near]]
            in_specs = [smem] + [in_vmem] * (len(args) - 1)
            aliases = {}
            if outputs is not None:
                aliases = {len(args): 0}
                args.append(kept(outputs, pltpu.HBM))
                in_specs.append(hbm)
            last = section == sections - 1
            padded = [vmem(rows + PAD, width)] if section % 2 == 0 else []
            outs = [whole] if last else [whole, block, *padded, *tails]
            cfg = (rows, width, section, chunk, sections, shards, segs_row, pieces)
            made = pl.pallas_call(
                functools.partial(layer_kernel, cfg),
                out_shape=outs,
                in_specs=in_specs,
                out_specs=[hbm] + [in_vmem] * (len(outs) - 1),
                scratch_shapes=scratch,
                input_output_aliases=aliases,
                cost_estimate=cost,
                compiler_params=pltpu.CompilerParams(vmem_limit_bytes=VMEM_BYTES),
                name="layer",
            )(*args)
            outputs = made[0]
            if not last:
                results[section, chunk] = made[1]
                whole_block, tails_out = made[1], iter(made[2:])
                got = {0: next(tails_out) if section % 2 == 0 else whole_block}
                for distance, take in pieces:
                    got[distance] = next(tails_out) if take < rows else whole_block
                far = max(got)
                if outbox and far > 0:
                    near = outbox[-1][0]
                    got[far], outbox[-1][0] = lax.optimization_barrier((got[far], near))
                sent = {d: send(got[d], d, section, section + 1) for d in got}
                outbox.append([sent[d] for d in sorted(got)])
        inbox = outbox
    return outputs[None]


def solution(mesh):
    in_specs = (
        P(None, "tm", None),
        P(),
        P("phase", None, None),
        P("phase", None, None),
        P("phase", None, None),
        P("phase", None, None),
        P("phase", None, None),
        P("phase", None, None),
    )
    out_specs = P("phase", None, "tm", None)
    return jax.shard_map(
        per_device, mesh=mesh, in_specs=in_specs, out_specs=out_specs, check_vma=False
    )
```

```python
import functools
import math

import jax
import jax.numpy as jnp
from jax import lax
from jax.experimental import pallas as pl
from jax.experimental.pallas import tpu as pltpu
from jax.sharding import PartitionSpec as P

HEADS = 16
SEG = 32
LC = 64
NMEM = 4
KW = 31

EPSILON = 1e-05
BACK = LC // SEG
HALO_SEGS = 1 + NMEM + BACK
HALO = HALO_SEGS * SEG
FAR = -1e30
OPEN = 3e38
TILE = 256
PAIR = 128
PAD = 16
SHIFT = 5
HEAD_SHIFT = 4
VMEM_BYTES = 32 * 1024 * 1024


def layer_norms(number, load, store):
    means = [jnp.mean(load(s), axis=-1, keepdims=True) for s in range(number)]
    scales = []
    for s in range(number):
        center = load(s) - means[s]
        scales.append(lax.rsqrt(jnp.mean(center * center, axis=-1, keepdims=True) + EPSILON))
    for s in range(number):
        store(s, (load(s) - means[s]) * scales[s])


def dot(a, b):
    return jnp.dot(a, b, preferred_element_type=jnp.float32)


def dot_nt(a, b):
    return lax.dot_general(a, b, (((1,), (1,)), ((), ())), preferred_element_type=jnp.float32)


def halo_pieces(rows):
    pieces = []
    left = HALO
    while left > 0:
        take = min(rows, left)
        pieces.append((len(pieces) + 1, take))
        left -= take
    return pieces


def by_segment(index, counts, first, number):
    out = jnp.zeros(index.shape, jnp.int32)
    for s in range(number):
        out = jnp.where(index == s, counts[first + s], out)
    return out


def iota(shape, dimension):
    return lax.broadcasted_iota(jnp.int32, shape, dimension)


def layer_kernel(cfg, *refs):
    rows, width, section, chunk, sections, shards, segs_row, pieces = cfg
    refs = list(refs)
    where = refs[0]
    wk, wv, wq, wo, wp, taps = refs[1:7]
    bias, mem_bias, pick, divisor, frame_mask = [ref.at[chunk] for ref in refs[7:12]]
    refs = refs[12:]
    count_p = len(pieces)
    own, halos, refs = refs[0], refs[1 : 1 + count_p], refs[1 + count_p :]
    if section == 0:
        own = own.at[chunk]
    if chunk > 0:
        befores, refs = refs[:count_p], refs[count_p:]
    if section > 0:
        earlier, refs = refs[0], refs[1:]
    if section + chunk > 0:
        refs = refs[1:]
    outputs, refs = refs[0], refs[1:]
    last = section == sections - 1
    if not last:
        result, refs = refs[0], refs[1:]
        if section % 2 == 0:
            padded, refs = refs[0], refs[1:]
        number = sum(1 for _, take in pieces if take < rows)
        tails, refs = refs[:number], refs[number:]
    (xe, normed, ke, ve, qe, ctx, res, cin, depth, gated, staged, osem) = refs
    if last:
        result = staged

    ext = HALO + rows
    segs = ext // SEG
    q_rows = rows + SEG
    q_seg = HALO_SEGS - 1
    mems = segs - 1 - (q_seg - NMEM)
    mem_pad = ke.shape[0] - ext
    key_row = (q_seg - BACK) * SEG
    keys = ke.shape[0] - key_row
    mem_keys = mem_bias.shape[1]
    head_dim = width // HEADS
    sum_rows = qe.shape[0] - q_rows
    phase, shard = where[0], where[1]

    if section > 0:
        @pl.when(phase == section - 1)
        def _():
            copy = pltpu.make_async_copy(earlier, outputs.at[chunk], osem.at[0])
            copy.start()
            copy.wait()

    @pl.when(phase == section)
    def _():
        for n, (distance, take) in enumerate(pieces):
            spot = pl.ds(HALO - (distance - 1) * rows - take, take)

            @pl.when(shard >= distance)
            def _():
                xe[spot, :] = halos[n][...]

            @pl.when(shard < distance)
            def _():
                if chunk > 0:
                    xe[spot, :] = befores[n][...]
                else:
                    xe[spot, :] = jnp.zeros((take, width), jnp.bfloat16)

        def load_x(s):
            if s < HALO_SEGS:
                part = xe[pl.ds(s * SEG, SEG), :]
            else:
                part = own[pl.ds((s - HALO_SEGS) * SEG, SEG), :]
            return part.astype(jnp.float32)

        def set_normed(s, value):
            normed[pl.ds(s * SEG, SEG), :] = value.astype(jnp.bfloat16)

        layer_norms(segs, load_x, set_normed)

        def columns(n):
            return pl.ds(pl.multiple_of(n * TILE, TILE), TILE)

        def tiles(unroll):
            return pl.loop(0, width // TILE, unroll=unroll)

        sums = dot(pick[...], normed[pl.ds(0, ext), :])
        normed[pl.ds(ext, sum_rows), :] = (sums / divisor[...]).astype(jnp.bfloat16)

        scale = 1.0 / math.sqrt(head_dim)

        @tiles(4)
        def _(n):
            at = columns(n)
            block = normed[pl.ds(0, ext), :]
            ke[pl.ds(0, ext), at] = dot(block, wk[:, at]).astype(jnp.bfloat16)
            ve[pl.ds(0, ext), at] = dot(block, wv[:, at]).astype(jnp.bfloat16)
            askers = normed[pl.ds(ext - q_rows, q_rows + sum_rows), :]
            qe[:, at] = (dot(askers, wq[:, at]) * scale).astype(jnp.bfloat16)

        own_head = (iota((HEADS, width), 1) // head_dim) == iota((HEADS, width), 0)
        sq = qe[pl.ds(q_rows, sum_rows), :].astype(jnp.float32)
        spread_q = []
        for m in range(mems):
            line_q = jnp.broadcast_to(sq[m : m + 1, :], (HEADS, width))
            spread_q.append(jnp.where(own_head, line_q, 0.0).astype(jnp.bfloat16))
        spread_q = jnp.concatenate(spread_q)
        ms = jnp.minimum(dot_nt(spread_q, ke[pl.ds(0, mem_keys), :]), mem_bias[...])
        me = jnp.exp(ms - jnp.max(ms, axis=-1, keepdims=True))
        mw = me * (1.0 / jnp.sum(me, axis=-1, keepdims=True))
        mo = dot(mw.astype(jnp.bfloat16), ve[pl.ds(0, mem_keys), :])
        lines = []
        for m in range(mems):
            part = jnp.where(own_head, mo[m * HEADS : (m + 1) * HEADS, :], 0.0)
            lines.append(jnp.sum(part, axis=0, keepdims=True))
        lines.append(jnp.zeros((mem_pad - mems, width), jnp.float32))
        memory = jnp.concatenate(lines).astype(jnp.bfloat16)

        @tiles(4)
        def _(n):
            at = columns(n)
            ke[pl.ds(ext, mem_pad), at] = dot(memory, wk[:, at]).astype(jnp.bfloat16)
            ve[pl.ds(ext, mem_pad), at] = dot(memory, wv[:, at]).astype(jnp.bfloat16)

        even = iota((q_rows, PAIR), 1) < head_dim

        @pl.loop(0, width // PAIR, unroll=8)
        def _(n):
            at = pl.ds(pl.multiple_of(n * PAIR, PAIR), PAIR)
            qp = qe[pl.ds(0, q_rows), at]
            zero = jnp.zeros_like(qp)
            q_both = jnp.concatenate([jnp.where(even, qp, zero), jnp.where(even, zero, qp)])
            raw = dot_nt(q_both, ke[pl.ds(key_row, keys), at])
            edge = bias[...]
            scores = jnp.minimum(raw, jnp.concatenate([edge, edge]))
            weight = jnp.exp(scores - jnp.max(scores, axis=-1, keepdims=True))
            inverse = 1.0 / jnp.sum(weight, axis=-1, keepdims=True)
            both = dot(weight.astype(jnp.bfloat16), ve[pl.ds(key_row, keys), at]) * inverse
            ctx[:, at] = jnp.where(even, both[:q_rows], both[q_rows:]).astype(jnp.bfloat16)

        @tiles(4)
        def _(n):
            at = columns(n)
            x_part = jnp.concatenate([xe[pl.ds(HALO - SEG, SEG), at], own[pl.ds(0, rows), at]])
            mixed = x_part.astype(jnp.float32) + dot(ctx[...], wo[:, at])
            res[:, at] = mixed.astype(jnp.bfloat16)

        def set_cin(s, value):
            mask = frame_mask[pl.ds(s * SEG, SEG), :]
            value = (value * mask).astype(jnp.bfloat16)
            cin[pl.ds(s * SEG, SEG), :] = value.astype(jnp.float32)

        layer_norms(
            q_rows // SEG, lambda s: res[pl.ds(s * SEG, SEG), :].astype(jnp.float32), set_cin
        )

        @pl.loop(0, width // PAIR, unroll=4)
        def _(n):
            at = pl.ds(pl.multiple_of(n * PAIR, PAIR), PAIR)
            total = jnp.zeros((rows, PAIR), jnp.float32)
            block = cin[:, at]
            start = SEG - (KW - 1)
            for residue in range(8):
                size = rows + (8 if residue else 0)
                part = None
                for o in range(start, start + KW):
                    if o % 8 == residue:
                        base = o - residue
                        term = taps[pl.ds(o - start, 1), at] * block[base : base + size]
                        part = term if part is None else part + term
                if residue:
                    part = pltpu.roll(part, size - residue, 0)[:rows]
                total = total + part
            depth[:, at] = total

        def set_gated(s, value):
            value = value * (1.0 / (1.0 + jnp.exp(-value)))
            gated[pl.ds(s * SEG, SEG), :] = value.astype(jnp.bfloat16)

        layer_norms(rows // SEG, lambda s: depth[pl.ds(s * SEG, SEG), :], set_gated)

        row_mask = frame_mask[pl.ds(SEG, rows), :]

        @tiles(4)
        def _(n):
            at = columns(n)
            mixed = res[pl.ds(SEG, rows), at].astype(jnp.float32) + dot(gated[...], wp[:, at])
            made = (mixed * row_mask).astype(jnp.bfloat16)
            result[:, at] = made
            if last:
                pltpu.make_async_copy(
                    result.at[:, at], outputs.at[chunk, :, at], osem.at[n]
                ).start()
            else:
                if section % 2 == 0:
                    padded[pl.ds(0, rows), at] = made
                    padded[pl.ds(rows, PAD), at] = jnp.zeros((PAD, TILE), jnp.bfloat16)
                for tail in tails:
                    tail[:, at] = made[rows - tail.shape[0] :]

        if last:
            for n in range(width // TILE):
                at = pl.ds(n * TILE, TILE)
                pltpu.make_async_copy(
                    result.at[:, at], outputs.at[chunk, :, at], osem.at[n]
                ).wait()


def load_kernel(cfg, where, frame_counts, *refs):
    rows, segs_row, micro = cfg
    sources, targets, taps, masks = refs[:7], refs[7:13], refs[13], refs[14:19]
    narrow_taps, sem = refs[19:]
    targets = [*targets, narrow_taps]
    copies = [
        pltpu.make_async_copy(source, target, sem.at[n])
        for n, (source, target) in enumerate(zip(sources, targets))
    ]
    for copy in copies:
        copy.start()
    bias, mem_bias, pick, divisor, frame_mask = masks
    q_rows, keys = bias.shape[1:]
    mem_keys = mem_bias.shape[2]
    sum_rows, ext = pick.shape[1:]
    segs = ext // SEG
    q_seg = HALO_SEGS - 1
    mem_first = q_seg - NMEM
    mems = segs - 1 - mem_first
    key_seg = q_seg - BACK
    win = ext - key_seg * SEG
    for chunk in range(micro):
        first = chunk * segs_row + where[1] * (rows // SEG) - HALO_SEGS
        counts = []
        for s in range(segs):
            safe = jnp.maximum(first + s, 0)
            value = frame_counts[safe // segs_row, safe % segs_row]
            counts.append(jnp.where(first + s >= 0, value, 0))

        row_seg = q_seg + (iota((q_rows, keys), 0) >> SHIFT)
        line = iota((1, keys), 1)
        kvalid = (line & (SEG - 1)) < by_segment(line >> SHIFT, counts, key_seg, win // SEG)
        mvalid = by_segment(line - win, counts, mem_first, mems) > 0
        live = (kvalid & (line < win)) | (mvalid & (line >= win))
        lows = jnp.where(line < win, key_seg + (line >> SHIFT), mem_first + 1 + line - win)
        highs = jnp.where(line < win, lows + BACK, lows + NMEM - 1)
        lows = jnp.where(live, lows, segs)
        good = (row_seg >= lows) & (row_seg <= highs)
        bias[chunk] = jnp.where(good, OPEN, FAR)

        mseg = mem_first + (iota((mems * HEADS, mem_keys), 0) >> HEAD_SHIFT)
        mline = iota((1, mem_keys), 1)
        mlow = mline >> SHIFT
        mlive = (mline & (SEG - 1)) < by_segment(mlow, counts, 0, mem_keys // SEG)
        mhigh = mlow + BACK
        mlow = jnp.where(mlive, mlow, segs)
        mem_bias[chunk] = jnp.where((mseg >= mlow) & (mseg <= mhigh), OPEN, FAR)

        sseg = iota((sum_rows, ext), 0) + mem_first
        sline = iota((1, ext), 1)
        smine = sline >> SHIFT
        slive = (sline & (SEG - 1)) < by_segment(smine, counts, 0, segs)
        smine = jnp.where(slive, smine, -1)
        pick[chunk] = jnp.where(sseg == smine, 1.0, 0.0).astype(jnp.bfloat16)
        scount = by_segment(iota((sum_rows, 1), 0), counts, mem_first, mems)
        divisor[chunk] = jnp.maximum(scount, 1).astype(jnp.float32)

        frame = iota((q_rows, 1), 0)
        frame_count = by_segment(frame >> SHIFT, counts, q_seg, q_rows // SEG)
        frame_mask[chunk] = ((frame & (SEG - 1)) < frame_count).astype(jnp.float32)
    for copy in copies:
        copy.wait()
    taps[pl.ds(0, KW), :] = narrow_taps[...].astype(jnp.float32)


def per_device(frames, frame_counts, w_query, w_key, w_value, w_out, conv_kernel, w_point):
    micro, rows, width = frames.shape
    sections = lax.axis_size("phase")
    shards = lax.axis_size("tm")
    segs_row = frame_counts.shape[1]
    pieces = halo_pieces(rows)
    ext = HALO + rows
    q_rows = rows + SEG
    mems = ext // SEG - 1 - (HALO_SEGS - 1 - NMEM)
    mem_pad = -(-mems // SEG) * SEG
    sum_rows = -(-mems // 16) * 16
    mem_keys = (mems + BACK) * SEG
    keys = ext + mem_pad - (HALO_SEGS - 1 - BACK) * SEG

    def send(block, distance, source, target):
        route = [
            (s * sections + source, (s + distance) % shards * sections + target)
            for s in range(shards)
        ]
        return lax.ppermute(block, ("tm", "phase"), route)

    inbox = [
        [None]
        + [
            send(frames[chunk, rows - take :, :], distance, distance % sections, 0)
            for distance, take in pieces
        ]
        for chunk in range(micro)
    ]

    where = jnp.stack([lax.axis_index("phase"), lax.axis_index("tm")]).astype(jnp.int32)

    def vmem(*shape, dtype=jnp.bfloat16):
        return pltpu.VMEM(shape, dtype)

    scratch = [
        vmem(HALO, width), vmem(ext + sum_rows, width),
        vmem(ext + mem_pad, width), vmem(ext + mem_pad, width),
        vmem(q_rows + sum_rows, width), vmem(q_rows, width), vmem(q_rows, width),
        vmem(q_rows, width, dtype=jnp.float32), vmem(rows, width, dtype=jnp.float32),
        vmem(rows, width), vmem(rows, width),
        pltpu.SemaphoreType.DMA((width // TILE,)),
    ]
    smem = pl.BlockSpec(memory_space=pltpu.SMEM)
    hbm = pl.BlockSpec(memory_space=pltpu.HBM)
    in_vmem = pl.BlockSpec(memory_space=pltpu.VMEM)
    def kept(array, space):
        return pltpu.with_memory_space_constraint(array, space)

    near_by = pl.pallas_call(
        functools.partial(load_kernel, (rows, segs_row, micro)),
        out_shape=[vmem(width, width)] * 5
        + [
            vmem(micro, rows, width),
            vmem(32, width, dtype=jnp.float32),
            vmem(micro, q_rows, keys, dtype=jnp.float32),
            vmem(micro, mems * HEADS, mem_keys, dtype=jnp.float32),
            vmem(micro, sum_rows, ext),
            vmem(micro, sum_rows, 1, dtype=jnp.float32),
            vmem(micro, q_rows, 1, dtype=jnp.float32),
        ],
        in_specs=[smem] * 2 + [hbm] * 7,
        out_specs=[in_vmem] * 12,
        scratch_shapes=[vmem(KW, width), pltpu.SemaphoreType.DMA((7,))],
        cost_estimate=pl.CostEstimate(flops=0, bytes_accessed=10**7, transcendentals=0),
        compiler_params=pltpu.CompilerParams(vmem_limit_bytes=4 * 1024 * 1024),
        name="load",
    )(
        where,
        kept(frame_counts, pltpu.HBM),
        *[kept(w[0], pltpu.HBM) for w in (w_key, w_value, w_query, w_out, w_point)],
        kept(frames, pltpu.HBM),
        kept(conv_kernel[0], pltpu.HBM),
    )
    near_by = [kept(w, pltpu.VMEM) for w in near_by]
    frames_near = near_by.pop(5)
    block = vmem(rows, width)
    tails = [vmem(take, width) for _, take in pieces if take < rows]
    whole = pltpu.HBM((micro, rows, width), jnp.bfloat16)
    cost = pl.CostEstimate(flops=6 * 10**9, bytes_accessed=12 * 10**6, transcendentals=10**6)

    outputs = None
    results = {}
    for section in range(sections):
        outbox = []
        for chunk in range(micro):
            own = inbox[chunk][0] if section > 0 else frames_near
            near = [own, *inbox[chunk][1:]]
            if chunk > 0:
                near += inbox[chunk - 1][1:]
            if section > 0:
                near.append(results[section - 1, chunk])
            args = [where, *near_by, *[kept(array, pltpu.VMEM) for array in near]]
            in_specs = [smem] + [in_vmem] * (len(args) - 1)
            aliases = {}
            if outputs is not None:
                aliases = {len(args): 0}
                args.append(kept(outputs, pltpu.HBM))
                in_specs.append(hbm)
            last = section == sections - 1
            padded = [vmem(rows + PAD, width)] if section % 2 == 0 else []
            outs = [whole] if last else [whole, block, *padded, *tails]
            cfg = (rows, width, section, chunk, sections, shards, segs_row, pieces)
            made = pl.pallas_call(
                functools.partial(layer_kernel, cfg),
                out_shape=outs,
                in_specs=in_specs,
                out_specs=[hbm] + [in_vmem] * (len(outs) - 1),
                scratch_shapes=scratch,
                input_output_aliases=aliases,
                cost_estimate=cost,
                compiler_params=pltpu.CompilerParams(vmem_limit_bytes=VMEM_BYTES),
                name="layer",
            )(*args)
            outputs = made[0]
            if not last:
                results[section, chunk] = made[1]
                whole_block, tails_out = made[1], iter(made[2:])
                got = {0: next(tails_out) if section % 2 == 0 else whole_block}
                for distance, take in pieces:
                    got[distance] = next(tails_out) if take < rows else whole_block
                far = max(got)
                if outbox and far > 0:
                    near = outbox[-1][0]
                    got[far], outbox[-1][0] = lax.optimization_barrier((got[far], near))
                sent = {d: send(got[d], d, section, section + 1) for d in got}
                outbox.append([sent[d] for d in sorted(got)])
        inbox = outbox
    return outputs[None]


def solution(mesh):
    in_specs = (
        P(None, "tm", None),
        P(),
        P("phase", None, None),
        P("phase", None, None),
        P("phase", None, None),
        P("phase", None, None),
        P("phase", None, None),
        P("phase", None, None),
    )
    out_specs = P("phase", None, "tm", None)
    return jax.shard_map(
        per_device, mesh=mesh, in_specs=in_specs, out_specs=out_specs, check_vma=False
    )
```
